128 devices in a mesh: leaf: 8 (over y, core), top: 16 (over x, z).
Axes of the slice: x: 4, y: 4, z: 4, core: 2. Of those that a mesh axis runs over, the one named last changes fastest.
Arguments:
- points: bfloat16 [1024, 64, 512], P(('leaf', 'top')), may hold values from -4 to 4
- right_sides: bfloat16 [1024, 64, 512], P(('leaf', 'top')), may hold values from -6 to 6
- leaf_basis: bfloat16 [1024, 512, 256], P(('leaf', 'top')), may hold values from -0.25 to 0.25
- transfer: bfloat16 [1024, 256, 256], P(('leaf', 'top')), may hold values from -0.125 to 0.125
- node_points: bfloat16 [8, 64, 256], P('leaf'), may hold values from -4 to 4
- neighbours: int32 [1024, 8], P(('leaf', 'top')), may hold values from -1 to 1023, as said below
- far_sources: int32 [1024, 16], P(('leaf', 'top')), may hold values from -1 to 1023, as said below
- skeleton: int32 [1024, 256], P(('leaf', 'top')), may hold values from 0 to 511, as said below
Outputs:
- product: bfloat16 [1024, 64, 512], P(('leaf', 'top'))
The draws below stay inside these ranges and needn't reach their ends.
Inputs may be any that keep to these rules, and one draw needn't show every extreme that they name: `neighbours`: every entry is -1 or a leaf index that differs from its row's own leaf index by at most 8. `far_sources`: for row g, with d = g // 8 and r = d // 16, entry k is -1 or a leaf index in [(r * 16 + k) * 8, (r * 16 + k + 1) * 8). `skeleton`: each row holds 256 different indices.
All inputs are finite; a program needn't handle non-finite values.
Results may differ from the reference program's by a relative error of at most 0.015.
Values may be sent and summed in bfloat16 or wider, within the bound.
No kernel may reach another device: no remote copies, remote signals or barrier semaphores. Data moves between devices by JAX's collectives and lax.ppermute only.
A program may use at most 128 MiB of HBM per device.

```python
import jax
import jax.numpy as jnp
from jax import lax

F = 64
RHS = 64
LP = 512
SK = 256
NB = 8
LEAF_DEV = 8
LEAVES = 1024
SPAN = 16
NODES = 8


def draw_points(key, part):
    key = jax.random.fold_in(key, 5)
    values = jnp.clip(jax.random.normal(key, (LEAVES, F, LP), jnp.float32), -4.0, 4.0)
    return values.astype(jnp.bfloat16)


def draw_node_points(key, part):
    key = jax.random.fold_in(key, 7)
    values = jnp.clip(jax.random.normal(key, (NODES, F, SK), jnp.float32), -4.0, 4.0)
    return values.astype(jnp.bfloat16)


def draw_neighbours(key, part):
    key = jax.random.fold_in(key, 11)
    offset_key, drop_key = jax.random.split(key)
    leaf_ids = jnp.arange(LEAVES, dtype=jnp.int32)
    offsets = jax.random.randint(offset_key, (LEAVES, NB), -LEAF_DEV, LEAF_DEV + 1, dtype=jnp.int32)
    candidate = leaf_ids[:, None] + offsets
    dropped = jax.random.randint(drop_key, (LEAVES, NB), 0, 5, dtype=jnp.int32) == 0
    inside = (candidate >= 0) & (candidate < LEAVES) & jnp.logical_not(dropped)
    return jnp.where(inside, candidate, -1).astype(jnp.int32)


def draw_far_sources(key, part):
    key = jax.random.fold_in(key, 23)
    local_key, drop_key = jax.random.split(key)
    leaf_ids = jnp.arange(LEAVES, dtype=jnp.int32)
    row_index = leaf_ids // LEAF_DEV // SPAN
    column_ids = jnp.arange(SPAN, dtype=jnp.int32)
    local_ids = jax.random.randint(local_key, (LEAVES, SPAN), 0, LEAF_DEV, dtype=jnp.int32)
    chosen = (row_index[:, None] * SPAN + column_ids[None, :]) * LEAF_DEV + local_ids
    dropped = jax.random.randint(drop_key, (LEAVES, SPAN), 0, 5, dtype=jnp.int32) == 0
    return jnp.where(dropped, -1, chosen).astype(jnp.int32)


def draw_skeleton(key, part):
    key = jax.random.fold_in(key, 37)
    scores = jax.random.randint(key, (LEAVES, LP), 0, 2 ** 20, dtype=jnp.int32) * LP + jnp.arange(LP, dtype=jnp.int32)[None, :]
    ordered = jnp.argsort(scores, axis=1, stable=True)
    return ordered[:, :SK].astype(jnp.int32)


def levels(key, dims, cuts, least, top_value):
    level, own = 1.0, jax.random.fold_in(key, 6)
    for axis_at, parts in cuts:
        heights = jnp.exp(jax.random.uniform(jax.random.fold_in(own, axis_at), (parts,), jnp.float32, least / len(cuts), top_value / len(cuts)))
        level = level * jnp.repeat(heights, dims[axis_at] // parts).reshape([-1 if axis == axis_at else 1 for axis in range(len(dims))])
    return level


def normal_values(own_key, dims, deviation, bound, pieces=(), held_as=jnp.bfloat16):
    result = jax.random.normal(own_key, dims, jnp.float32) * deviation
    if len(pieces) > 0:
        result = levels(own_key, dims, pieces, -0.22, 0.18) * result
    return jnp.clip(result, min=-bound, max=bound).astype(held_as)


def setup_inputs(seed: int = 0) -> dict:
    keys = jax.random.split(jax.random.key(seed), 9)
    points = draw_points(jax.random.fold_in(keys[8], 71), 0)
    right_sides = normal_values(keys[1], (LEAVES, RHS, LP), 1.0, 6.0, ((0, 128),))
    leaf_basis = normal_values(keys[2], (LEAVES, LP, SK), LP ** -0.5, 0.25, ((0, 128),))
    transfer = normal_values(keys[3], (LEAVES, SK, SK), (SK * LEAF_DEV) ** -0.5, 0.125, ((0, 128),))
    node_points = draw_node_points(jax.random.fold_in(keys[8], 71), 0)
    neighbours = draw_neighbours(jax.random.fold_in(keys[8], 71), 0)
    far_sources = draw_far_sources(jax.random.fold_in(keys[8], 71), 0)
    skeleton = draw_skeleton(jax.random.fold_in(keys[8], 71), 0)
    return dict(points=points, right_sides=right_sides, leaf_basis=leaf_basis, transfer=transfer, node_points=node_points, neighbours=neighbours, far_sources=far_sources, skeleton=skeleton)


def kernel_block(source, target):
    source_f = source.astype(jnp.float32)
    target_f = target.astype(jnp.float32)
    crossed = jnp.einsum('fa,fb->ab', source_f, target_f, precision=lax.Precision.HIGHEST)
    source_norm = jnp.sum(jnp.square(source_f), axis=0)
    target_norm = jnp.sum(jnp.square(target_f), axis=0)
    distance = source_norm[:, None] + target_norm[None, :] - 2.0 * crossed
    return jnp.exp(distance * (-2.0 / F)).astype(jnp.bfloat16)


def reference(points, right_sides, leaf_basis, transfer, node_points, neighbours, far_sources, skeleton):
    highest = lax.Precision.HIGHEST
    charges = jnp.einsum('lrp,lps->lrs', right_sides.astype(jnp.float32), leaf_basis.astype(jnp.float32), precision=highest).astype(jnp.bfloat16)
    skel_points = jnp.take_along_axis(points, skeleton[:, None, :], axis=2)
    leaf_terms = jnp.einsum('lrs,lst->lrt', charges.astype(jnp.float32), transfer.astype(jnp.float32), precision=highest)
    per_node = LEAVES // NODES
    node_charge = jnp.sum(leaf_terms.reshape(NODES, per_node, RHS, SK), axis=1).astype(jnp.bfloat16)
    node_kernel = jax.vmap(lambda source: jax.vmap(lambda target: kernel_block(source, target))(node_points))(node_points)
    others = jnp.arange(NODES)[:, None] != jnp.arange(NODES)[None, :]
    node_kernel = jnp.where(others[:, :, None, None], node_kernel, jnp.zeros_like(node_kernel))
    top_potential = jnp.einsum('mrs,mnst->nrt', node_charge.astype(jnp.float32), node_kernel.astype(jnp.float32), precision=highest).astype(jnp.bfloat16)

    def one_leaf(leaf):
        far_ids = far_sources[leaf]
        far_present = far_ids >= 0
        far_safe = jnp.where(far_present, far_ids, 0)
        source_points = skel_points[far_safe]
        source_charges = charges[far_safe]
        source_charges = jnp.where(far_present[:, None, None], source_charges, jnp.zeros_like(source_charges))
        tiles = jax.vmap(kernel_block, (0, None))(source_points, skel_points[leaf])
        leaf_potential = jnp.einsum('krs,kst->rt', source_charges.astype(jnp.float32), tiles.astype(jnp.float32), precision=highest)
        node = leaf // per_node
        potential = (leaf_potential + jnp.dot(top_potential[node], transfer[leaf].T, preferred_element_type=jnp.float32)).astype(jnp.bfloat16)
        near_ids = neighbours[leaf]
        near_present = near_ids >= 0
        near_safe = jnp.where(near_present, near_ids, 0)
        near_tiles = jax.vmap(kernel_block, (0, None))(points[near_safe], points[leaf])
        near_weights = right_sides[near_safe]
        near_weights = jnp.where(near_present[:, None, None], near_weights, jnp.zeros_like(near_weights))
        near_sum = jnp.einsum('jrp,jpq->rq', near_weights.astype(jnp.float32), near_tiles.astype(jnp.float32), precision=highest)
        far_out = jnp.dot(potential, leaf_basis[leaf].T, preferred_element_type=jnp.float32)
        return (near_sum + far_out).astype(jnp.bfloat16)

    return lax.map(one_leaf, jnp.arange(LEAVES))
```

```python
import functools

import jax
import jax.numpy as jnp
from jax import lax
from jax.experimental import pallas as pl
from jax.experimental.pallas import tpu as pltpu
from jax.sharding import PartitionSpec as P

BF = jnp.bfloat16
F32 = jnp.float32
F = 64
RHS = 64
LP = 512
SK = 256
LD = 8
SIDE = 4
AUG = 128
VM = pl.BlockSpec(memory_space=pltpu.VMEM)
SM = pl.BlockSpec(memory_space=pltpu.SMEM)


def params(mib=40):
    return pltpu.CompilerParams(vmem_limit_bytes=mib * 2**20)


def norm_rows(points, first):
    norm = jnp.sum(points * points, axis=0, keepdims=True) * (-2.0 / F)
    high = norm.astype(BF).astype(F32)
    mid = (norm - high).astype(BF).astype(F32)
    low = norm - high - mid
    row = lax.broadcasted_iota(jnp.int32, (16, points.shape[1]), 0)
    at = 0 if first else 3
    ones = jnp.where(row < 6, 1.0, 0.0).astype(F32)
    rows = jnp.where(row == at + 1, mid, jnp.where(row == at + 2, low, ones))
    return jnp.where(row == at, high, rows)


def source_side(points):
    points = points.astype(F32)
    zeros = jnp.zeros((AUG - F - 16, points.shape[1]), F32)
    full = jnp.concatenate([points, norm_rows(points, True), zeros], axis=0)
    return full.T.astype(BF)


def target_side(points):
    points = points.astype(F32)
    zeros = jnp.zeros((AUG - F - 16, points.shape[1]), F32)
    full = jnp.concatenate([points * (4.0 / F), norm_rows(points, False), zeros], axis=0)
    return full.astype(BF)


def prep_kernel(
    points, sides, basis, transfer, skeleton, far, near_msg, source_msg, target_msg, node, ids
):
    leaf = pl.program_id(0)
    near_msg[0, :F, :] = points[0]
    near_msg[0, F:, :] = sides[0]
    charge = jnp.dot(sides[0], basis[0], preferred_element_type=F32).astype(BF)
    position = lax.broadcasted_iota(jnp.int32, (LP, SK), 0)
    chosen = jnp.where(position == skeleton[0], 1.0, 0.0).astype(BF)
    skel = jnp.dot(points[0], chosen, preferred_element_type=F32).astype(BF)
    source_msg[pl.ds(pl.multiple_of(leaf * 2 * F, 2 * F), F), :] = charge
    source_msg[pl.ds(pl.multiple_of(leaf * 2 * F + F, F), F), :] = skel
    target_msg[pl.ds(pl.multiple_of(leaf * F, F), F), :] = skel
    part = jnp.dot(charge, transfer[0], preferred_element_type=F32)

    @pl.when(leaf == 0)
    def _():
        node[...] = part
        ids[...] = jnp.zeros_like(ids)
        named = far[...]
        ids[:LD, : SIDE * SIDE] = jnp.where(named >= 0, named & (LD - 1), -1).astype(F32)
        target_msg[LD * F :, :] = ids[...].astype(BF)

    @pl.when(leaf > 0)
    def _():
        node[...] += part

    @pl.when(leaf == LD - 1)
    def _():
        source_msg[LD * 2 * F :, :] = node[...].astype(BF)


def prep(points, sides, basis, transfer, skeleton, far):
    def block(*shape):
        return pl.BlockSpec((1, *shape), lambda i: (i, 0, 0))

    def whole(*shape):
        return pl.BlockSpec(shape, lambda i: (0,) * len(shape))

    source_rows, target_rows = LD * 2 * F + RHS, LD * F + 16
    return pl.pallas_call(
        prep_kernel,
        grid=(LD,),
        in_specs=[
            block(F, LP),
            block(RHS, LP),
            block(LP, SK),
            block(SK, SK),
            block(1, SK),
            whole(LD, SIDE * SIDE),
        ],
        out_specs=[block(2 * F, LP), whole(source_rows, SK), whole(target_rows, SK)],
        out_shape=[
            jax.ShapeDtypeStruct((LD, 2 * F, LP), BF),
            jax.ShapeDtypeStruct((source_rows, SK), BF),
            jax.ShapeDtypeStruct((target_rows, SK), BF),
        ],
        scratch_shapes=[pltpu.VMEM((RHS, SK), F32), pltpu.VMEM((16, SK), F32)],
        compiler_params=params(24),
        cost_estimate=pl.CostEstimate(
            flops=10**9, bytes_accessed=6 * 10**6, transcendentals=0
        ),
        name="prep",
    )(points, sides, basis, transfer, skeleton.reshape(LD, 1, SK), far)


def far_kernel(
    ids, place, s0, s1, s2, s3, t0, t1, t2, t3, nodes, own, r1, r2, r3, top, side, tile
):
    sources = (s0, s1, s2, s3)
    for d, source in enumerate(sources):

        @pl.loop(0, LD)
        def _(leaf, d=d, source=source):
            rows = pl.ds(pl.multiple_of(leaf * 2 * F + F, F), F)
            side[d * LD + leaf] = source_side(source[rows, :])

    x, z, self_node = place[0], place[1], place[2]
    shifts = (0, SIDE - 1, 1, 2)
    for b, (target, out) in enumerate(zip((t0, t1, t2, t3), (own, r1, r2, r3))):

        @pl.loop(0, LD)
        def _(leaf, b=b, target=target, out=out):
            rows = pl.ds(pl.multiple_of(leaf * F, F), F)
            points = target_side(target[rows, :])
            weights = []
            for d, source in enumerate(sources):
                column = lax.rem(x + shifts[d], SIDE) * SIDE + z
                named = ids[b * LD + leaf, column]
                at = jnp.maximum(named, 0)
                tile[d * SK : (d + 1) * SK, :] = jnp.exp(
                    jnp.dot(side[d * LD + at], points, preferred_element_type=F32)
                ).astype(BF)
                weight = source[pl.ds(pl.multiple_of(at * 2 * F, 2 * F), RHS), :]
                weights.append(jnp.where(named >= 0, weight, jnp.zeros_like(weight)))
            total = jnp.dot(
                jnp.concatenate(weights, axis=1), tile[...], preferred_element_type=F32
            )
            out[rows, :] = total.astype(out.dtype)

    points = target_side(nodes[self_node, RHS:, :])
    top[...] = jnp.zeros_like(top)
    total = jnp.zeros((RHS, SK), F32)
    for m in range(nodes.shape[0]):
        kernel = jnp.exp(
            jnp.dot(source_side(nodes[m, RHS:, :]), points, preferred_element_type=F32)
        ).astype(BF)
        weight = nodes[m, :RHS, :]
        weight = jnp.where(self_node == m, jnp.zeros_like(weight), weight)
        total += jnp.dot(weight, kernel, preferred_element_type=F32)
    top[...] = total
    for out in (r1, r2, r3):
        out[LD * F :, :] = total.astype(BF)


def far(ids, place, sources, targets, nodes):
    rows = LD * F
    return pl.pallas_call(
        far_kernel,
        in_specs=[SM, SM] + [VM] * 9,
        out_specs=[VM] * 5,
        out_shape=[jax.ShapeDtypeStruct((rows, SK), F32)]
        + [jax.ShapeDtypeStruct((rows + RHS, SK), BF)] * 3
        + [jax.ShapeDtypeStruct((RHS, SK), F32)],
        scratch_shapes=[
            pltpu.VMEM((SIDE * LD, SK, AUG), BF),
            pltpu.VMEM((SIDE * SK, SK), BF),
        ],
        compiler_params=params(),
        cost_estimate=pl.CostEstimate(
            flops=15 * 10**9, bytes_accessed=8 * 10**6, transcendentals=8 * 10**6
        ),
        name="far",
    )(ids, place, *sources, *targets, nodes)


def near_kernel(ids, first, own, before, after, out, side, rights, tile):
    for d, block in enumerate((before, own, after)):

        @pl.loop(0, LD)
        def _(leaf, d=d, block=block):
            side[d * LD + leaf] = source_side(block[leaf, :F, :])
            rights[d * LD + leaf] = block[leaf, F:, :]

    @pl.loop(0, LD)
    def _(leaf):
        points = target_side(own[leaf, :F, :])
        total = jnp.zeros((RHS, LP), F32)
        for group in range(2):
            weights = []
            for d in range(4):
                named = ids[leaf, group * 4 + d]
                at = jnp.clip(named - first[0], 0, 3 * LD - 1)
                tile[d * LP : (d + 1) * LP, :] = jnp.exp(
                    jnp.dot(side[at], points, preferred_element_type=F32)
                ).astype(BF)
                weight = rights[at]
                weights.append(jnp.where(named >= 0, weight, jnp.zeros_like(weight)))
            total += jnp.dot(
                jnp.concatenate(weights, axis=1), tile[...], preferred_element_type=F32
            )
        out[leaf] = total


def near(ids, first, own, before, after):
    return pl.pallas_call(
        near_kernel,
        in_specs=[SM, SM, VM, VM, VM],
        out_specs=VM,
        out_shape=jax.ShapeDtypeStruct((LD, RHS, LP), F32),
        scratch_shapes=[
            pltpu.VMEM((3 * LD, LP, AUG), BF),
            pltpu.VMEM((3 * LD, RHS, LP), BF),
            pltpu.VMEM((4 * LP, LP), BF),
        ],
        compiler_params=params(),
        cost_estimate=pl.CostEstimate(
            flops=30 * 10**9, bytes_accessed=4 * 10**6, transcendentals=16 * 10**6
        ),
        name="near",
    )(ids, first, own, before, after)


def final_kernel(near_sum, basis, transfer, own, r1, r2, r3, t0, q1, q2, q3, out):
    top = t0[...] + q1[...].astype(F32) + q2[...].astype(F32) + q3[...].astype(F32)
    potential = own[...] + r1[...].astype(F32) + r2[...].astype(F32) + r3[...].astype(F32)
    nt = (((1,), (1,)), ((), ()))
    potential += lax.dot_general(top.astype(BF), transfer[0], nt, preferred_element_type=F32)
    far_out = lax.dot_general(potential.astype(BF), basis[0], nt, preferred_element_type=F32)
    out[0] = (near_sum[0] + far_out).astype(BF)


def final(near_sum, basis, transfer, own, returned, top):
    def block(*shape):
        return pl.BlockSpec((1, *shape), lambda i: (i, 0, 0))

    row = pl.BlockSpec((RHS, SK), lambda i: (i, 0))
    zero = pl.BlockSpec((RHS, SK), lambda i: (0, 0))
    last = pl.BlockSpec((RHS, SK), lambda i: (LD, 0))
    return pl.pallas_call(
        final_kernel,
        grid=(LD,),
        in_specs=[block(RHS, LP), block(LP, SK), block(SK, SK)]
        + [row] * 4
        + [zero]
        + [last] * 3,
        out_specs=block(RHS, LP),
        out_shape=jax.ShapeDtypeStruct((LD, RHS, LP), BF),
        compiler_params=params(24),
        cost_estimate=pl.CostEstimate(
            flops=10**9, bytes_accessed=6 * 10**6, transcendentals=0
        ),
        name="final",
    )(near_sum, basis, transfer, own, *returned, top, *returned)


def shifted(value, dx, dz):
    pairs = []
    for x in range(SIDE):
        for z in range(SIDE):
            to = (x + dx) % SIDE * SIDE + (z + dz) % SIDE
            pairs.append((x * SIDE + z, to))
    return lax.ppermute(value, "top", pairs)


def on_device(
    points, right_sides, leaf_basis, transfer, node_points, neighbours, far_sources, skeleton
):
    node, at = lax.axis_index("leaf"), lax.axis_index("top")
    position = node * SIDE * SIDE + at
    near_msg, source_msg, target_msg = prep(
        points, right_sides, leaf_basis, transfer, skeleton, far_sources
    )
    sources = [source_msg]
    sources += [shifted(source_msg, dx, 0) for dx in (1, -1, 2)]
    targets = [target_msg]
    targets += [shifted(target_msg, 0, dz) for dz in (1, -1, 2)]
    count = lax.axis_size("leaf") * lax.axis_size("top")
    up = [(i, i + 1) for i in range(count - 1)]
    before = lax.ppermute(near_msg, ("leaf", "top"), up)
    after = lax.ppermute(near_msg, ("leaf", "top"), [(j, i) for i, j in up])
    row_charge = sum(s[LD * 2 * F :].astype(F32) for s in sources).astype(BF)
    nodes = lax.all_gather(
        jnp.concatenate([row_charge, node_points[0]], axis=0), "leaf", axis=0
    )
    ids = jnp.concatenate([t[LD * F : LD * F + LD, : SIDE * SIDE] for t in targets], axis=0)
    place = jnp.stack([at // SIDE, at % SIDE, node]).astype(jnp.int32)
    own, r1, r2, r3, top = far(ids.astype(jnp.int32), place, sources, targets, nodes)
    returned = [
        shifted(r, 0, dz) for r, dz in ((r1, -1), (r2, 1), (r3, 2))
    ]
    first = ((position - 1) * LD).astype(jnp.int32).reshape(1)
    near_sum = near(neighbours, first, near_msg, before, after)
    return final(near_sum, leaf_basis, transfer, own, returned, top)


def solution(mesh):
    leaves = P(("leaf", "top"), None, None)
    lists = P(("leaf", "top"), None)
    in_specs = (leaves, leaves, leaves, leaves, P("leaf", None, None), lists, lists, lists)
    return jax.shard_map(
        on_device, mesh=mesh, in_specs=in_specs, out_specs=leaves, check_vma=False
    )
```

```python
import functools

import jax
import jax.numpy as jnp
from jax import lax
from jax.experimental import pallas as pl
from jax.experimental.pallas import tpu as pltpu
from jax.sharding import PartitionSpec as P

BF = jnp.bfloat16
F32 = jnp.float32
F = 64
RHS = 64
LP = 512
SK = 256
LD = 8
SIDE = 4
AUG = 128
VM = pl.BlockSpec(memory_space=pltpu.VMEM)
SM = pl.BlockSpec(memory_space=pltpu.SMEM)


def params(mib=40):
    return pltpu.CompilerParams(vmem_limit_bytes=mib * 2**20)


def cost(us):
    return pl.CostEstimate(flops=us * 10**9, bytes_accessed=10**6, transcendentals=0)


def norm_rows(points, first):
    norm = jnp.sum(points * points, axis=0, keepdims=True) * (-2.0 / F)
    high = norm.astype(BF).astype(F32)
    mid = (norm - high).astype(BF).astype(F32)
    low = norm - high - mid
    row = lax.broadcasted_iota(jnp.int32, (16, points.shape[1]), 0)
    at = 0 if first else 3
    ones = jnp.where(row < 6, 1.0, 0.0).astype(F32)
    rows = jnp.where(row == at + 1, mid, jnp.where(row == at + 2, low, ones))
    return jnp.where(row == at, high, rows)


def source_side(points):
    points = points.astype(F32)
    zeros = jnp.zeros((AUG - F - 16, points.shape[1]), F32)
    full = jnp.concatenate([points, norm_rows(points, True), zeros], axis=0)
    return full.astype(BF).T


def target_side(points):
    points = points.astype(F32)
    zeros = jnp.zeros((AUG - F - 16, points.shape[1]), F32)
    full = jnp.concatenate([points * (4.0 / F), norm_rows(points, False), zeros], axis=0)
    return full.astype(BF)


def prep_kernel(
    points, sides, basis, transfer, skeleton, far, near_msg, source_msg, target_msg, node, ids
):
    leaf = pl.program_id(0)
    near_msg[0, :F, :] = points[0]
    near_msg[0, F:, :] = sides[0]
    charge = jnp.dot(sides[0], basis[0], preferred_element_type=F32).astype(BF)
    position = lax.broadcasted_iota(jnp.int32, (LP, SK), 0)
    chosen = jnp.where(position == skeleton[pl.ds(leaf, 1), :], 1.0, 0.0).astype(BF)
    skel = jnp.dot(points[0], chosen, preferred_element_type=F32).astype(BF)
    source_msg[pl.ds(pl.multiple_of(leaf * 2 * F, 2 * F), F), :] = charge
    source_msg[pl.ds(pl.multiple_of(leaf * 2 * F + F, F), F), :] = skel
    target_msg[pl.ds(pl.multiple_of(leaf * F, F), F), :] = skel
    part = jnp.dot(charge, transfer[0], preferred_element_type=F32)

    @pl.when(leaf == 0)
    def _():
        node[...] = part
        ids[...] = jnp.zeros_like(ids)
        named = far[...]
        ids[:LD, : SIDE * SIDE] = jnp.where(named >= 0, named & (LD - 1), -1).astype(F32)
        target_msg[LD * F :, :] = ids[...].astype(BF)

    @pl.when(leaf > 0)
    def _():
        node[...] += part

    @pl.when(leaf == LD - 1)
    def _():
        source_msg[LD * 2 * F :, :] = node[...].astype(BF)


def prep(points, sides, basis, transfer, skeleton, far):
    def block(*shape):
        return pl.BlockSpec((1, *shape), lambda i: (i, 0, 0))

    def whole(*shape):
        return pl.BlockSpec(shape, lambda i: (0,) * len(shape))

    source_rows, target_rows = LD * 2 * F + RHS, LD * F + 16
    return pl.pallas_call(
        prep_kernel,
        grid=(LD,),
        in_specs=[
            block(F, LP),
            block(RHS, LP),
            block(LP, SK),
            block(SK, SK),
            whole(LD, SK),
            whole(LD, SIDE * SIDE),
        ],
        out_specs=[block(2 * F, LP), whole(source_rows, SK), whole(target_rows, SK)],
        out_shape=[
            jax.ShapeDtypeStruct((LD, 2 * F, LP), BF),
            jax.ShapeDtypeStruct((source_rows, SK), BF),
            jax.ShapeDtypeStruct((target_rows, SK), BF),
        ],
        scratch_shapes=[pltpu.VMEM((RHS, SK), F32), pltpu.VMEM((16, SK), F32)],
        compiler_params=params(56),
        cost_estimate=cost(4),
        name="prep",
    )(points, sides, basis, transfer, skeleton, far)


def far_targets(ids, place, side, sources, target, out, b):
    x, z = place[0], place[1]
    shifts = (0, SIDE - 1, 1, 2)

    @pl.loop(0, LD, unroll=2)
    def _(leaf):
        rows = pl.ds(pl.multiple_of(leaf * F, F), F)
        points = target_side(target[rows, :])
        weights, tiles = [], []
        for d, source in enumerate(sources):
            column = lax.rem(x + shifts[d], SIDE) * SIDE + z
            named = ids[b * LD + leaf, column]
            at = jnp.maximum(named, 0)
            tiles.append(
                jnp.exp(
                    jnp.dot(side[d * LD + at], points, preferred_element_type=F32)
                ).astype(BF)
            )
            weight = source[pl.ds(pl.multiple_of(at * 2 * F, 2 * F), RHS), :]
            weights.append(jnp.where(named >= 0, weight, jnp.zeros_like(weight)))
        total = jnp.dot(
            jnp.concatenate(weights, axis=1),
            jnp.concatenate(tiles, axis=0),
            preferred_element_type=F32,
        )
        out[rows, :] = total.astype(out.dtype)


def far_own_kernel(ids, place, s0, s1, s2, s3, t0, out, side):
    sources = (s0, s1, s2, s3)
    for d, source in enumerate(sources):

        @pl.loop(0, LD)
        def _(leaf, d=d, source=source):
            rows = pl.ds(pl.multiple_of(leaf * 2 * F + F, F), F)
            side[d * LD + leaf] = source_side(source[rows, :])

    far_targets(ids, place, side, sources, t0, out, 0)


def far_own(ids, place, sources, target):
    return pl.pallas_call(
        far_own_kernel,
        in_specs=[SM, SM] + [VM] * 5,
        out_specs=[VM] * 2,
        out_shape=[
            jax.ShapeDtypeStruct((LD * F, SK), F32),
            jax.ShapeDtypeStruct((SIDE * LD, SK, AUG), BF),
        ],
        compiler_params=params(16),
        cost_estimate=cost(6),
        name="far_own",
    )(ids, place, *sources, target)


def far_rest_kernel(ids, place, side, s0, s1, s2, s3, gathered, r1, r2, r3):
    z = place[1]
    for b, out in enumerate((r1, r2, r3)):
        other = lax.rem(z + (SIDE - 1, 1, 2)[b], SIDE)
        far_targets(
            ids, place, side, (s0, s1, s2, s3), gathered.at[other], out, b + 1
        )


def far_rest(ids, place, side, sources, gathered):
    return pl.pallas_call(
        far_rest_kernel,
        in_specs=[SM, SM] + [VM] * 6,
        out_specs=[VM] * 3,
        out_shape=[jax.ShapeDtypeStruct((LD * F, SK), BF)] * 3,
        compiler_params=params(16),
        cost_estimate=cost(10),
        name="far_rest",
    )(ids, place, side, *sources, gathered)


def top_kernel(mine, pair, n1, n2, n3, a1, a2, a3, top, r1, r2, r3):
    points = target_side(mine[RHS:, :])
    total = jnp.zeros((RHS, SK), F32)
    rows = 2 * RHS
    others = [pair] + [n.at[i * rows : (i + 1) * rows] for n in (n1, n2, n3) for i in range(2)]
    for other in others:
        kernel = jnp.exp(
            jnp.dot(source_side(other[RHS:, :]), points, preferred_element_type=F32)
        ).astype(BF)
        total += jnp.dot(other[:RHS, :], kernel, preferred_element_type=F32)
    top[...] = total
    for given, out in ((a1, r1), (a2, r2), (a3, r3)):
        out[: LD * F, :] = given[...]
        out[LD * F :, :] = total.astype(BF)


def top_sum(mine, pair, others, parts):
    return pl.pallas_call(
        top_kernel,
        in_specs=[VM] * 8,
        out_specs=[VM] * 4,
        out_shape=[jax.ShapeDtypeStruct((RHS, SK), F32)]
        + [jax.ShapeDtypeStruct((LD * F + RHS, SK), BF)] * 3,
        compiler_params=params(16),
        cost_estimate=cost(2),
        name="top_sum",
    )(mine, pair, *others, *parts)


def near_groups(ids, first, leaf, low, high, points, side, rights, slots):
    count = jnp.int32(0)
    for d in range(ids.shape[1]):
        slots[d] = 0
    for d in range(ids.shape[1]):
        named = ids[leaf, d]
        at = named - first
        here = (named >= 0) & (at >= low) & (at < high)
        slots[count] = jnp.clip(at - low, 0, high - low - 1)
        count += here.astype(jnp.int32)
    size = 4

    def group(g, total):
        weights, tiles = [], []
        for d in range(size):
            k = g * size + d
            at = slots[k]
            tiles.append(
                jnp.exp(jnp.dot(side[at], points, preferred_element_type=F32)).astype(BF)
            )
            weight = rights(at)
            weights.append(jnp.where(k < count, weight, jnp.zeros_like(weight)))
        return total + jnp.dot(
            jnp.concatenate(weights, axis=1),
            jnp.concatenate(tiles, axis=0),
            preferred_element_type=F32,
        )

    return lax.fori_loop(
        0, lax.div(count + size - 1, size), group, jnp.zeros((RHS, LP), F32)
    )


def near_own_kernel(ids, first, own, out, side, slots):
    @pl.loop(0, LD)
    def _(leaf):
        side[leaf] = source_side(own[leaf, :F, :])

    @pl.loop(0, LD)
    def _(leaf):
        points = target_side(own[leaf, :F, :])
        out[leaf] = near_groups(
            ids, first[0], leaf, LD, 2 * LD, points, side, lambda at: own[at, F:, :], slots
        )


def near_own(ids, first, own):
    return pl.pallas_call(
        near_own_kernel,
        in_specs=[SM, SM, VM],
        out_specs=VM,
        out_shape=jax.ShapeDtypeStruct((LD, RHS, LP), F32),
        scratch_shapes=[pltpu.VMEM((LD, LP, AUG), BF), pltpu.SMEM((16,), jnp.int32)],
        compiler_params=params(16),
        cost_estimate=cost(9),
        name="near_own",
    )(ids, first, own)


def near_rest_kernel(ids, first, own, before, after, given, out, side, rights, slots):
    for d, block in enumerate((before, after)):

        @pl.loop(0, LD)
        def _(leaf, d=d, block=block):
            side[d * LD + leaf] = source_side(block[leaf, :F, :])
            rights[d * LD + leaf] = block[leaf, F:, :]

    @pl.loop(0, LD)
    def _(leaf):
        points = target_side(own[leaf, :F, :])
        total = given[leaf]
        for low in (0, 2 * LD):
            base = 0 if low == 0 else LD
            total += near_groups(
                ids, first[0], leaf, low, low + LD, points, side.at[base : base + LD],
                lambda at, base=base: rights[base + at], slots,
            )
        out[leaf] = total


def near_rest(ids, first, own, before, after, given):
    return pl.pallas_call(
        near_rest_kernel,
        in_specs=[SM, SM, VM, VM, VM, VM],
        out_specs=VM,
        out_shape=jax.ShapeDtypeStruct((LD, RHS, LP), F32),
        scratch_shapes=[
            pltpu.VMEM((2 * LD, LP, AUG), BF),
            pltpu.VMEM((2 * LD, RHS, LP), BF),
            pltpu.SMEM((16,), jnp.int32),
        ],
        compiler_params=params(24),
        cost_estimate=cost(11),
        name="near_rest",
    )(ids, first, own, before, after, given)


def final_kernel(near_sum, basis, transfer, own, r1, r2, r3, top, out):
    nt = (((1,), (1,)), ((), ()))
    last = LD * F
    total = top[...]
    for r in (r1, r2, r3):
        total += r[last:, :].astype(F32)
    total = total.astype(BF)

    @pl.loop(0, LD, unroll=2)
    def _(leaf):
        rows = pl.ds(pl.multiple_of(leaf * F, F), F)
        potential = own[rows, :]
        for r in (r1, r2, r3):
            potential += r[rows, :].astype(F32)
        potential += lax.dot_general(total, transfer[leaf], nt, preferred_element_type=F32)
        far_out = lax.dot_general(
            potential.astype(BF), basis[leaf], nt, preferred_element_type=F32
        )
        out[leaf] = (near_sum[leaf] + far_out).astype(BF)


def final(near_sum, basis, transfer, own, returned, top):
    return pl.pallas_call(
        final_kernel,
        in_specs=[VM] * 8,
        out_specs=VM,
        out_shape=jax.ShapeDtypeStruct((LD, RHS, LP), BF),
        compiler_params=params(16),
        cost_estimate=cost(3),
        name="final",
    )(near_sum, basis, transfer, own, *returned, top)


def shifted(value, dx, dz):
    pairs = []
    for x in range(SIDE):
        for z in range(SIDE):
            to = (x + dx) % SIDE * SIDE + (z + dz) % SIDE
            pairs.append((x * SIDE + z, to))
    return lax.ppermute(value, "top", pairs)


def leaf_shifted(value, dy):
    count = lax.axis_size("leaf")
    if dy == 0:
        return lax.ppermute(value, "leaf", [(i, i ^ 1) for i in range(count)])
    return lax.ppermute(value, "leaf", [(i, (i + 2 * dy) % count) for i in range(count)])


def on_device(
    points, right_sides, leaf_basis, transfer, node_points, neighbours, far_sources, skeleton
):
    node, at = lax.axis_index("leaf"), lax.axis_index("top")
    position = node * SIDE * SIDE + at
    near_msg, source_msg, target_msg = prep(
        points, right_sides, leaf_basis, transfer, skeleton, far_sources
    )
    sources = [source_msg]
    sources += [shifted(source_msg, dx, 0) for dx in (1, -1, 2)]
    lines = [[x * SIDE + z for z in range(SIDE)] for x in range(SIDE)]
    gathered = lax.all_gather(target_msg, "top", axis=0, axis_index_groups=lines)
    count = lax.axis_size("leaf") * lax.axis_size("top")
    up = [(i, i + 1) for i in range(count - 1)]
    before = lax.ppermute(near_msg, ("leaf", "top"), up)
    after = lax.ppermute(near_msg, ("leaf", "top"), [(j, i) for i, j in up])
    first = ((position - 1) * LD).astype(jnp.int32).reshape(1)
    near_sum = near_own(neighbours, first, near_msg)

    sources[1:], near_sum = lax.optimization_barrier((sources[1:], near_sum))
    row_charge = sum(s[LD * 2 * F :].astype(F32) for s in sources).astype(BF)
    mine = jnp.concatenate([row_charge, node_points[0]], axis=0)
    pair = leaf_shifted(mine, 0)
    place = jnp.stack([at // SIDE, at % SIDE]).astype(jnp.int32)
    own_ids = jnp.where(far_sources >= 0, far_sources & (LD - 1), -1)
    own, side = far_own(own_ids, place, sources, target_msg)
    both = jnp.concatenate([mine, pair], axis=0)
    others = [leaf_shifted(both, dy) for dy in (1, -1, 2)]
    ids = gathered[:, LD * F : LD * F + LD, : SIDE * SIDE].astype(jnp.int32)
    z = at % SIDE
    order = [z] + [lax.rem(z + d, SIDE) for d in (SIDE - 1, 1, 2)]
    ids = jnp.concatenate([lax.dynamic_index_in_dim(ids, o, keepdims=False) for o in order])
    parts = far_rest(ids, place, side, sources, gathered)
    top, *parts = top_sum(mine, pair, others, parts)
    returned = [shifted(r, 0, dz) for r, dz in zip(parts, (-1, 1, 2))]
    near_sum = near_rest(neighbours, first, near_msg, before, after, near_sum)
    return final(near_sum, leaf_basis, transfer, own, returned, top)


def solution(mesh):
    leaves = P(("leaf", "top"), None, None)
    lists = P(("leaf", "top"), None)
    in_specs = (leaves, leaves, leaves, leaves, P("leaf", None, None), lists, lists, lists)
    return jax.shard_map(
        on_device, mesh=mesh, in_specs=in_specs, out_specs=leaves, check_vma=False
    )
```

```python
import functools

import jax
import jax.numpy as jnp
from jax import lax
from jax.experimental import pallas as pl
from jax.experimental.pallas import tpu as pltpu
from jax.sharding import PartitionSpec as P

BF = jnp.bfloat16
F32 = jnp.float32
F = 64
RHS = 64
LP = 512
SK = 256
LD = 8
SIDE = 4
AUG = 128
VM = pl.BlockSpec(memory_space=pltpu.VMEM)
SM = pl.BlockSpec(memory_space=pltpu.SMEM)


def params(mib=40):
    return pltpu.CompilerParams(vmem_limit_bytes=mib * 2**20)


def cost(us):
    return pl.CostEstimate(flops=us * 10**9, bytes_accessed=10**6, transcendentals=0)


def norm_rows(points, first):
    norm = jnp.sum(points * points, axis=0, keepdims=True) * (-2.0 / F)
    high = norm.astype(BF).astype(F32)
    mid = (norm - high).astype(BF).astype(F32)
    low = norm - high - mid
    row = lax.broadcasted_iota(jnp.int32, (16, points.shape[1]), 0)
    at = 0 if first else 3
    ones = jnp.where(row < 6, 1.0, 0.0).astype(F32)
    rows = jnp.where(row == at + 1, mid, jnp.where(row == at + 2, low, ones))
    return jnp.where(row == at, high, rows)


def source_side(points):
    points = points.astype(F32)
    zeros = jnp.zeros((AUG - F - 16, points.shape[1]), F32)
    full = jnp.concatenate([points, norm_rows(points, True), zeros], axis=0)
    return full.astype(BF).T


def target_side(points):
    points = points.astype(F32)
    zeros = jnp.zeros((AUG - F - 16, points.shape[1]), F32)
    full = jnp.concatenate([points * (4.0 / F), norm_rows(points, False), zeros], axis=0)
    return full.astype(BF)


def prep_kernel(
    points, sides, basis, transfer, skeleton, far, near_msg, source_msg, target_msg,
    own_points, own_sides, own_basis, own_transfer, node, ids, sems, out_sems,
):
    def fetch(leaf):
        pairs = (
            (points, own_points),
            (sides, own_sides),
            (basis, own_basis),
            (transfer, own_transfer),
        )
        return [
            pltpu.make_async_copy(src.at[leaf], dst.at[leaf], sems.at[k, leaf])
            for k, (src, dst) in enumerate(pairs)
        ]

    for leaf in range(LD):
        for copy in fetch(leaf):
            copy.start()
    stacked = [
        pltpu.make_async_copy(points, near_msg.at[:, :F, :], out_sems.at[0]),
        pltpu.make_async_copy(sides, near_msg.at[:, F:, :], out_sems.at[1]),
    ]
    for copy in stacked:
        copy.start()
    ids[...] = jnp.zeros_like(ids)
    named = far[...]
    ids[:LD, : SIDE * SIDE] = jnp.where(named >= 0, named & (LD - 1), -1).astype(F32)
    target_msg[LD * F :, :] = ids[...].astype(BF)
    node[...] = jnp.zeros_like(node)
    position = lax.broadcasted_iota(jnp.int32, (LP, SK), 0)
    for leaf in range(LD):
        for copy in fetch(leaf):
            copy.wait()
        charge = jnp.dot(
            own_sides[leaf], own_basis[leaf], preferred_element_type=F32
        ).astype(BF)
        chosen = jnp.where(position == skeleton[leaf : leaf + 1, :], 1.0, 0.0).astype(BF)
        skel = jnp.dot(own_points[leaf], chosen, preferred_element_type=F32).astype(BF)
        source_msg[leaf * 2 * F : leaf * 2 * F + F, :] = charge
        source_msg[leaf * 2 * F + F : (leaf + 1) * 2 * F, :] = skel
        target_msg[leaf * F : (leaf + 1) * F, :] = skel
        node[...] += jnp.dot(charge, own_transfer[leaf], preferred_element_type=F32)
    source_msg[LD * 2 * F :, :] = node[...].astype(BF)
    for copy in stacked:
        copy.wait()


def prep(points, sides, basis, transfer, skeleton, far):
    anywhere = pl.BlockSpec(memory_space=pl.ANY)
    return pl.pallas_call(
        prep_kernel,
        in_specs=[anywhere] * 4 + [VM] * 2,
        out_specs=[anywhere, VM, VM],
        out_shape=[
            jax.ShapeDtypeStruct((LD, 2 * F, LP), BF),
            jax.ShapeDtypeStruct((LD * 2 * F + RHS, SK), BF),
            jax.ShapeDtypeStruct((LD * F + 16, SK), BF),
        ],
        scratch_shapes=[
            pltpu.VMEM((LD, F, LP), BF),
            pltpu.VMEM((LD, RHS, LP), BF),
            pltpu.VMEM((LD, LP, SK), BF),
            pltpu.VMEM((LD, SK, SK), BF),
            pltpu.VMEM((RHS, SK), F32),
            pltpu.VMEM((16, SK), F32),
            pltpu.SemaphoreType.DMA((4, LD)),
            pltpu.SemaphoreType.DMA((2,)),
        ],
        compiler_params=params(56),
        cost_estimate=cost(4),
        name="prep",
    )(points, sides, basis, transfer, skeleton, far)


def far_total(ids, columns, row, target, side, weight_of):
    points = target_side(target)
    weights, tiles = [], []
    for d, column in enumerate(columns):
        named = ids[row, column]
        at = jnp.maximum(named, 0)
        tiles.append(
            jnp.exp(
                jnp.dot(side[d * LD + at], points, preferred_element_type=F32)
            ).astype(BF)
        )
        weight = weight_of(d, at)
        weights.append(jnp.where(named >= 0, weight, jnp.zeros_like(weight)))
    if len(weights) == 1:
        return jnp.dot(weights[0], tiles[0], preferred_element_type=F32)
    return jnp.dot(
        jnp.concatenate(weights, axis=1),
        jnp.concatenate(tiles, axis=0),
        preferred_element_type=F32,
    )


def rows_of(leaf):
    return pl.ds(pl.multiple_of(leaf * F, F), F)


def charges_at(source, leaf):
    return source[pl.ds(pl.multiple_of(leaf * 2 * F, 2 * F), RHS), :]


def skeleton_at(source, leaf):
    return source[pl.ds(pl.multiple_of(leaf * 2 * F + F, F), F), :]


def columns_of(place, shifts):
    x, z = place[0], place[1]
    return [x * SIDE + lax.rem(z + shift, SIDE) for shift in shifts]


def far_loop(ids, place, side, sources, targets, outs, base):
    columns = columns_of(place, (0, SIDE - 1, 1))
    for b, (target, out) in enumerate(zip(targets, outs)):

        @pl.loop(0, LD, unroll=2)
        def _(leaf, b=b, target=target, out=out):
            out[rows_of(leaf), :] = far_total(
                ids, columns, (base + b) * LD + leaf, target[rows_of(leaf), :], side,
                lambda d, at: charges_at(sources[d], at),
            )


def far_a_kernel(ids, place, s0, s1, s2, t0, t1, o0, o1, side):
    for d, source in enumerate((s0, s1, s2)):

        @pl.loop(0, LD, unroll=2)
        def _(leaf, d=d, source=source):
            side[d * LD + leaf] = source_side(skeleton_at(source, leaf))

    far_loop(ids, place, side, (s0, s1, s2), (t0, t1), (o0, o1), 0)


def far_a(ids, place, sources, targets):
    return pl.pallas_call(
        far_a_kernel,
        in_specs=[SM, SM] + [VM] * 5,
        out_specs=[VM] * 3,
        out_shape=[jax.ShapeDtypeStruct((LD * F, SK), F32)] * 2
        + [jax.ShapeDtypeStruct((3 * LD, SK, AUG), BF)],
        compiler_params=params(16),
        cost_estimate=cost(7),
        name="far_a",
    )(ids, place, *sources, *targets)


def far_b_kernel(ids, place, side, s0, s1, s2, t2, t3, o2, o3):
    far_loop(ids, place, side, (s0, s1, s2), (t2, t3), (o2, o3), 2)


def far_b(ids, place, side, sources, targets):
    return pl.pallas_call(
        far_b_kernel,
        in_specs=[SM, SM] + [VM] * 6,
        out_specs=[VM] * 2,
        out_shape=[jax.ShapeDtypeStruct((LD * F, SK), F32)] * 2,
        compiler_params=params(16),
        cost_estimate=cost(5),
        name="far_b",
    )(ids, place, side, *sources, *targets)


def far_c_kernel(
    ids, place, low, high, t0, t1, t2, t3, a0, a1, a2, a3, own, r1, r2, r3, side, weights
):
    half = LD // 2
    for d, source in enumerate((low, high)):

        @pl.loop(0, half, unroll=2)
        def _(leaf, d=d, source=source):
            side[d * half + leaf] = source_side(skeleton_at(source, leaf))
            weights[d * half + leaf] = charges_at(source, leaf)

    columns = columns_of(place, (2,))
    given = (a0, a1, a2, a3)
    for b, (target, out) in enumerate(zip((t0, t1, t2, t3), (own, r1, r2, r3))):

        @pl.loop(0, LD, unroll=4)
        def _(leaf, b=b, target=target, out=out):
            total = far_total(
                ids, columns, b * LD + leaf, target[rows_of(leaf), :], side,
                lambda d, at: weights[at],
            )
            out[rows_of(leaf), :] = (given[b][rows_of(leaf), :] + total).astype(out.dtype)


def far_c(ids, place, halves, targets, given):
    return pl.pallas_call(
        far_c_kernel,
        in_specs=[SM, SM] + [VM] * 10,
        out_specs=[VM] * 4,
        out_shape=[jax.ShapeDtypeStruct((LD * F, SK), F32)]
        + [jax.ShapeDtypeStruct((LD * F, SK), BF)] * 3,
        scratch_shapes=[
            pltpu.VMEM((LD, SK, AUG), BF),
            pltpu.VMEM((LD, RHS, SK), BF),
        ],
        compiler_params=params(16),
        cost_estimate=cost(5),
        name="far_c",
    )(ids, place, *halves, *targets, *given)


def top_kernel(mine, pair, n1, n2, n3, a1, a2, a3, top, r1, r2, r3):
    points = target_side(mine[RHS:, :])
    total = jnp.zeros((RHS, SK), F32)
    rows = 2 * RHS
    others = [pair] + [n.at[i * rows : (i + 1) * rows] for n in (n1, n2, n3) for i in range(2)]
    for other in others:
        kernel = jnp.exp(
            jnp.dot(source_side(other[RHS:, :]), points, preferred_element_type=F32)
        ).astype(BF)
        total += jnp.dot(other[:RHS, :], kernel, preferred_element_type=F32)
    top[...] = total
    for given, out in ((a1, r1), (a2, r2), (a3, r3)):
        out[: LD * F, :] = given[...]
        out[LD * F :, :] = total.astype(BF)


def top_sum(mine, pair, others, parts):
    return pl.pallas_call(
        top_kernel,
        in_specs=[VM] * 8,
        out_specs=[VM] * 4,
        out_shape=[jax.ShapeDtypeStruct((RHS, SK), F32)]
        + [jax.ShapeDtypeStruct((LD * F + RHS, SK), BF)] * 3,
        compiler_params=params(16),
        cost_estimate=cost(2),
        name="top_sum",
    )(mine, pair, *others, *parts)


def near_groups(ids, leaf, place_of, points, side, rights, slots):
    count = jnp.int32(0)
    for d in range(ids.shape[1]):
        slots[d] = 0
    for d in range(ids.shape[1]):
        here, at = place_of(ids[leaf, d])
        slots[count] = jnp.where(here, at, 0)
        count += here.astype(jnp.int32)
    size = 4

    def group(g, total):
        weights, tiles = [], []
        for d in range(size):
            k = g * size + d
            at = slots[k]
            tiles.append(
                jnp.exp(jnp.dot(side[at], points, preferred_element_type=F32)).astype(BF)
            )
            weight = rights(at)
            weights.append(jnp.where(k < count, weight, jnp.zeros_like(weight)))
        return total + jnp.dot(
            jnp.concatenate(weights, axis=1),
            jnp.concatenate(tiles, axis=0),
            preferred_element_type=F32,
        )

    return lax.fori_loop(
        0, lax.div(count + size - 1, size), group, jnp.zeros((RHS, LP), F32)
    )


def near_own_kernel(ids, first, own, out, side, slots):
    @pl.loop(0, LD, unroll=2)
    def _(leaf):
        side[leaf] = source_side(own[leaf, :F, :])

    def place_of(named):
        at = named - first[0]
        return (named >= 0) & (at >= 0) & (at < LD), at

    @pl.loop(0, LD)
    def _(leaf):
        points = target_side(own[leaf, :F, :])
        out[leaf] = near_groups(
            ids, leaf, place_of, points, side, lambda at: own[at, F:, :], slots
        )


def near_own(ids, first, own):
    return pl.pallas_call(
        near_own_kernel,
        in_specs=[SM, SM, VM],
        out_specs=VM,
        out_shape=jax.ShapeDtypeStruct((LD, RHS, LP), F32),
        scratch_shapes=[pltpu.VMEM((LD, LP, AUG), BF), pltpu.SMEM((16,), jnp.int32)],
        compiler_params=params(16),
        cost_estimate=cost(9),
        name="near_own",
    )(ids, first, own)


def near_rest_kernel(ids, first, own, before, after, given, out, side, rights, slots):
    for d, block in enumerate((before, after)):

        @pl.loop(0, LD, unroll=2)
        def _(leaf, d=d, block=block):
            side[d * LD + leaf] = source_side(block[leaf, :F, :])
            rights[d * LD + leaf] = block[leaf, F:, :]

    def place_of(named):
        at = named - first[0]
        below = (at >= -LD) & (at < 0)
        above = (at >= LD) & (at < 2 * LD)
        return (named >= 0) & (below | above), jnp.where(below, at + LD, at)

    @pl.loop(0, LD)
    def _(leaf):
        points = target_side(own[leaf, :F, :])
        out[leaf] = given[leaf] + near_groups(
            ids, leaf, place_of, points, side, lambda at: rights[at], slots
        )


def near_rest(ids, first, own, before, after, given):
    return pl.pallas_call(
        near_rest_kernel,
        in_specs=[SM, SM, VM, VM, VM, VM],
        out_specs=VM,
        out_shape=jax.ShapeDtypeStruct((LD, RHS, LP), F32),
        scratch_shapes=[
            pltpu.VMEM((2 * LD, LP, AUG), BF),
            pltpu.VMEM((2 * LD, RHS, LP), BF),
            pltpu.SMEM((16,), jnp.int32),
        ],
        compiler_params=params(24),
        cost_estimate=cost(11),
        name="near_rest",
    )(ids, first, own, before, after, given)


def final_kernel(near_sum, basis, transfer, own, r1, r2, r3, top, out):
    nt = (((1,), (1,)), ((), ()))
    last = LD * F
    total = top[...]
    for r in (r1, r2, r3):
        total += r[last:, :].astype(F32)
    total = total.astype(BF)

    @pl.loop(0, LD, unroll=2)
    def _(leaf):
        rows = pl.ds(pl.multiple_of(leaf * F, F), F)
        potential = own[rows, :]
        for r in (r1, r2, r3):
            potential += r[rows, :].astype(F32)
        potential += lax.dot_general(total, transfer[leaf], nt, preferred_element_type=F32)
        far_out = lax.dot_general(
            potential.astype(BF), basis[leaf], nt, preferred_element_type=F32
        )
        out[leaf] = (near_sum[leaf] + far_out).astype(BF)


def final(near_sum, basis, transfer, own, returned, top):
    return pl.pallas_call(
        final_kernel,
        in_specs=[VM] * 8,
        out_specs=VM,
        out_shape=jax.ShapeDtypeStruct((LD, RHS, LP), BF),
        compiler_params=params(16),
        cost_estimate=cost(3),
        name="final",
    )(near_sum, basis, transfer, own, *returned, top)


def shifted(value, dx, dz):
    pairs = []
    for x in range(SIDE):
        for z in range(SIDE):
            to = (x + dx) % SIDE * SIDE + (z + dz) % SIDE
            pairs.append((x * SIDE + z, to))
    return lax.ppermute(value, "top", pairs)


def leaf_shifted(value, dy):
    count = lax.axis_size("leaf")
    if dy == 0:
        return lax.ppermute(value, "leaf", [(i, i ^ 1) for i in range(count)])
    return lax.ppermute(value, "leaf", [(i, (i + 2 * dy) % count) for i in range(count)])


def on_device(
    points, right_sides, leaf_basis, transfer, node_points, neighbours, far_sources, skeleton
):
    node, at = lax.axis_index("leaf"), lax.axis_index("top")
    position = node * SIDE * SIDE + at
    near_msg, source_msg, target_msg = prep(
        points, right_sides, leaf_basis, transfer, skeleton, far_sources
    )
    sources = [source_msg] + [shifted(source_msg, 0, dz) for dz in (1, -1)]
    targets = [target_msg] + [shifted(target_msg, dx, 0) for dx in (1, -1, 2)]
    first = (position * LD).astype(jnp.int32).reshape(1)
    near_sum = near_own(neighbours, first, near_msg)

    sources, targets, near_msg, near_sum = lax.optimization_barrier(
        (sources, targets, near_msg, near_sum)
    )
    half = LD * F
    low = shifted(sources[1][:half], 0, 1)
    high = shifted(sources[2][half:], 0, -1)
    count = lax.axis_size("leaf") * lax.axis_size("top")
    up = [(i, i + 1) for i in range(count - 1)]
    before = lax.ppermute(near_msg, ("leaf", "top"), up)
    after = lax.ppermute(near_msg, ("leaf", "top"), [(j, i) for i, j in up])
    ids = jnp.concatenate([t[LD * F : LD * F + LD, : SIDE * SIDE] for t in targets])
    ids = ids.astype(jnp.int32)
    place = jnp.stack([at // SIDE, at % SIDE]).astype(jnp.int32)
    part0, part1, side = far_a(ids, place, sources, targets[:2])

    low, high, part0, part1, side = lax.optimization_barrier((low, high, part0, part1, side))
    line_charge = sum(s[2 * half :].astype(F32) for s in sources) + high[half:].astype(F32)
    mine = jnp.concatenate([line_charge.astype(BF), node_points[0]], axis=0)
    pair = leaf_shifted(mine, 0)
    part2, part3 = far_b(ids, place, side, sources, targets[2:])
    pair, part2, part3 = lax.optimization_barrier((pair, part2, part3))
    both = jnp.concatenate([mine, pair], axis=0)
    others = [leaf_shifted(both, dy) for dy in (1, -1, 2)]
    own, *parts = far_c(ids, place, (low, high), targets, (part0, part1, part2, part3))
    top, *parts = top_sum(mine, pair, others, parts)
    returned = [shifted(r, dx, 0) for r, dx in zip(parts, (-1, 1, 2))]
    near_sum = near_rest(neighbours, first, near_msg, before, after, near_sum)
    return final(near_sum, leaf_basis, transfer, own, returned, top)


def solution(mesh):
    leaves = P(("leaf", "top"), None, None)
    lists = P(("leaf", "top"), None)
    in_specs = (leaves, leaves, leaves, leaves, P("leaf", None, None), lists, lists, lists)
    return jax.shard_map(
        on_device, mesh=mesh, in_specs=in_specs, out_specs=leaves, check_vma=False
    )
```

```python
import functools

import jax
import jax.numpy as jnp
from jax import lax
from jax.experimental import pallas as pl
from jax.experimental.pallas import tpu as pltpu
from jax.sharding import PartitionSpec as P

BF = jnp.bfloat16
F32 = jnp.float32
F = 64
RHS = 64
LP = 512
SK = 256
LD = 8
SIDE = 4
AUG = 128
UNROLL = 2
VM = pl.BlockSpec(memory_space=pltpu.VMEM)
SM = pl.BlockSpec(memory_space=pltpu.SMEM)


def params(mib=40):
    return pltpu.CompilerParams(vmem_limit_bytes=mib * 2**20)


def cost(us):
    return pl.CostEstimate(flops=us * 10**9, bytes_accessed=10**6, transcendentals=0)


def norm_rows(points, first):
    norm = jnp.sum(points * points, axis=0, keepdims=True) * (-2.0 / F)
    high = norm.astype(BF).astype(F32)
    mid = (norm - high).astype(BF).astype(F32)
    low = norm - high - mid
    row = lax.broadcasted_iota(jnp.int32, (16, points.shape[1]), 0)
    at = 0 if first else 3
    ones = jnp.where(row < 6, 1.0, 0.0).astype(F32)
    rows = jnp.where(row == at + 1, mid, jnp.where(row == at + 2, low, ones))
    return jnp.where(row == at, high, rows)


def source_side(points):
    points = points.astype(F32)
    zeros = jnp.zeros((AUG - F - 16, points.shape[1]), F32)
    full = jnp.concatenate([points, norm_rows(points, True), zeros], axis=0)
    return full.astype(BF).T


def target_side(points):
    points = points.astype(F32)
    zeros = jnp.zeros((AUG - F - 16, points.shape[1]), F32)
    full = jnp.concatenate([points * (4.0 / F), norm_rows(points, False), zeros], axis=0)
    return full.astype(BF)


def prep_kernel(
    points, sides, basis, transfer, skeleton, far, near_msg, source_msg, target_msg,
    own_basis, own_transfer, node, ids, sems,
):
    def fetch(leaf):
        pairs = (
            (points, near_msg.at[leaf, :F, :]),
            (sides, near_msg.at[leaf, F:, :]),
            (basis, own_basis.at[leaf]),
            (transfer, own_transfer.at[leaf]),
        )
        return [
            pltpu.make_async_copy(src.at[leaf], dst, sems.at[k, leaf])
            for k, (src, dst) in enumerate(pairs)
        ]

    for leaf in range(LD):
        for copy in fetch(leaf):
            copy.start()
    ids[...] = jnp.zeros_like(ids)
    named = far[...]
    ids[:LD, : SIDE * SIDE] = jnp.where(named >= 0, named & (LD - 1), -1).astype(F32)
    target_msg[LD * F :, :] = ids[...].astype(BF)
    position = lax.broadcasted_iota(jnp.int32, (LP, SK), 0)
    node[...] = jnp.zeros_like(node)
    for leaf in range(LD):
        for copy in fetch(leaf):
            copy.wait()
        charge = jnp.dot(
            near_msg[leaf, F:, :], own_basis[leaf], preferred_element_type=F32
        ).astype(BF)
        chosen = jnp.where(position == skeleton[leaf : leaf + 1, :], 1.0, 0.0).astype(BF)
        skel = jnp.dot(near_msg[leaf, :F, :], chosen, preferred_element_type=F32).astype(BF)
        source_msg[leaf * 2 * F : leaf * 2 * F + F, :] = charge
        source_msg[leaf * 2 * F + F : (leaf + 1) * 2 * F, :] = skel
        target_msg[leaf * F : (leaf + 1) * F, :] = skel
        node[...] += jnp.dot(charge, own_transfer[leaf], preferred_element_type=F32)
    source_msg[LD * 2 * F :, :] = node[...].astype(BF)


def prep(points, sides, basis, transfer, skeleton, far):
    anywhere = pl.BlockSpec(memory_space=pl.ANY)
    return pl.pallas_call(
        prep_kernel,
        in_specs=[anywhere] * 4 + [VM] * 2,
        out_specs=[VM] * 3,
        out_shape=[
            jax.ShapeDtypeStruct((LD, 2 * F, LP), BF),
            jax.ShapeDtypeStruct((LD * 2 * F + RHS, SK), BF),
            jax.ShapeDtypeStruct((LD * F + 16, SK), BF),
        ],
        scratch_shapes=[
            pltpu.VMEM((LD, LP, SK), BF),
            pltpu.VMEM((LD, SK, SK), BF),
            pltpu.VMEM((RHS, SK), F32),
            pltpu.VMEM((16, SK), F32),
            pltpu.SemaphoreType.DMA((4, LD)),
        ],
        compiler_params=params(56),
        cost_estimate=cost(4),
        name="prep",
    )(points, sides, basis, transfer, skeleton, far)


def far_total(ids, columns, row, target, side, weight_of):
    points = target_side(target)
    weights, tiles = [], []
    for d, column in enumerate(columns):
        named = ids[row, column]
        at = jnp.maximum(named, 0)
        tiles.append(
            jnp.exp(
                jnp.dot(side[d * LD + at], points, preferred_element_type=F32)
            ).astype(BF)
        )
        weight = weight_of(d, at)
        weights.append(jnp.where(named >= 0, weight, jnp.zeros_like(weight)))
    if len(weights) == 1:
        return jnp.dot(weights[0], tiles[0], preferred_element_type=F32)
    return jnp.dot(
        jnp.concatenate(weights, axis=1),
        jnp.concatenate(tiles, axis=0),
        preferred_element_type=F32,
    )


def rows_of(leaf):
    return pl.ds(pl.multiple_of(leaf * F, F), F)


def charges_at(source, leaf):
    return source[pl.ds(pl.multiple_of(leaf * 2 * F, 2 * F), RHS), :]


def skeleton_at(source, leaf):
    return source[pl.ds(pl.multiple_of(leaf * 2 * F + F, F), F), :]


def columns_of(place):
    x, z = place[0], place[1]
    return [lax.rem(x + shift, SIDE) * SIDE + z for shift in (0, SIDE - 1, 1, 2)]


def far_loop(ids, place, side, sources, targets, outs, base):
    columns = columns_of(place)
    for b, (target, out) in enumerate(zip(targets, outs)):

        @pl.loop(0, LD, unroll=UNROLL)
        def _(leaf, b=b, target=target, out=out):
            out[rows_of(leaf), :] = far_total(
                ids, columns, (base + b) * LD + leaf, target[rows_of(leaf), :], side,
                lambda d, at: charges_at(sources[d], at),
            ).astype(out.dtype)


def far_a_kernel(ids, place, s0, s1, s2, s3, t0, t1, o0, o1, side):
    for d, source in enumerate((s0, s1, s2, s3)):

        @pl.loop(0, LD, unroll=UNROLL)
        def _(leaf, d=d, source=source):
            side[d * LD + leaf] = source_side(skeleton_at(source, leaf))

    far_loop(ids, place, side, (s0, s1, s2, s3), (t0, t1), (o0, o1), 0)


def far_a(ids, place, sources, targets):
    return pl.pallas_call(
        far_a_kernel,
        in_specs=[SM, SM] + [VM] * 6,
        out_specs=[VM] * 3,
        out_shape=[
            jax.ShapeDtypeStruct((LD * F, SK), F32),
            jax.ShapeDtypeStruct((LD * F, SK), BF),
            jax.ShapeDtypeStruct((SIDE * LD, SK, AUG), BF),
        ],
        compiler_params=params(16),
        cost_estimate=cost(9),
        name="far_a",
    )(ids, place, *sources, *targets)


def far_b_kernel(ids, place, side, s0, s1, s2, s3, t2, t3, o2, o3):
    far_loop(ids, place, side, (s0, s1, s2, s3), (t2, t3), (o2, o3), 2)


def far_b(ids, place, side, sources, targets):
    return pl.pallas_call(
        far_b_kernel,
        in_specs=[SM, SM] + [VM] * 7,
        out_specs=[VM] * 2,
        out_shape=[jax.ShapeDtypeStruct((LD * F, SK), BF)] * 2,
        compiler_params=params(16),
        cost_estimate=cost(7),
        name="far_b",
    )(ids, place, side, *sources, *targets)


def top_kernel(mine, pair, n1, n2, n3, a1, a2, a3, top, r1, r2, r3):
    points = target_side(mine[RHS:, :])
    total = jnp.zeros((RHS, SK), F32)
    rows = 2 * RHS
    others = [pair] + [n.at[i * rows : (i + 1) * rows] for n in (n1, n2, n3) for i in range(2)]
    for other in others:
        kernel = jnp.exp(
            jnp.dot(source_side(other[RHS:, :]), points, preferred_element_type=F32)
        ).astype(BF)
        total += jnp.dot(other[:RHS, :], kernel, preferred_element_type=F32)
    top[...] = total
    for given, out in ((a1, r1), (a2, r2), (a3, r3)):
        out[: LD * F, :] = given[...]
        out[LD * F :, :] = total.astype(BF)


def top_sum(mine, pair, others, parts):
    return pl.pallas_call(
        top_kernel,
        in_specs=[VM] * 8,
        out_specs=[VM] * 4,
        out_shape=[jax.ShapeDtypeStruct((RHS, SK), F32)]
        + [jax.ShapeDtypeStruct((LD * F + RHS, SK), BF)] * 3,
        compiler_params=params(16),
        cost_estimate=cost(2),
        name="top_sum",
    )(mine, pair, *others, *parts)


def near_groups(ids, leaf, place_of, points, side, rights, slots):
    count = jnp.int32(0)
    for d in range(ids.shape[1]):
        slots[d] = 0
    for d in range(ids.shape[1]):
        here, at = place_of(ids[leaf, d])
        slots[count] = jnp.where(here, at, 0)
        count += here.astype(jnp.int32)
    size = 4

    def group(g, total):
        weights, tiles = [], []
        for d in range(size):
            k = g * size + d
            at = slots[k]
            tiles.append(
                jnp.exp(jnp.dot(side[at], points, preferred_element_type=F32)).astype(BF)
            )
            weight = rights(at)
            weights.append(jnp.where(k < count, weight, jnp.zeros_like(weight)))
        return total + jnp.dot(
            jnp.concatenate(weights, axis=1),
            jnp.concatenate(tiles, axis=0),
            preferred_element_type=F32,
        )

    return lax.fori_loop(
        0, lax.div(count + size - 1, size), group, jnp.zeros((RHS, LP), F32)
    )


def near_own_kernel(ids, first, own, out, side, slots):
    @pl.loop(0, LD, unroll=2)
    def _(leaf):
        side[leaf] = source_side(own[leaf, :F, :])

    def place_of(named):
        at = named - first[0]
        return (named >= 0) & (at >= 0) & (at < LD), at

    @pl.loop(0, LD)
    def _(leaf):
        points = target_side(own[leaf, :F, :])
        out[leaf] = near_groups(
            ids, leaf, place_of, points, side, lambda at: own[at, F:, :], slots
        )


def near_own(ids, first, own):
    return pl.pallas_call(
        near_own_kernel,
        in_specs=[SM, SM, VM],
        out_specs=VM,
        out_shape=jax.ShapeDtypeStruct((LD, RHS, LP), F32),
        scratch_shapes=[pltpu.VMEM((LD, LP, AUG), BF), pltpu.SMEM((16,), jnp.int32)],
        compiler_params=params(16),
        cost_estimate=cost(9),
        name="near_own",
    )(ids, first, own)


def near_rest_kernel(ids, first, own, before, after, given, out, side, rights, slots):
    for d, block in enumerate((before, after)):

        @pl.loop(0, LD, unroll=2)
        def _(leaf, d=d, block=block):
            side[d * LD + leaf] = source_side(block[leaf, :F, :])
            rights[d * LD + leaf] = block[leaf, F:, :]

    def place_of(named):
        at = named - first[0]
        below = (at >= -LD) & (at < 0)
        above = (at >= LD) & (at < 2 * LD)
        return (named >= 0) & (below | above), jnp.where(below, at + LD, at)

    @pl.loop(0, LD)
    def _(leaf):
        points = target_side(own[leaf, :F, :])
        out[leaf] = given[leaf] + near_groups(
            ids, leaf, place_of, points, side, lambda at: rights[at], slots
        )


def near_rest(ids, first, own, before, after, given):
    return pl.pallas_call(
        near_rest_kernel,
        in_specs=[SM, SM, VM, VM, VM, VM],
        out_specs=VM,
        out_shape=jax.ShapeDtypeStruct((LD, RHS, LP), F32),
        scratch_shapes=[
            pltpu.VMEM((2 * LD, LP, AUG), BF),
            pltpu.VMEM((2 * LD, RHS, LP), BF),
            pltpu.SMEM((16,), jnp.int32),
        ],
        compiler_params=params(24),
        cost_estimate=cost(11),
        name="near_rest",
    )(ids, first, own, before, after, given)


def final_kernel(near_sum, basis, transfer, own, r1, r2, r3, top, out):
    nt = (((1,), (1,)), ((), ()))
    last = LD * F
    total = top[...]
    for r in (r1, r2, r3):
        total += r[last:, :].astype(F32)
    total = total.astype(BF)

    @pl.loop(0, LD, unroll=2)
    def _(leaf):
        rows = pl.ds(pl.multiple_of(leaf * F, F), F)
        potential = own[rows, :]
        for r in (r1, r2, r3):
            potential += r[rows, :].astype(F32)
        potential += lax.dot_general(total, transfer[leaf], nt, preferred_element_type=F32)
        far_out = lax.dot_general(
            potential.astype(BF), basis[leaf], nt, preferred_element_type=F32
        )
        out[leaf] = (near_sum[leaf] + far_out).astype(BF)


def final(near_sum, basis, transfer, own, returned, top):
    return pl.pallas_call(
        final_kernel,
        in_specs=[VM] * 8,
        out_specs=VM,
        out_shape=jax.ShapeDtypeStruct((LD, RHS, LP), BF),
        compiler_params=params(16),
        cost_estimate=cost(3),
        name="final",
    )(near_sum, basis, transfer, own, *returned, top)


def shifted(value, dx, dz):
    pairs = []
    for x in range(SIDE):
        for z in range(SIDE):
            to = (x + dx) % SIDE * SIDE + (z + dz) % SIDE
            pairs.append((x * SIDE + z, to))
    return lax.ppermute(value, "top", pairs)


def leaf_shifted(value, dy):
    count = lax.axis_size("leaf")
    if dy == 0:
        return lax.ppermute(value, "leaf", [(i, i ^ 1) for i in range(count)])
    return lax.ppermute(value, "leaf", [(i, (i + 2 * dy) % count) for i in range(count)])


def on_device(
    points, right_sides, leaf_basis, transfer, node_points, neighbours, far_sources, skeleton
):
    node, at = lax.axis_index("leaf"), lax.axis_index("top")
    position = node * SIDE * SIDE + at
    near_msg, source_msg, target_msg = prep(
        points, right_sides, leaf_basis, transfer, skeleton, far_sources
    )
    sources = [source_msg] + [shifted(source_msg, dx, 0) for dx in (1, -1, 2)]
    targets = [target_msg] + [shifted(target_msg, 0, dz) for dz in (1, -1)]
    first = (position * LD).astype(jnp.int32).reshape(1)
    near_sum = near_own(neighbours, first, near_msg)

    targets, target_msg, near_msg, near_sum = lax.optimization_barrier(
        (targets, target_msg, near_msg, near_sum)
    )
    targets.append(shifted(target_msg, 0, 2))
    count = lax.axis_size("leaf") * lax.axis_size("top")
    up = [(i, i + 1) for i in range(count - 1)]
    before = lax.ppermute(near_msg, ("leaf", "top"), up)
    after = lax.ppermute(near_msg, ("leaf", "top"), [(j, i) for i, j in up])

    sources, near_sum = lax.optimization_barrier((sources, near_sum))
    line_charge = sum(s[2 * LD * F :].astype(F32) for s in sources)
    mine = jnp.concatenate([line_charge.astype(BF), node_points[0]], axis=0)
    pair = leaf_shifted(mine, 0)
    ids = jnp.concatenate([t[LD * F : LD * F + LD, : SIDE * SIDE] for t in targets])
    ids = ids.astype(jnp.int32)
    place = jnp.stack([at // SIDE, at % SIDE]).astype(jnp.int32)
    own, part1, side = far_a(ids, place, sources, targets[:2])
    pair, own, side = lax.optimization_barrier((pair, own, side))
    both = jnp.concatenate([mine, pair], axis=0)
    others = [leaf_shifted(both, dy) for dy in (1, -1, 2)]
    parts = [part1] + list(far_b(ids, place, side, sources, targets[2:]))
    top, *parts = top_sum(mine, pair, others, parts)
    returned = [shifted(r, 0, dz) for r, dz in zip(parts, (-1, 1, 2))]
    near_sum = near_rest(neighbours, first, near_msg, before, after, near_sum)
    return final(near_sum, leaf_basis, transfer, own, returned, top)


def solution(mesh):
    leaves = P(("leaf", "top"), None, None)
    lists = P(("leaf", "top"), None)
    in_specs = (leaves, leaves, leaves, leaves, P("leaf", None, None), lists, lists, lists)
    return jax.shard_map(
        on_device, mesh=mesh, in_specs=in_specs, out_specs=leaves, check_vma=False
    )
```

```python
import functools

import jax
import jax.numpy as jnp
from jax import lax
from jax.experimental import pallas as pl
from jax.experimental.pallas import tpu as pltpu
from jax.sharding import PartitionSpec as P

BF = jnp.bfloat16
F32 = jnp.float32
F = 64
RHS = 64
LP = 512
SK = 256
LD = 8
SIDE = 4
AUG = 128
UNROLL = 8
VM = pl.BlockSpec(memory_space=pltpu.VMEM)
SM = pl.BlockSpec(memory_space=pltpu.SMEM)


def params(mib=40):
    return pltpu.CompilerParams(vmem_limit_bytes=mib * 2**20)


def cost(us):
    return pl.CostEstimate(flops=us * 10**9, bytes_accessed=10**6, transcendentals=0)


def norm_rows(points, first):
    norm = jnp.sum(points * points, axis=0, keepdims=True) * (-2.0 / F)
    high = norm.astype(BF).astype(F32)
    mid = (norm - high).astype(BF).astype(F32)
    low = norm - high - mid
    row = lax.broadcasted_iota(jnp.int32, (16, points.shape[1]), 0)
    at = 0 if first else 3
    ones = jnp.where(row < 6, 1.0, 0.0).astype(F32)
    rows = jnp.where(row == at + 1, mid, jnp.where(row == at + 2, low, ones))
    return jnp.where(row == at, high, rows)


def source_side(points):
    points = points.astype(F32)
    zeros = jnp.zeros((AUG - F - 16, points.shape[1]), F32)
    full = jnp.concatenate([points, norm_rows(points, True), zeros], axis=0)
    return full.astype(BF).T


def target_side(points):
    points = points.astype(F32)
    zeros = jnp.zeros((AUG - F - 16, points.shape[1]), F32)
    full = jnp.concatenate([points * (4.0 / F), norm_rows(points, False), zeros], axis=0)
    return full.astype(BF)


def prep_kernel(
    points, sides, basis, transfer, skeleton, far, near_msg, source_msg, target_msg,
    own_basis, own_transfer, node, ids, sems,
):
    def fetch(leaf):
        pairs = (
            (points, near_msg.at[leaf, :F, :]),
            (sides, near_msg.at[leaf, F:, :]),
            (basis, own_basis.at[leaf]),
            (transfer, own_transfer.at[leaf]),
        )
        return [
            pltpu.make_async_copy(src.at[leaf], dst, sems.at[k, leaf])
            for k, (src, dst) in enumerate(pairs)
        ]

    for leaf in range(LD):
        for copy in fetch(leaf):
            copy.start()
    ids[...] = jnp.zeros_like(ids)
    named = far[...]
    ids[:LD, : SIDE * SIDE] = jnp.where(named >= 0, named & (LD - 1), -1).astype(F32)
    target_msg[LD * F :, :] = ids[...].astype(BF)
    position = lax.broadcasted_iota(jnp.int32, (LP, SK), 0)
    node[...] = jnp.zeros_like(node)
    for leaf in range(LD):
        for copy in fetch(leaf):
            copy.wait()
        charge = jnp.dot(
            near_msg[leaf, F:, :], own_basis[leaf], preferred_element_type=F32
        ).astype(BF)
        chosen = jnp.where(position == skeleton[leaf : leaf + 1, :], 1.0, 0.0).astype(BF)
        skel = jnp.dot(near_msg[leaf, :F, :], chosen, preferred_element_type=F32).astype(BF)
        source_msg[leaf * 2 * F : leaf * 2 * F + F, :] = charge
        source_msg[leaf * 2 * F + F : (leaf + 1) * 2 * F, :] = skel
        target_msg[leaf * F : (leaf + 1) * F, :] = skel
        node[...] += jnp.dot(charge, own_transfer[leaf], preferred_element_type=F32)
    source_msg[LD * 2 * F :, :] = node[...].astype(BF)


def prep(points, sides, basis, transfer, skeleton, far):
    anywhere = pl.BlockSpec(memory_space=pl.ANY)
    return pl.pallas_call(
        prep_kernel,
        in_specs=[anywhere] * 4 + [VM] * 2,
        out_specs=[VM] * 3,
        out_shape=[
            jax.ShapeDtypeStruct((LD, 2 * F, LP), BF),
            jax.ShapeDtypeStruct((LD * 2 * F + RHS, SK), BF),
            jax.ShapeDtypeStruct((LD * F + 16, SK), BF),
        ],
        scratch_shapes=[
            pltpu.VMEM((LD, LP, SK), BF),
            pltpu.VMEM((LD, SK, SK), BF),
            pltpu.VMEM((RHS, SK), F32),
            pltpu.VMEM((16, SK), F32),
            pltpu.SemaphoreType.DMA((4, LD)),
        ],
        compiler_params=params(56),
        cost_estimate=cost(4),
        name="prep",
    )(points, sides, basis, transfer, skeleton, far)


def far_total(ids, columns, row, target, side, weight_of):
    points = target_side(target)
    weights, tiles = [], []
    for d, column in enumerate(columns):
        named = ids[row, column]
        at = jnp.maximum(named, 0)
        tiles.append(
            jnp.exp(
                jnp.dot(side[d * LD + at], points, preferred_element_type=F32)
            ).astype(BF)
        )
        weight = weight_of(d, at)
        weights.append(jnp.where(named >= 0, weight, jnp.zeros_like(weight)))
    if len(weights) == 1:
        return jnp.dot(weights[0], tiles[0], preferred_element_type=F32)
    return jnp.dot(
        jnp.concatenate(weights, axis=1),
        jnp.concatenate(tiles, axis=0),
        preferred_element_type=F32,
    )


def rows_of(leaf):
    return pl.ds(pl.multiple_of(leaf * F, F), F)


def charges_at(source, leaf):
    return source[pl.ds(pl.multiple_of(leaf * 2 * F, 2 * F), RHS), :]


def skeleton_at(source, leaf):
    return source[pl.ds(pl.multiple_of(leaf * 2 * F + F, F), F), :]


def columns_of(place):
    x, z = place[0], place[1]
    return [lax.rem(x + shift, SIDE) * SIDE + z for shift in (0, SIDE - 1, 1, 2)]


def near_sources(ids, columns, side, sources, target, out, base):
    @pl.loop(0, LD, unroll=UNROLL)
    def _(leaf):
        out[rows_of(leaf), :] = far_total(
            ids, columns, base * LD + leaf, target[rows_of(leaf), :], side,
            lambda d, at: charges_at(sources[d], at),
        ).astype(out.dtype)


def far_a_kernel(ids, place, s0, s1, s2, t0, t1, t2, o0, o1, o2, side):
    sources = (s0, s1, s2)
    for d, source in enumerate(sources):

        @pl.loop(0, LD, unroll=UNROLL)
        def _(leaf, d=d, source=source):
            side[d * LD + leaf] = source_side(skeleton_at(source, leaf))

    columns = columns_of(place)[:3]
    for b, (target, out) in enumerate(((t0, o0), (t1, o1), (t2, o2))):
        near_sources(ids, columns, side, sources, target, out, b)


def far_a(ids, place, sources, targets):
    return pl.pallas_call(
        far_a_kernel,
        in_specs=[SM, SM] + [VM] * 6,
        out_specs=[VM] * 4,
        out_shape=[jax.ShapeDtypeStruct((LD * F, SK), F32)] * 3
        + [jax.ShapeDtypeStruct((3 * LD, SK, AUG), BF)],
        compiler_params=params(16),
        cost_estimate=cost(9),
        name="far_a",
    )(ids, place, *sources, *targets)


def far_b_kernel(ids, place, given, s0, s1, s2, s3, t3, o3, last, side):
    sources = (s0, s1, s2, s3)

    @pl.loop(0, LD, unroll=UNROLL)
    def _(leaf):
        value = source_side(skeleton_at(s3, leaf))
        side[3 * LD + leaf] = value
        last[leaf] = value

    side[: 3 * LD] = given[...]
    near_sources(ids, columns_of(place), side, sources, t3, o3, 3)


def far_b(ids, place, side, sources, target):
    return pl.pallas_call(
        far_b_kernel,
        in_specs=[SM, SM] + [VM] * 6,
        out_specs=[VM] * 2,
        out_shape=[
            jax.ShapeDtypeStruct((LD * F, SK), BF),
            jax.ShapeDtypeStruct((LD, SK, AUG), BF),
        ],
        scratch_shapes=[pltpu.VMEM((SIDE * LD, SK, AUG), BF)],
        compiler_params=params(16),
        cost_estimate=cost(4),
        name="far_b",
    )(ids, place, side, *sources, target)


def far_c_kernel(ids, place, side, s3, t0, t1, t2, a0, a1, a2, own, r1, r2):
    columns = columns_of(place)[3:]
    for b, (target, given, out) in enumerate(((t0, a0, own), (t1, a1, r1), (t2, a2, r2))):

        @pl.loop(0, LD, unroll=UNROLL)
        def _(leaf, b=b, target=target, given=given, out=out):
            total = far_total(
                ids, columns, b * LD + leaf, target[rows_of(leaf), :], side,
                lambda d, at: charges_at(s3, at),
            )
            out[rows_of(leaf), :] = (given[rows_of(leaf), :] + total).astype(out.dtype)


def far_c(ids, place, side, source, targets, given):
    return pl.pallas_call(
        far_c_kernel,
        in_specs=[SM, SM] + [VM] * 8,
        out_specs=[VM] * 3,
        out_shape=[jax.ShapeDtypeStruct((LD * F, SK), F32)]
        + [jax.ShapeDtypeStruct((LD * F, SK), BF)] * 2,
        compiler_params=params(16),
        cost_estimate=cost(4),
        name="far_c",
    )(ids, place, side, source, *targets, *given)


def top_kernel(mine, pair, n1, n2, n3, a1, a2, a3, top, r1, r2, r3):
    points = target_side(mine[RHS:, :])
    total = jnp.zeros((RHS, SK), F32)
    rows = 2 * RHS
    others = [pair] + [n.at[i * rows : (i + 1) * rows] for n in (n1, n2, n3) for i in range(2)]
    for other in others:
        kernel = jnp.exp(
            jnp.dot(source_side(other[RHS:, :]), points, preferred_element_type=F32)
        ).astype(BF)
        total += jnp.dot(other[:RHS, :], kernel, preferred_element_type=F32)
    top[...] = total
    for given, out in ((a1, r1), (a2, r2), (a3, r3)):
        out[: LD * F, :] = given[...]
        out[LD * F :, :] = total.astype(BF)


def top_sum(mine, pair, others, parts):
    return pl.pallas_call(
        top_kernel,
        in_specs=[VM] * 8,
        out_specs=[VM] * 4,
        out_shape=[jax.ShapeDtypeStruct((RHS, SK), F32)]
        + [jax.ShapeDtypeStruct((LD * F + RHS, SK), BF)] * 3,
        compiler_params=params(16),
        cost_estimate=cost(2),
        name="top_sum",
    )(mine, pair, *others, *parts)


def near_groups(ids, leaf, place_of, points, side, rights, slots, out, given=None):
    count = jnp.int32(0)
    for d in range(ids.shape[1]):
        slots[d] = 0
    for d in range(ids.shape[1]):
        here, at = place_of(ids[leaf, d])
        slots[count] = jnp.where(here, at, 0)
        count += here.astype(jnp.int32)
    size = 4

    def group(start, used, total):
        tiles, weights = [], []
        for d in range(used):
            at = slots[start + d]
            tiles.append(
                jnp.exp(jnp.dot(side[at], points, preferred_element_type=F32)).astype(BF)
            )
            weights.append(rights(at))
        return total + jnp.dot(
            jnp.concatenate(weights, axis=1),
            jnp.concatenate(tiles, axis=0),
            preferred_element_type=F32,
        )

    full = lax.div(count, size)
    total = lax.fori_loop(
        0, full, lambda g, t: group(g * size, size, t), jnp.zeros((RHS, LP), F32)
    )
    out[...] = total if given is None else total + given[...]
    for used in range(1, size):

        @pl.when(count - full * size == used)
        def _(used=used):
            out[...] = group(full * size, used, out[...])


def near_own_kernel(ids, first, own, out, side, slots):
    @pl.loop(0, LD, unroll=4)
    def _(leaf):
        side[leaf] = source_side(own[leaf, :F, :])

    def place_of(named):
        at = named - first[0]
        return (named >= 0) & (at >= 0) & (at < LD), at

    @pl.loop(0, LD)
    def _(leaf):
        points = target_side(own[leaf, :F, :])
        near_groups(
            ids, leaf, place_of, points, side, lambda at: own[at, F:, :], slots, out.at[leaf]
        )


def near_own(ids, first, own):
    return pl.pallas_call(
        near_own_kernel,
        in_specs=[SM, SM, VM],
        out_specs=VM,
        out_shape=jax.ShapeDtypeStruct((LD, RHS, LP), F32),
        scratch_shapes=[pltpu.VMEM((LD, LP, AUG), BF), pltpu.SMEM((16,), jnp.int32)],
        compiler_params=params(16),
        cost_estimate=cost(9),
        name="near_own",
    )(ids, first, own)


def near_rest_kernel(ids, first, own, before, after, given, out, side, rights, slots):
    for d, block in enumerate((before, after)):

        @pl.loop(0, LD, unroll=4)
        def _(leaf, d=d, block=block):
            side[d * LD + leaf] = source_side(block[leaf, :F, :])
            rights[d * LD + leaf] = block[leaf, F:, :]

    def place_of(named):
        at = named - first[0]
        below = (at >= -LD) & (at < 0)
        above = (at >= LD) & (at < 2 * LD)
        return (named >= 0) & (below | above), jnp.where(below, at + LD, at)

    @pl.loop(0, LD)
    def _(leaf):
        points = target_side(own[leaf, :F, :])
        near_groups(
            ids, leaf, place_of, points, side, lambda at: rights[at], slots, out.at[leaf],
            given.at[leaf],
        )


def near_rest(ids, first, own, before, after, given):
    return pl.pallas_call(
        near_rest_kernel,
        in_specs=[SM, SM, VM, VM, VM, VM],
        out_specs=VM,
        out_shape=jax.ShapeDtypeStruct((LD, RHS, LP), F32),
        scratch_shapes=[
            pltpu.VMEM((2 * LD, LP, AUG), BF),
            pltpu.VMEM((2 * LD, RHS, LP), BF),
            pltpu.SMEM((16,), jnp.int32),
        ],
        compiler_params=params(24),
        cost_estimate=cost(11),
        name="near_rest",
    )(ids, first, own, before, after, given)


def final_kernel(near_sum, basis, transfer, own, r1, r2, r3, top, out):
    nt = (((1,), (1,)), ((), ()))
    last = LD * F
    total = top[...]
    for r in (r1, r2, r3):
        total += r[last:, :].astype(F32)
    total = total.astype(BF)

    @pl.loop(0, LD, unroll=2)
    def _(leaf):
        rows = pl.ds(pl.multiple_of(leaf * F, F), F)
        potential = own[rows, :]
        for r in (r1, r2, r3):
            potential += r[rows, :].astype(F32)
        potential += lax.dot_general(total, transfer[leaf], nt, preferred_element_type=F32)
        far_out = lax.dot_general(
            potential.astype(BF), basis[leaf], nt, preferred_element_type=F32
        )
        out[leaf] = (near_sum[leaf] + far_out).astype(BF)


def final(near_sum, basis, transfer, own, returned, top):
    return pl.pallas_call(
        final_kernel,
        in_specs=[VM] * 8,
        out_specs=VM,
        out_shape=jax.ShapeDtypeStruct((LD, RHS, LP), BF),
        compiler_params=params(16),
        cost_estimate=cost(3),
        name="final",
    )(near_sum, basis, transfer, own, *returned, top)


def shifted(value, dx, dz):
    pairs = []
    for x in range(SIDE):
        for z in range(SIDE):
            to = (x + dx) % SIDE * SIDE + (z + dz) % SIDE
            pairs.append((x * SIDE + z, to))
    return lax.ppermute(value, "top", pairs)


def leaf_shifted(value, dy):
    count = lax.axis_size("leaf")
    if dy == 0:
        return lax.ppermute(value, "leaf", [(i, i ^ 1) for i in range(count)])
    return lax.ppermute(value, "leaf", [(i, (i + 2 * dy) % count) for i in range(count)])


def on_device(
    points, right_sides, leaf_basis, transfer, node_points, neighbours, far_sources, skeleton
):
    node, at = lax.axis_index("leaf"), lax.axis_index("top")
    position = node * SIDE * SIDE + at
    near_msg, source_msg, target_msg = prep(
        points, right_sides, leaf_basis, transfer, skeleton, far_sources
    )
    sources = [source_msg] + [shifted(source_msg, dx, 0) for dx in (1, -1, 2)]
    targets = [target_msg] + [shifted(target_msg, 0, dz) for dz in (1, -1)]
    first = (position * LD).astype(jnp.int32).reshape(1)
    near_sum = near_own(neighbours, first, near_msg)

    targets, sources[:3], near_msg, near_sum = lax.optimization_barrier(
        (targets, sources[:3], near_msg, near_sum)
    )
    targets.append(shifted(targets[0], 0, 2))
    count = lax.axis_size("leaf") * lax.axis_size("top")
    up = [(i, i + 1) for i in range(count - 1)]
    before = lax.ppermute(near_msg, ("leaf", "top"), up)
    after = lax.ppermute(near_msg, ("leaf", "top"), [(j, i) for i, j in up])

    def ids_of(which):
        ids = jnp.concatenate([t[LD * F : LD * F + LD, : SIDE * SIDE] for t in which])
        return ids.astype(jnp.int32)

    place = jnp.stack([at // SIDE, at % SIDE]).astype(jnp.int32)
    *given, side = far_a(ids_of(targets[:3]), place, sources[:3], targets[:3])
    sources[3], given, side, targets[3] = lax.optimization_barrier(
        (sources[3], given, side, targets[3])
    )
    line_charge = sum(s[2 * LD * F :].astype(F32) for s in sources)
    mine = jnp.concatenate([line_charge.astype(BF), node_points[0]], axis=0)
    pair = leaf_shifted(mine, 0)
    ids = ids_of(targets)
    r3, last = far_b(ids, place, side, sources, targets[3])
    pair, r3, last = lax.optimization_barrier((pair, r3, last))
    both = jnp.concatenate([mine, pair], axis=0)
    others = [leaf_shifted(both, dy) for dy in (1, -1, 2)]
    own, r1, r2 = far_c(ids, place, last, sources[3], targets[:3], given)
    top, *parts = top_sum(mine, pair, others, (r1, r2, r3))
    returned = [shifted(r, 0, dz) for r, dz in zip(parts, (-1, 1, 2))]
    near_sum = near_rest(neighbours, first, near_msg, before, after, near_sum)
    return final(near_sum, leaf_basis, transfer, own, returned, top)


def solution(mesh):
    leaves = P(("leaf", "top"), None, None)
    lists = P(("leaf", "top"), None)
    in_specs = (leaves, leaves, leaves, leaves, P("leaf", None, None), lists, lists, lists)
    return jax.shard_map(
        on_device, mesh=mesh, in_specs=in_specs, out_specs=leaves, check_vma=False
    )
```

```python
import functools

import jax
import jax.numpy as jnp
from jax import lax
from jax.experimental import pallas as pl
from jax.experimental.pallas import tpu as pltpu
from jax.sharding import PartitionSpec as P

BF = jnp.bfloat16
F32 = jnp.float32
F = 64
RHS = 64
LP = 512
SK = 256
LD = 8
SIDE = 4
AUG = 128
UNROLL = 8
VM = pl.BlockSpec(memory_space=pltpu.VMEM)
SM = pl.BlockSpec(memory_space=pltpu.SMEM)


def params(mib=40):
    return pltpu.CompilerParams(vmem_limit_bytes=mib * 2**20)


def cost(us):
    return pl.CostEstimate(flops=int(us * 10**9), bytes_accessed=10**6, transcendentals=0)


def norm_rows(points, first):
    norm = jnp.sum(points * points, axis=0, keepdims=True) * (-2.0 / F)
    high = norm.astype(BF).astype(F32)
    mid = (norm - high).astype(BF).astype(F32)
    low = norm - high - mid
    row = lax.broadcasted_iota(jnp.int32, (16, points.shape[1]), 0)
    at = 0 if first else 3
    ones = jnp.where(row < 6, 1.0, 0.0).astype(F32)
    rows = jnp.where(row == at + 1, mid, jnp.where(row == at + 2, low, ones))
    return jnp.where(row == at, high, rows)


def source_side(points):
    points = points.astype(F32)
    zeros = jnp.zeros((AUG - F - 16, points.shape[1]), F32)
    full = jnp.concatenate([points, norm_rows(points, True), zeros], axis=0)
    return full.astype(BF).T


def target_side(points):
    points = points.astype(F32)
    zeros = jnp.zeros((AUG - F - 16, points.shape[1]), F32)
    full = jnp.concatenate([points * (4.0 / F), norm_rows(points, False), zeros], axis=0)
    return full.astype(BF)


def prep_kernel(
    points, sides, basis, transfer, skeleton, far, near_msg, source_msg, target_msg,
    own_basis, own_transfer, node, ids, sems,
):
    def fetch(leaf):
        pairs = (
            (points, near_msg.at[leaf, :F, :]),
            (sides, near_msg.at[leaf, F:, :]),
            (basis, own_basis.at[leaf]),
            (transfer, own_transfer.at[leaf]),
        )
        return [
            pltpu.make_async_copy(src.at[leaf], dst, sems.at[k, leaf])
            for k, (src, dst) in enumerate(pairs)
        ]

    for leaf in range(LD):
        for copy in fetch(leaf):
            copy.start()
    ids[...] = jnp.zeros_like(ids)
    named = far[...]
    ids[:LD, : SIDE * SIDE] = jnp.where(named >= 0, named & (LD - 1), -1).astype(F32)
    target_msg[LD * F :, :] = ids[...].astype(BF)
    position = lax.broadcasted_iota(jnp.int32, (LP, SK), 0)
    node[...] = jnp.zeros_like(node)
    for leaf in range(LD):
        for copy in fetch(leaf):
            copy.wait()
        charge = jnp.dot(
            near_msg[leaf, F:, :], own_basis[leaf], preferred_element_type=F32
        ).astype(BF)
        chosen = jnp.where(position == skeleton[leaf : leaf + 1, :], 1.0, 0.0).astype(BF)
        skel = jnp.dot(near_msg[leaf, :F, :], chosen, preferred_element_type=F32).astype(BF)
        source_msg[leaf * 2 * F : leaf * 2 * F + F, :] = charge
        source_msg[leaf * 2 * F + F : (leaf + 1) * 2 * F, :] = skel
        target_msg[leaf * F : (leaf + 1) * F, :] = skel
        node[...] += jnp.dot(charge, own_transfer[leaf], preferred_element_type=F32)
    source_msg[LD * 2 * F :, :] = node[...].astype(BF)


def prep(points, sides, basis, transfer, skeleton, far):
    anywhere = pl.BlockSpec(memory_space=pl.ANY)
    return pl.pallas_call(
        prep_kernel,
        in_specs=[anywhere] * 4 + [VM] * 2,
        out_specs=[VM] * 3,
        out_shape=[
            jax.ShapeDtypeStruct((LD, 2 * F, LP), BF),
            jax.ShapeDtypeStruct((LD * 2 * F + RHS, SK), BF),
            jax.ShapeDtypeStruct((LD * F + 16, SK), BF),
        ],
        scratch_shapes=[
            pltpu.VMEM((LD, LP, SK), BF),
            pltpu.VMEM((LD, SK, SK), BF),
            pltpu.VMEM((RHS, SK), F32),
            pltpu.VMEM((16, SK), F32),
            pltpu.SemaphoreType.DMA((4, LD)),
        ],
        compiler_params=params(56),
        cost_estimate=cost(4),
        name="prep",
    )(points, sides, basis, transfer, skeleton, far)


def far_total(ids, columns, row, target, side, weight_of):
    points = target_side(target)
    weights, tiles = [], []
    for d, column in enumerate(columns):
        named = ids[row, column]
        at = jnp.maximum(named, 0)
        tiles.append(
            jnp.exp(
                jnp.dot(side[d * LD + at], points, preferred_element_type=F32)
            ).astype(BF)
        )
        weight = weight_of(d, at)
        weights.append(jnp.where(named >= 0, weight, jnp.zeros_like(weight)))
    if len(weights) == 1:
        return jnp.dot(weights[0], tiles[0], preferred_element_type=F32)
    return jnp.dot(
        jnp.concatenate(weights, axis=1),
        jnp.concatenate(tiles, axis=0),
        preferred_element_type=F32,
    )


def rows_of(leaf):
    return pl.ds(pl.multiple_of(leaf * F, F), F)


def charges_at(source, leaf):
    return source[pl.ds(pl.multiple_of(leaf * 2 * F, 2 * F), RHS), :]


def skeleton_at(source, leaf):
    return source[pl.ds(pl.multiple_of(leaf * 2 * F + F, F), F), :]


def columns_of(place):
    x, z = place[0], place[1]
    return [lax.rem(x + shift, SIDE) * SIDE + z for shift in (0, SIDE - 1, 1, 2)]


def near_sources(ids, columns, side, sources, target, out, base):
    @pl.loop(0, LD, unroll=UNROLL)
    def _(leaf):
        out[rows_of(leaf), :] = far_total(
            ids, columns, base * LD + leaf, target[rows_of(leaf), :], side,
            lambda d, at: charges_at(sources[d], at),
        ).astype(out.dtype)


def sides_kernel(s0, s1, s2, side):
    for d, source in enumerate((s0, s1, s2)):

        @pl.loop(0, LD, unroll=UNROLL)
        def _(leaf, d=d, source=source):
            side[d * LD + leaf] = source_side(skeleton_at(source, leaf))


def sides_of(sources):
    return pl.pallas_call(
        sides_kernel,
        in_specs=[VM] * 3,
        out_specs=VM,
        out_shape=jax.ShapeDtypeStruct((3 * LD, SK, AUG), BF),
        compiler_params=params(16),
        cost_estimate=cost(0.01),
        name="sides",
    )(*sources)


def far_a_kernel(ids, place, side, s0, s1, s2, t0, t1, t2, o0, o1, o2):
    columns = columns_of(place)[:3]
    for b, (target, out) in enumerate(((t0, o0), (t1, o1), (t2, o2))):
        near_sources(ids, columns, side, (s0, s1, s2), target, out, b)


def far_a(ids, place, side, sources, targets):
    return pl.pallas_call(
        far_a_kernel,
        in_specs=[SM, SM] + [VM] * 7,
        out_specs=[VM] * 3,
        out_shape=[jax.ShapeDtypeStruct((LD * F, SK), F32)] * 3,
        compiler_params=params(16),
        cost_estimate=cost(0.01),
        name="far_a",
    )(ids, place, side, *sources, *targets)


def far_b_kernel(ids, place, given, s0, s1, s2, low, high, t3, o3, last, right, side):
    half = LD // 2
    for d, source in enumerate((low, high)):

        @pl.loop(0, half, unroll=half)
        def _(leaf, d=d, source=source):
            value = source_side(skeleton_at(source, leaf))
            side[3 * LD + d * half + leaf] = value
            last[d * half + leaf] = value
            right[d * half + leaf] = charges_at(source, leaf)

    side[: 3 * LD] = given[...]
    columns = columns_of(place)

    def weight_of(d, at):
        return right[at] if d == 3 else charges_at((s0, s1, s2)[d], at)

    @pl.loop(0, LD, unroll=UNROLL)
    def _(leaf):
        out = far_total(
            ids, columns, 3 * LD + leaf, t3[rows_of(leaf), :], side, weight_of
        )
        o3[rows_of(leaf), :] = out.astype(o3.dtype)


def far_b(ids, place, side, sources, halves, target):
    return pl.pallas_call(
        far_b_kernel,
        in_specs=[SM, SM] + [VM] * 7,
        out_specs=[VM] * 3,
        out_shape=[
            jax.ShapeDtypeStruct((LD * F, SK), BF),
            jax.ShapeDtypeStruct((LD, SK, AUG), BF),
            jax.ShapeDtypeStruct((LD, RHS, SK), BF),
        ],
        scratch_shapes=[pltpu.VMEM((SIDE * LD, SK, AUG), BF)],
        compiler_params=params(16),
        cost_estimate=cost(4),
        name="far_b",
    )(ids, place, side, *sources, *halves, target)


def far_c_kernel(ids, place, side, right, t0, t1, t2, a0, a1, a2, own, r1, r2):
    columns = columns_of(place)[3:]
    for b, (target, given, out) in enumerate(((t0, a0, own), (t1, a1, r1), (t2, a2, r2))):

        @pl.loop(0, LD, unroll=UNROLL)
        def _(leaf, b=b, target=target, given=given, out=out):
            total = far_total(
                ids, columns, b * LD + leaf, target[rows_of(leaf), :], side,
                lambda d, at: right[at],
            )
            out[rows_of(leaf), :] = (given[rows_of(leaf), :] + total).astype(out.dtype)


def far_c(ids, place, side, right, targets, given):
    return pl.pallas_call(
        far_c_kernel,
        in_specs=[SM, SM] + [VM] * 8,
        out_specs=[VM] * 3,
        out_shape=[jax.ShapeDtypeStruct((LD * F, SK), F32)]
        + [jax.ShapeDtypeStruct((LD * F, SK), BF)] * 2,
        compiler_params=params(16),
        cost_estimate=cost(4),
        name="far_c",
    )(ids, place, side, right, *targets, *given)


def top_kernel(mine, pair, n1, n2, n3, a1, a2, a3, top, r1, r2, r3):
    points = target_side(mine[RHS:, :])
    total = jnp.zeros((RHS, SK), F32)
    rows = 2 * RHS
    others = [pair] + [n.at[i * rows : (i + 1) * rows] for n in (n1, n2, n3) for i in range(2)]
    for other in others:
        kernel = jnp.exp(
            jnp.dot(source_side(other[RHS:, :]), points, preferred_element_type=F32)
        ).astype(BF)
        total += jnp.dot(other[:RHS, :], kernel, preferred_element_type=F32)
    top[...] = total
    for given, out in ((a1, r1), (a2, r2), (a3, r3)):
        out[: LD * F, :] = given[...]
        out[LD * F :, :] = total.astype(BF)


def top_sum(mine, pair, others, parts):
    return pl.pallas_call(
        top_kernel,
        in_specs=[VM] * 8,
        out_specs=[VM] * 4,
        out_shape=[jax.ShapeDtypeStruct((RHS, SK), F32)]
        + [jax.ShapeDtypeStruct((LD * F + RHS, SK), BF)] * 3,
        compiler_params=params(16),
        cost_estimate=cost(2),
        name="top_sum",
    )(mine, pair, *others, *parts)


def near_groups(ids, leaf, place_of, points, side, rights, slots, out, given=None):
    count = jnp.int32(0)
    for d in range(ids.shape[1]):
        slots[d] = 0
    for d in range(ids.shape[1]):
        here, at = place_of(ids[leaf, d])
        slots[count] = jnp.where(here, at, 0)
        count += here.astype(jnp.int32)
    size = 4

    def group(start, used, total):
        tiles, weights = [], []
        for d in range(used):
            at = slots[start + d]
            tiles.append(
                jnp.exp(jnp.dot(side[at], points, preferred_element_type=F32)).astype(BF)
            )
            weights.append(rights(at))
        return total + jnp.dot(
            jnp.concatenate(weights, axis=1),
            jnp.concatenate(tiles, axis=0),
            preferred_element_type=F32,
        )

    full = lax.div(count, size)
    total = lax.fori_loop(
        0, full, lambda g, t: group(g * size, size, t), jnp.zeros((RHS, LP), F32)
    )
    out[...] = total if given is None else total + given[...]
    for used in range(1, size):

        @pl.when(count - full * size == used)
        def _(used=used):
            out[...] = group(full * size, used, out[...])


def near_own_kernel(ids, first, own, out, side, slots):
    @pl.loop(0, LD, unroll=4)
    def _(leaf):
        side[leaf] = source_side(own[leaf, :F, :])

    def place_of(named):
        at = named - first[0]
        return (named >= 0) & (at >= 0) & (at < LD), at

    @pl.loop(0, LD)
    def _(leaf):
        points = target_side(own[leaf, :F, :])
        near_groups(
            ids, leaf, place_of, points, side, lambda at: own[at, F:, :], slots, out.at[leaf]
        )


def near_own(ids, first, own):
    return pl.pallas_call(
        near_own_kernel,
        in_specs=[SM, SM, VM],
        out_specs=VM,
        out_shape=jax.ShapeDtypeStruct((LD, RHS, LP), F32),
        scratch_shapes=[pltpu.VMEM((LD, LP, AUG), BF), pltpu.SMEM((16,), jnp.int32)],
        compiler_params=params(16),
        cost_estimate=cost(9),
        name="near_own",
    )(ids, first, own)


def near_rest_kernel(ids, first, own, before, after, given, out, side, rights, slots):
    for d, block in enumerate((before, after)):

        @pl.loop(0, LD, unroll=4)
        def _(leaf, d=d, block=block):
            side[d * LD + leaf] = source_side(block[leaf, :F, :])
            rights[d * LD + leaf] = block[leaf, F:, :]

    def place_of(named):
        at = named - first[0]
        below = (at >= -LD) & (at < 0)
        above = (at >= LD) & (at < 2 * LD)
        return (named >= 0) & (below | above), jnp.where(below, at + LD, at)

    @pl.loop(0, LD)
    def _(leaf):
        points = target_side(own[leaf, :F, :])
        near_groups(
            ids, leaf, place_of, points, side, lambda at: rights[at], slots, out.at[leaf],
            given.at[leaf],
        )


def near_rest(ids, first, own, before, after, given):
    return pl.pallas_call(
        near_rest_kernel,
        in_specs=[SM, SM, VM, VM, VM, VM],
        out_specs=VM,
        out_shape=jax.ShapeDtypeStruct((LD, RHS, LP), F32),
        scratch_shapes=[
            pltpu.VMEM((2 * LD, LP, AUG), BF),
            pltpu.VMEM((2 * LD, RHS, LP), BF),
            pltpu.SMEM((16,), jnp.int32),
        ],
        compiler_params=params(24),
        cost_estimate=cost(11),
        name="near_rest",
    )(ids, first, own, before, after, given)


def final_kernel(near_sum, basis, transfer, own, r1, r2, r3, top, out):
    nt = (((1,), (1,)), ((), ()))
    last = LD * F
    total = top[...]
    for r in (r1, r2, r3):
        total += r[last:, :].astype(F32)
    total = total.astype(BF)

    @pl.loop(0, LD, unroll=2)
    def _(leaf):
        rows = pl.ds(pl.multiple_of(leaf * F, F), F)
        potential = own[rows, :]
        for r in (r1, r2, r3):
            potential += r[rows, :].astype(F32)
        potential += lax.dot_general(total, transfer[leaf], nt, preferred_element_type=F32)
        far_out = lax.dot_general(
            potential.astype(BF), basis[leaf], nt, preferred_element_type=F32
        )
        out[leaf] = (near_sum[leaf] + far_out).astype(BF)


def final(near_sum, basis, transfer, own, returned, top):
    return pl.pallas_call(
        final_kernel,
        in_specs=[VM] * 8,
        out_specs=VM,
        out_shape=jax.ShapeDtypeStruct((LD, RHS, LP), BF),
        compiler_params=params(16),
        cost_estimate=cost(3),
        name="final",
    )(near_sum, basis, transfer, own, *returned, top)


def shifted(value, dx, dz):
    pairs = []
    for x in range(SIDE):
        for z in range(SIDE):
            to = (x + dx) % SIDE * SIDE + (z + dz) % SIDE
            pairs.append((x * SIDE + z, to))
    return lax.ppermute(value, "top", pairs)


def leaf_shifted(value, dy):
    count = lax.axis_size("leaf")
    if dy == 0:
        return lax.ppermute(value, "leaf", [(i, i ^ 1) for i in range(count)])
    return lax.ppermute(value, "leaf", [(i, (i + 2 * dy) % count) for i in range(count)])


def on_device(
    points, right_sides, leaf_basis, transfer, node_points, neighbours, far_sources, skeleton
):
    node, at = lax.axis_index("leaf"), lax.axis_index("top")
    position = node * SIDE * SIDE + at
    near_msg, source_msg, target_msg = prep(
        points, right_sides, leaf_basis, transfer, skeleton, far_sources
    )
    sources = [source_msg] + [shifted(source_msg, dx, 0) for dx in (1, -1)]
    targets = [target_msg] + [shifted(target_msg, 0, dz) for dz in (1, -1, 2)]
    first = (position * LD).astype(jnp.int32).reshape(1)
    near_sum = near_own(neighbours, first, near_msg)

    targets[:3], sources, near_msg, near_sum = lax.optimization_barrier(
        (targets[:3], sources, near_msg, near_sum)
    )
    half = LD * F
    low, high = shifted(sources[1][:half], 1, 0), shifted(sources[2][half:], -1, 0)
    side = sides_of(sources)
    near_msg, side = lax.optimization_barrier((near_msg, side))
    count = lax.axis_size("leaf") * lax.axis_size("top")
    up = [(i, i + 1) for i in range(count - 1)]
    before = lax.ppermute(near_msg, ("leaf", "top"), up)
    after = lax.ppermute(near_msg, ("leaf", "top"), [(j, i) for i, j in up])

    def ids_of(which):
        ids = jnp.concatenate([t[LD * F : LD * F + LD, : SIDE * SIDE] for t in which])
        return ids.astype(jnp.int32)

    place = jnp.stack([at // SIDE, at % SIDE]).astype(jnp.int32)
    given = far_a(ids_of(targets[:3]), place, side, sources, targets[:3])
    low, high, given, targets[3] = lax.optimization_barrier((low, high, given, targets[3]))
    line_charge = sum(s[2 * half :].astype(F32) for s in sources) + high[half:].astype(F32)
    mine = jnp.concatenate([line_charge.astype(BF), node_points[0]], axis=0)
    pair = leaf_shifted(mine, 0)
    ids = ids_of(targets)
    r3, last, right = far_b(ids, place, side, sources, (low, high), targets[3])
    pair, r3, last = lax.optimization_barrier((pair, r3, last))
    both = jnp.concatenate([mine, pair], axis=0)
    others = [leaf_shifted(both, dy) for dy in (1, -1, 2)]
    own, r1, r2 = far_c(ids, place, last, right, targets[:3], given)
    top, *parts = top_sum(mine, pair, others, (r1, r2, r3))
    returned = [shifted(r, 0, dz) for r, dz in zip(parts, (-1, 1, 2))]
    near_sum = near_rest(neighbours, first, near_msg, before, after, near_sum)
    return final(near_sum, leaf_basis, transfer, own, returned, top)


def solution(mesh):
    leaves = P(("leaf", "top"), None, None)
    lists = P(("leaf", "top"), None)
    in_specs = (leaves, leaves, leaves, leaves, P("leaf", None, None), lists, lists, lists)
    return jax.shard_map(
        on_device, mesh=mesh, in_specs=in_specs, out_specs=leaves, check_vma=False
    )
```

```python
import functools

import jax
import jax.numpy as jnp
from jax import lax
from jax.experimental import pallas as pl
from jax.experimental.pallas import tpu as pltpu
from jax.sharding import PartitionSpec as P

BF = jnp.bfloat16
F32 = jnp.float32
F = 64
RHS = 64
LP = 512
SK = 256
LD = 8
SIDE = 4
AUG = 128
UNROLL = 8
BATCH = 2
VM = pl.BlockSpec(memory_space=pltpu.VMEM)
SM = pl.BlockSpec(memory_space=pltpu.SMEM)


def params(mib=40):
    return pltpu.CompilerParams(vmem_limit_bytes=mib * 2**20)


def cost(us):
    return pl.CostEstimate(flops=int(us * 10**9), bytes_accessed=10**6, transcendentals=0)


def norm_rows(points, first):
    norm = jnp.sum(points * points, axis=0, keepdims=True) * (-2.0 / F)
    high = norm.astype(BF).astype(F32)
    mid = (norm - high).astype(BF).astype(F32)
    low = norm - high - mid
    row = lax.broadcasted_iota(jnp.int32, (16, points.shape[1]), 0)
    at = 0 if first else 3
    ones = jnp.where(row < 6, 1.0, 0.0).astype(F32)
    rows = jnp.where(row == at + 1, mid, jnp.where(row == at + 2, low, ones))
    return jnp.where(row == at, high, rows)


def source_side(points):
    points = points.astype(F32)
    zeros = jnp.zeros((AUG - F - 16, points.shape[1]), F32)
    full = jnp.concatenate([points, norm_rows(points, True), zeros], axis=0)
    return full.astype(BF).T


def target_side(points):
    points = points.astype(F32)
    zeros = jnp.zeros((AUG - F - 16, points.shape[1]), F32)
    full = jnp.concatenate([points * (4.0 / F), norm_rows(points, False), zeros], axis=0)
    return full.astype(BF)


def prep_kernel(
    points, sides, basis, transfer, skeleton, far, near_msg, source_msg, target_msg,
    own_basis, own_transfer, node, ids, sems,
):
    def fetch(leaf):
        pairs = (
            (points, near_msg.at[leaf, :F, :]),
            (sides, near_msg.at[leaf, F:, :]),
            (basis, own_basis.at[leaf]),
            (transfer, own_transfer.at[leaf]),
        )
        return [
            pltpu.make_async_copy(src.at[leaf], dst, sems.at[k, leaf])
            for k, (src, dst) in enumerate(pairs)
        ]

    for leaf in range(LD):
        for copy in fetch(leaf):
            copy.start()
    ids[...] = jnp.zeros_like(ids)
    named = far[...]
    ids[:LD, : SIDE * SIDE] = jnp.where(named >= 0, named & (LD - 1), -1).astype(F32)
    target_msg[LD * F :, :] = ids[...].astype(BF)
    position = lax.broadcasted_iota(jnp.int32, (LP, SK), 0)
    node[...] = jnp.zeros_like(node)
    for leaf in range(LD):
        for copy in fetch(leaf):
            copy.wait()
        charge = jnp.dot(
            near_msg[leaf, F:, :], own_basis[leaf], preferred_element_type=F32
        ).astype(BF)
        chosen = jnp.where(position == skeleton[leaf : leaf + 1, :], 1.0, 0.0).astype(BF)
        skel = jnp.dot(near_msg[leaf, :F, :], chosen, preferred_element_type=F32).astype(BF)
        source_msg[leaf * 2 * F : leaf * 2 * F + F, :] = charge
        source_msg[leaf * 2 * F + F : (leaf + 1) * 2 * F, :] = skel
        target_msg[leaf * F : (leaf + 1) * F, :] = skel
        node[...] += jnp.dot(charge, own_transfer[leaf], preferred_element_type=F32)
    source_msg[LD * 2 * F :, :] = node[...].astype(BF)


def prep(points, sides, basis, transfer, skeleton, far):
    anywhere = pl.BlockSpec(memory_space=pl.ANY)
    return pl.pallas_call(
        prep_kernel,
        in_specs=[anywhere] * 4 + [VM] * 2,
        out_specs=[VM] * 3,
        out_shape=[
            jax.ShapeDtypeStruct((LD, 2 * F, LP), BF),
            jax.ShapeDtypeStruct((LD * 2 * F + RHS, SK), BF),
            jax.ShapeDtypeStruct((LD * F + 16, SK), BF),
        ],
        scratch_shapes=[
            pltpu.VMEM((LD, LP, SK), BF),
            pltpu.VMEM((LD, SK, SK), BF),
            pltpu.VMEM((RHS, SK), F32),
            pltpu.VMEM((16, SK), F32),
            pltpu.SemaphoreType.DMA((4, LD)),
        ],
        compiler_params=params(56),
        cost_estimate=cost(4),
        name="prep",
    )(points, sides, basis, transfer, skeleton, far)


def far_run(ids, columns, jobs, side_of, weight_of, tile):
    depth = len(columns)

    def first(slot, job):
        row, target, _ = job
        points = target_side(target())
        for d, column in enumerate(columns):
            at = jnp.maximum(ids[row, column], 0)
            tile[slot, d * SK : (d + 1) * SK, :] = jnp.exp(
                jnp.dot(side_of(d, at), points, preferred_element_type=F32)
            ).astype(BF)

    def second(slot, job):
        row, _, store = job
        weights = []
        for d, column in enumerate(columns):
            named = ids[row, column]
            weight = weight_of(d, jnp.maximum(named, 0))
            weights.append(jnp.where(named >= 0, weight, jnp.zeros_like(weight)))
        weight = weights[0] if depth == 1 else jnp.concatenate(weights, axis=1)
        store(jnp.dot(weight, tile[slot, : depth * SK, :], preferred_element_type=F32))

    slots = 2 * BATCH
    groups = [jobs[i : i + BATCH] for i in range(0, len(jobs), BATCH)]
    for g in range(len(groups) + 1):
        if g < len(groups):
            for k, job in enumerate(groups[g]):
                first((g * BATCH + k) % slots, job)
        if g > 0:
            for k, job in enumerate(groups[g - 1]):
                second(((g - 1) * BATCH + k) % slots, job)


def target_jobs(base, target, out, given=None):
    def job(leaf):
        rows = slice(leaf * F, leaf * F + F)

        def store(total):
            if given is not None:
                total = total + given[rows, :]
            out[rows, :] = total.astype(out.dtype)

        return base * LD + leaf, lambda: target[rows, :], store

    return [job(leaf) for leaf in range(LD)]


def rows_of(leaf):
    return pl.ds(pl.multiple_of(leaf * F, F), F)


def charges_at(source, leaf):
    return source[pl.ds(pl.multiple_of(leaf * 2 * F, 2 * F), RHS), :]


def skeleton_at(source, leaf):
    return source[pl.ds(pl.multiple_of(leaf * 2 * F + F, F), F), :]


def columns_of(place):
    x, z = place[0], place[1]
    return [lax.rem(x + shift, SIDE) * SIDE + z for shift in (0, SIDE - 1, 1, 2)]


def sides_kernel(s0, s1, s2, side):
    for d, source in enumerate((s0, s1, s2)):

        @pl.loop(0, LD, unroll=UNROLL)
        def _(leaf, d=d, source=source):
            side[d * LD + leaf] = source_side(skeleton_at(source, leaf))


def sides_of(sources):
    return pl.pallas_call(
        sides_kernel,
        in_specs=[VM] * 3,
        out_specs=VM,
        out_shape=jax.ShapeDtypeStruct((3 * LD, SK, AUG), BF),
        compiler_params=params(16),
        cost_estimate=cost(0.01),
        name="sides",
    )(*sources)


def far_a_kernel(ids, place, side, s0, s1, s2, t0, t1, t2, o0, o1, o2, tile):
    jobs = []
    for b, (target, out) in enumerate(((t0, o0), (t1, o1), (t2, o2))):
        jobs += target_jobs(b, target, out)
    far_run(
        ids, columns_of(place)[:3], jobs, lambda d, at: side[d * LD + at],
        lambda d, at: charges_at((s0, s1, s2)[d], at), tile,
    )


def far_a(ids, place, side, sources, targets):
    return pl.pallas_call(
        far_a_kernel,
        in_specs=[SM, SM] + [VM] * 7,
        out_specs=[VM] * 3,
        out_shape=[jax.ShapeDtypeStruct((LD * F, SK), F32)] * 3,
        scratch_shapes=[pltpu.VMEM((2 * BATCH, 3 * SK, SK), BF)],
        compiler_params=params(16),
        cost_estimate=cost(0.01),
        name="far_a",
    )(ids, place, side, *sources, *targets)


def far_b_kernel(ids, place, side, s0, s1, s2, s3, t3, o3, last, tile):
    @pl.loop(0, LD, unroll=UNROLL)
    def _(leaf):
        last[leaf] = source_side(skeleton_at(s3, leaf))

    far_run(
        ids, columns_of(place), target_jobs(3, t3, o3),
        lambda d, at: last[at] if d == 3 else side[d * LD + at],
        lambda d, at: charges_at((s0, s1, s2, s3)[d], at), tile,
    )


def far_b(ids, place, side, sources, target):
    return pl.pallas_call(
        far_b_kernel,
        in_specs=[SM, SM] + [VM] * 6,
        out_specs=[VM] * 2,
        out_shape=[
            jax.ShapeDtypeStruct((LD * F, SK), BF),
            jax.ShapeDtypeStruct((LD, SK, AUG), BF),
        ],
        scratch_shapes=[pltpu.VMEM((2 * BATCH, SIDE * SK, SK), BF)],
        compiler_params=params(16),
        cost_estimate=cost(3),
        name="far_b",
    )(ids, place, side, *sources, target)


def far_c_kernel(ids, place, side, s3, t0, t1, t2, a0, a1, a2, own, r1, r2, tile):
    jobs = []
    for b, (target, given, out) in enumerate(((t0, a0, own), (t1, a1, r1), (t2, a2, r2))):
        jobs += target_jobs(b, target, out, given)
    far_run(
        ids, columns_of(place)[3:], jobs, lambda d, at: side[at],
        lambda d, at: charges_at(s3, at), tile,
    )


def far_c(ids, place, side, source, targets, given):
    return pl.pallas_call(
        far_c_kernel,
        in_specs=[SM, SM] + [VM] * 8,
        out_specs=[VM] * 3,
        out_shape=[jax.ShapeDtypeStruct((LD * F, SK), F32)]
        + [jax.ShapeDtypeStruct((LD * F, SK), BF)] * 2,
        scratch_shapes=[pltpu.VMEM((2 * BATCH, SK, SK), BF)],
        compiler_params=params(16),
        cost_estimate=cost(4),
        name="far_c",
    )(ids, place, side, source, *targets, *given)


def top_kernel(mine, pair, n1, n2, n3, a1, a2, a3, top, r1, r2, r3):
    points = target_side(mine[RHS:, :])
    total = jnp.zeros((RHS, SK), F32)
    rows = 2 * RHS
    others = [pair] + [n.at[i * rows : (i + 1) * rows] for n in (n1, n2, n3) for i in range(2)]
    for other in others:
        kernel = jnp.exp(
            jnp.dot(source_side(other[RHS:, :]), points, preferred_element_type=F32)
        ).astype(BF)
        total += jnp.dot(other[:RHS, :], kernel, preferred_element_type=F32)
    top[...] = total
    for given, out in ((a1, r1), (a2, r2), (a3, r3)):
        out[: LD * F, :] = given[...]
        out[LD * F :, :] = total.astype(BF)


def top_sum(mine, pair, others, parts):
    return pl.pallas_call(
        top_kernel,
        in_specs=[VM] * 8,
        out_specs=[VM] * 4,
        out_shape=[jax.ShapeDtypeStruct((RHS, SK), F32)]
        + [jax.ShapeDtypeStruct((LD * F + RHS, SK), BF)] * 3,
        compiler_params=params(16),
        cost_estimate=cost(2),
        name="top_sum",
    )(mine, pair, *others, *parts)


def near_groups(ids, leaf, place_of, points, side, rights, slots, out, given=None):
    count = jnp.int32(0)
    for d in range(ids.shape[1]):
        slots[d] = 0
    for d in range(ids.shape[1]):
        here, at = place_of(ids[leaf, d])
        slots[count] = jnp.where(here, at, 0)
        count += here.astype(jnp.int32)
    size = 4

    def group(start, used, total):
        tiles, weights = [], []
        for d in range(used):
            at = slots[start + d]
            tiles.append(
                jnp.exp(jnp.dot(side[at], points, preferred_element_type=F32)).astype(BF)
            )
            weights.append(rights(at))
        return total + jnp.dot(
            jnp.concatenate(weights, axis=1),
            jnp.concatenate(tiles, axis=0),
            preferred_element_type=F32,
        )

    full = lax.div(count, size)
    total = lax.fori_loop(
        0, full, lambda g, t: group(g * size, size, t), jnp.zeros((RHS, LP), F32)
    )
    out[...] = total if given is None else total + given[...]
    for used in range(1, size):

        @pl.when(count - full * size == used)
        def _(used=used):
            out[...] = group(full * size, used, out[...])


def near_own_kernel(ids, first, own, out, side, slots):
    @pl.loop(0, LD, unroll=4)
    def _(leaf):
        side[leaf] = source_side(own[leaf, :F, :])

    def place_of(named):
        at = named - first[0]
        return (named >= 0) & (at >= 0) & (at < LD), at

    @pl.loop(0, LD)
    def _(leaf):
        points = target_side(own[leaf, :F, :])
        near_groups(
            ids, leaf, place_of, points, side, lambda at: own[at, F:, :], slots, out.at[leaf]
        )


def near_own(ids, first, own):
    return pl.pallas_call(
        near_own_kernel,
        in_specs=[SM, SM, VM],
        out_specs=VM,
        out_shape=jax.ShapeDtypeStruct((LD, RHS, LP), F32),
        scratch_shapes=[pltpu.VMEM((LD, LP, AUG), BF), pltpu.SMEM((16,), jnp.int32)],
        compiler_params=params(16),
        cost_estimate=cost(9),
        name="near_own",
    )(ids, first, own)


def near_rest_kernel(ids, first, own, before, after, given, out, side, rights, slots):
    for d, block in enumerate((before, after)):

        @pl.loop(0, LD, unroll=4)
        def _(leaf, d=d, block=block):
            side[d * LD + leaf] = source_side(block[leaf, :F, :])
            rights[d * LD + leaf] = block[leaf, F:, :]

    def place_of(named):
        at = named - first[0]
        below = (at >= -LD) & (at < 0)
        above = (at >= LD) & (at < 2 * LD)
        return (named >= 0) & (below | above), jnp.where(below, at + LD, at)

    @pl.loop(0, LD)
    def _(leaf):
        points = target_side(own[leaf, :F, :])
        near_groups(
            ids, leaf, place_of, points, side, lambda at: rights[at], slots, out.at[leaf],
            given.at[leaf],
        )


def near_rest(ids, first, own, before, after, given):
    return pl.pallas_call(
        near_rest_kernel,
        in_specs=[SM, SM, VM, VM, VM, VM],
        out_specs=VM,
        out_shape=jax.ShapeDtypeStruct((LD, RHS, LP), F32),
        scratch_shapes=[
            pltpu.VMEM((2 * LD, LP, AUG), BF),
            pltpu.VMEM((2 * LD, RHS, LP), BF),
            pltpu.SMEM((16,), jnp.int32),
        ],
        compiler_params=params(24),
        cost_estimate=cost(11),
        name="near_rest",
    )(ids, first, own, before, after, given)


def final_kernel(near_sum, basis, transfer, own, r1, r2, r3, top, out):
    nt = (((1,), (1,)), ((), ()))
    last = LD * F
    total = top[...]
    for r in (r1, r2, r3):
        total += r[last:, :].astype(F32)
    total = total.astype(BF)

    @pl.loop(0, LD, unroll=UNROLL)
    def _(leaf):
        rows = pl.ds(pl.multiple_of(leaf * F, F), F)
        potential = own[rows, :]
        for r in (r1, r2, r3):
            potential += r[rows, :].astype(F32)
        potential += lax.dot_general(total, transfer[leaf], nt, preferred_element_type=F32)
        far_out = lax.dot_general(
            potential.astype(BF), basis[leaf], nt, preferred_element_type=F32
        )
        out[leaf] = (near_sum[leaf] + far_out).astype(BF)


def final(near_sum, basis, transfer, own, returned, top):
    return pl.pallas_call(
        final_kernel,
        in_specs=[VM] * 8,
        out_specs=VM,
        out_shape=jax.ShapeDtypeStruct((LD, RHS, LP), BF),
        compiler_params=params(16),
        cost_estimate=cost(3),
        name="final",
    )(near_sum, basis, transfer, own, *returned, top)


def shifted(value, dx, dz):
    pairs = []
    for x in range(SIDE):
        for z in range(SIDE):
            to = (x + dx) % SIDE * SIDE + (z + dz) % SIDE
            pairs.append((x * SIDE + z, to))
    return lax.ppermute(value, "top", pairs)


def leaf_shifted(value, dy):
    count = lax.axis_size("leaf")
    if dy == 0:
        return lax.ppermute(value, "leaf", [(i, i ^ 1) for i in range(count)])
    return lax.ppermute(value, "leaf", [(i, (i + 2 * dy) % count) for i in range(count)])


def on_device(
    points, right_sides, leaf_basis, transfer, node_points, neighbours, far_sources, skeleton
):
    node, at = lax.axis_index("leaf"), lax.axis_index("top")
    position = node * SIDE * SIDE + at
    near_msg, source_msg, target_msg = prep(
        points, right_sides, leaf_basis, transfer, skeleton, far_sources
    )
    sources = [source_msg] + [shifted(source_msg, dx, 0) for dx in (1, -1)]
    targets = [target_msg] + [shifted(target_msg, 0, dz) for dz in (1, -1, 2)]
    first = (position * LD).astype(jnp.int32).reshape(1)
    near_sum = near_own(neighbours, first, near_msg)

    targets[:3], sources, near_msg, near_sum = lax.optimization_barrier(
        (targets[:3], sources, near_msg, near_sum)
    )
    opposite = shifted(sources[1], 1, 0)
    side = sides_of(sources)
    near_msg, side = lax.optimization_barrier((near_msg, side))
    count = lax.axis_size("leaf") * lax.axis_size("top")
    up = [(i, i + 1) for i in range(count - 1)]
    before = lax.ppermute(near_msg, ("leaf", "top"), up)
    after = lax.ppermute(near_msg, ("leaf", "top"), [(j, i) for i, j in up])

    def ids_of(which):
        ids = jnp.concatenate([t[LD * F : LD * F + LD, : SIDE * SIDE] for t in which])
        return ids.astype(jnp.int32)

    place = jnp.stack([at // SIDE, at % SIDE]).astype(jnp.int32)
    given = far_a(ids_of(targets[:3]), place, side, sources, targets[:3])
    opposite, given, targets[3] = lax.optimization_barrier((opposite, given, targets[3]))
    sources.append(opposite)
    line_charge = sum(s[2 * LD * F :].astype(F32) for s in sources)
    mine = jnp.concatenate([line_charge.astype(BF), node_points[0]], axis=0)
    pair = leaf_shifted(mine, 0)
    ids = ids_of(targets)
    r3, last = far_b(ids, place, side, sources, targets[3])
    pair, r3, last = lax.optimization_barrier((pair, r3, last))
    both = jnp.concatenate([mine, pair], axis=0)
    others = [leaf_shifted(both, dy) for dy in (1, -1, 2)]
    own, r1, r2 = far_c(ids, place, last, opposite, targets[:3], given)
    top, *parts = top_sum(mine, pair, others, (r1, r2, r3))
    returned = [shifted(r, 0, dz) for r, dz in zip(parts, (-1, 1, 2))]
    near_sum = near_rest(neighbours, first, near_msg, before, after, near_sum)
    return final(near_sum, leaf_basis, transfer, own, returned, top)


def solution(mesh):
    leaves = P(("leaf", "top"), None, None)
    lists = P(("leaf", "top"), None)
    in_specs = (leaves, leaves, leaves, leaves, P("leaf", None, None), lists, lists, lists)
    return jax.shard_map(
        on_device, mesh=mesh, in_specs=in_specs, out_specs=leaves, check_vma=False
    )
```

```python
import functools

import jax
import jax.numpy as jnp
from jax import lax
from jax.experimental import pallas as pl
from jax.experimental.pallas import tpu as pltpu
from jax.sharding import PartitionSpec as P

BF = jnp.bfloat16
F32 = jnp.float32
F = 64
RHS = 64
LP = 512
SK = 256
LD = 8
SIDE = 4
AUG = 128
UNROLL = 8
BATCH = 2
VM = pl.BlockSpec(memory_space=pltpu.VMEM)
SM = pl.BlockSpec(memory_space=pltpu.SMEM)


def params(mib=40):
    return pltpu.CompilerParams(vmem_limit_bytes=mib * 2**20)


def cost(us):
    return pl.CostEstimate(flops=int(us * 10**9), bytes_accessed=10**6, transcendentals=0)


def norm_rows(points, first):
    norm = jnp.sum(points * points, axis=0, keepdims=True) * (-2.0 / F)
    high = norm.astype(BF).astype(F32)
    mid = (norm - high).astype(BF).astype(F32)
    low = norm - high - mid
    row = lax.broadcasted_iota(jnp.int32, (16, points.shape[1]), 0)
    at = 0 if first else 3
    ones = jnp.where(row < 6, 1.0, 0.0).astype(F32)
    rows = jnp.where(row == at + 1, mid, jnp.where(row == at + 2, low, ones))
    return jnp.where(row == at, high, rows)


def source_side(points):
    points = points.astype(F32)
    zeros = jnp.zeros((AUG - F - 16, points.shape[1]), F32)
    full = jnp.concatenate([points, norm_rows(points, True), zeros], axis=0)
    return full.astype(BF).T


def target_side(points):
    points = points.astype(F32)
    zeros = jnp.zeros((AUG - F - 16, points.shape[1]), F32)
    full = jnp.concatenate([points * (4.0 / F), norm_rows(points, False), zeros], axis=0)
    return full.astype(BF)


def prep_kernel(
    points, sides, basis, transfer, skeleton, far, near_msg, source_msg, target_msg,
    own_basis, own_transfer, node, ids, sems,
):
    def fetch(leaf):
        pairs = (
            (points, near_msg.at[leaf, :F, :]),
            (sides, near_msg.at[leaf, F:, :]),
            (basis, own_basis.at[leaf]),
            (transfer, own_transfer.at[leaf]),
        )
        return [
            pltpu.make_async_copy(src.at[leaf], dst, sems.at[k, leaf])
            for k, (src, dst) in enumerate(pairs)
        ]

    for leaf in range(LD):
        for copy in fetch(leaf):
            copy.start()
    ids[...] = jnp.zeros_like(ids)
    named = far[...]
    ids[:LD, : SIDE * SIDE] = jnp.where(named >= 0, named & (LD - 1), -1).astype(F32)
    target_msg[LD * F :, :] = ids[...].astype(BF)
    position = lax.broadcasted_iota(jnp.int32, (LP, SK), 0)
    node[...] = jnp.zeros_like(node)
    for leaf in range(LD):
        for copy in fetch(leaf):
            copy.wait()
        charge = jnp.dot(
            near_msg[leaf, F:, :], own_basis[leaf], preferred_element_type=F32
        ).astype(BF)
        chosen = jnp.where(position == skeleton[leaf : leaf + 1, :], 1.0, 0.0).astype(BF)
        skel = jnp.dot(near_msg[leaf, :F, :], chosen, preferred_element_type=F32).astype(BF)
        source_msg[leaf * 2 * F : leaf * 2 * F + F, :] = charge
        source_msg[leaf * 2 * F + F : (leaf + 1) * 2 * F, :] = skel
        target_msg[leaf * F : (leaf + 1) * F, :] = skel
        node[...] += jnp.dot(charge, own_transfer[leaf], preferred_element_type=F32)
    source_msg[LD * 2 * F :, :] = node[...].astype(BF)


def prep(points, sides, basis, transfer, skeleton, far):
    anywhere = pl.BlockSpec(memory_space=pl.ANY)
    return pl.pallas_call(
        prep_kernel,
        in_specs=[anywhere] * 4 + [VM] * 2,
        out_specs=[VM] * 3,
        out_shape=[
            jax.ShapeDtypeStruct((LD, 2 * F, LP), BF),
            jax.ShapeDtypeStruct((LD * 2 * F + RHS, SK), BF),
            jax.ShapeDtypeStruct((LD * F + 16, SK), BF),
        ],
        scratch_shapes=[
            pltpu.VMEM((LD, LP, SK), BF),
            pltpu.VMEM((LD, SK, SK), BF),
            pltpu.VMEM((RHS, SK), F32),
            pltpu.VMEM((16, SK), F32),
            pltpu.SemaphoreType.DMA((4, LD)),
        ],
        compiler_params=params(56),
        cost_estimate=cost(4),
        name="prep",
    )(points, sides, basis, transfer, skeleton, far)


def far_run(ids, columns, jobs, side_of, weight_of, tile):
    depth = len(columns)

    def first(slot, job):
        row, target, _ = job
        points = target_side(target())
        for d, column in enumerate(columns):
            at = jnp.maximum(ids[row, column], 0)
            tile[slot, d * SK : (d + 1) * SK, :] = jnp.exp(
                jnp.dot(side_of(d, at), points, preferred_element_type=F32)
            ).astype(BF)

    def second(slot, job):
        row, _, store = job
        weights = []
        for d, column in enumerate(columns):
            named = ids[row, column]
            weight = weight_of(d, jnp.maximum(named, 0))
            weights.append(jnp.where(named >= 0, weight, jnp.zeros_like(weight)))
        weight = weights[0] if depth == 1 else jnp.concatenate(weights, axis=1)
        store(jnp.dot(weight, tile[slot, : depth * SK, :], preferred_element_type=F32))

    slots = 2 * BATCH
    groups = [jobs[i : i + BATCH] for i in range(0, len(jobs), BATCH)]
    for g in range(len(groups) + 1):
        if g < len(groups):
            for k, job in enumerate(groups[g]):
                first((g * BATCH + k) % slots, job)
        if g > 0:
            for k, job in enumerate(groups[g - 1]):
                second(((g - 1) * BATCH + k) % slots, job)


def target_jobs(base, target, out, given=None):
    def job(leaf):
        rows = slice(leaf * F, leaf * F + F)

        def store(total):
            if given is not None:
                total = total + given[rows, :]
            out[rows, :] = total.astype(out.dtype)

        return base * LD + leaf, lambda: target[rows, :], store

    return [job(leaf) for leaf in range(LD)]


def rows_of(leaf):
    return pl.ds(pl.multiple_of(leaf * F, F), F)


def charges_at(source, leaf):
    return source[pl.ds(pl.multiple_of(leaf * 2 * F, 2 * F), RHS), :]


def skeleton_at(source, leaf):
    return source[pl.ds(pl.multiple_of(leaf * 2 * F + F, F), F), :]


def columns_of(place):
    x, z = place[0], place[1]
    return [lax.rem(x + shift, SIDE) * SIDE + z for shift in (0, SIDE - 1, 1, 2)]


def sides_kernel(s0, s1, s2, side):
    for d, source in enumerate((s0, s1, s2)):

        @pl.loop(0, LD, unroll=UNROLL)
        def _(leaf, d=d, source=source):
            side[d * LD + leaf] = source_side(skeleton_at(source, leaf))


def sides_of(sources):
    return pl.pallas_call(
        sides_kernel,
        in_specs=[VM] * 3,
        out_specs=VM,
        out_shape=jax.ShapeDtypeStruct((3 * LD, SK, AUG), BF),
        compiler_params=params(16),
        cost_estimate=cost(0.01),
        name="sides",
    )(*sources)


def far_a_kernel(ids, place, side, s0, s1, s2, t0, t1, t2, o0, o1, o2, tile):
    jobs = []
    for b, (target, out) in enumerate(((t0, o0), (t1, o1), (t2, o2))):
        jobs += target_jobs(b, target, out)
    far_run(
        ids, columns_of(place)[:3], jobs, lambda d, at: side[d * LD + at],
        lambda d, at: charges_at((s0, s1, s2)[d], at), tile,
    )


def far_a(ids, place, side, sources, targets):
    return pl.pallas_call(
        far_a_kernel,
        in_specs=[SM, SM] + [VM] * 7,
        out_specs=[VM] * 3,
        out_shape=[jax.ShapeDtypeStruct((LD * F, SK), F32)] * 3,
        scratch_shapes=[pltpu.VMEM((2 * BATCH, 3 * SK, SK), BF)],
        compiler_params=params(16),
        cost_estimate=cost(0.01),
        name="far_a",
    )(ids, place, side, *sources, *targets)


def far_b_kernel(ids, place, side, s0, s1, s2, s3, t3, o3, last, tile):
    @pl.loop(0, LD, unroll=UNROLL)
    def _(leaf):
        last[leaf] = source_side(skeleton_at(s3, leaf))

    far_run(
        ids, columns_of(place), target_jobs(3, t3, o3),
        lambda d, at: last[at] if d == 3 else side[d * LD + at],
        lambda d, at: charges_at((s0, s1, s2, s3)[d], at), tile,
    )


def far_b(ids, place, side, sources, target):
    return pl.pallas_call(
        far_b_kernel,
        in_specs=[SM, SM] + [VM] * 6,
        out_specs=[VM] * 2,
        out_shape=[
            jax.ShapeDtypeStruct((LD * F, SK), BF),
            jax.ShapeDtypeStruct((LD, SK, AUG), BF),
        ],
        scratch_shapes=[pltpu.VMEM((2 * BATCH, SIDE * SK, SK), BF)],
        compiler_params=params(16),
        cost_estimate=cost(3),
        name="far_b",
    )(ids, place, side, *sources, target)


def far_c_kernel(ids, place, side, s3, t0, t1, t2, a0, a1, a2, own, r1, r2, tile):
    jobs = []
    for b, (target, given, out) in enumerate(((t0, a0, own), (t1, a1, r1), (t2, a2, r2))):
        jobs += target_jobs(b, target, out, given)
    far_run(
        ids, columns_of(place)[3:], jobs, lambda d, at: side[at],
        lambda d, at: charges_at(s3, at), tile,
    )


def far_c(ids, place, side, source, targets, given):
    return pl.pallas_call(
        far_c_kernel,
        in_specs=[SM, SM] + [VM] * 8,
        out_specs=[VM] * 3,
        out_shape=[jax.ShapeDtypeStruct((LD * F, SK), F32)]
        + [jax.ShapeDtypeStruct((LD * F, SK), BF)] * 2,
        scratch_shapes=[pltpu.VMEM((2 * BATCH, SK, SK), BF)],
        compiler_params=params(16),
        cost_estimate=cost(4),
        name="far_c",
    )(ids, place, side, source, *targets, *given)


def top_kernel(mine, pair, n1, n2, n3, top, sent):
    points = target_side(mine[RHS:, :])
    total = jnp.zeros((RHS, SK), F32)
    rows = 2 * RHS
    others = [pair] + [n.at[i * rows : (i + 1) * rows] for n in (n1, n2, n3) for i in range(2)]
    for other in others:
        kernel = jnp.exp(
            jnp.dot(source_side(other[RHS:, :]), points, preferred_element_type=F32)
        ).astype(BF)
        total += jnp.dot(other[:RHS, :], kernel, preferred_element_type=F32)
    top[...] = total
    sent[...] = total.astype(BF)


def top_sum(mine, pair, others):
    return pl.pallas_call(
        top_kernel,
        in_specs=[VM] * 5,
        out_specs=[VM] * 2,
        out_shape=[
            jax.ShapeDtypeStruct((RHS, SK), F32),
            jax.ShapeDtypeStruct((RHS, SK), BF),
        ],
        compiler_params=params(16),
        cost_estimate=cost(0.01),
        name="top_sum",
    )(mine, pair, *others)


def near_groups(ids, leaf, place_of, points, side, rights, slots, out, given=None):
    count = jnp.int32(0)
    for d in range(ids.shape[1]):
        slots[d] = 0
    for d in range(ids.shape[1]):
        here, at = place_of(ids[leaf, d])
        slots[count] = jnp.where(here, at, 0)
        count += here.astype(jnp.int32)
    size = 4

    def group(start, used, total):
        tiles, weights = [], []
        for d in range(used):
            at = slots[start + d]
            tiles.append(
                jnp.exp(jnp.dot(side[at], points, preferred_element_type=F32)).astype(BF)
            )
            weights.append(rights(at))
        return total + jnp.dot(
            jnp.concatenate(weights, axis=1),
            jnp.concatenate(tiles, axis=0),
            preferred_element_type=F32,
        )

    full = lax.div(count, size)
    total = lax.fori_loop(
        0, full, lambda g, t: group(g * size, size, t), jnp.zeros((RHS, LP), F32)
    )
    out[...] = total if given is None else total + given[...]
    for used in range(1, size):

        @pl.when(count - full * size == used)
        def _(used=used):
            out[...] = group(full * size, used, out[...])


def near_own_kernel(ids, first, own, out, side, slots):
    @pl.loop(0, LD, unroll=4)
    def _(leaf):
        side[leaf] = source_side(own[leaf, :F, :])

    def place_of(named):
        at = named - first[0]
        return (named >= 0) & (at >= 0) & (at < LD), at

    @pl.loop(0, LD)
    def _(leaf):
        points = target_side(own[leaf, :F, :])
        near_groups(
            ids, leaf, place_of, points, side, lambda at: own[at, F:, :], slots, out.at[leaf]
        )


def near_own(ids, first, own):
    return pl.pallas_call(
        near_own_kernel,
        in_specs=[SM, SM, VM],
        out_specs=VM,
        out_shape=jax.ShapeDtypeStruct((LD, RHS, LP), F32),
        scratch_shapes=[pltpu.VMEM((LD, LP, AUG), BF), pltpu.SMEM((16,), jnp.int32)],
        compiler_params=params(16),
        cost_estimate=cost(9),
        name="near_own",
    )(ids, first, own)


def near_rest_leaves(ids, first, own, given, out, side, rights, slots, begin):
    def place_of(named):
        at = named - first[0]
        below = (at >= -LD) & (at < 0)
        above = (at >= LD) & (at < 2 * LD)
        return (named >= 0) & (below | above), jnp.where(below, at + LD, at)

    @pl.loop(0, out.shape[0])
    def _(k):
        leaf = k + begin
        points = target_side(own[leaf, :F, :])
        near_groups(
            ids, leaf, place_of, points, side, lambda at: rights[at], slots, out.at[k],
            given.at[leaf],
        )


def near_rest_a_kernel(ids, first, own, before, after, given, out, side, rights, slots):
    for d, block in enumerate((before, after)):

        @pl.loop(0, LD, unroll=4)
        def _(leaf, d=d, block=block):
            side[d * LD + leaf] = source_side(block[leaf, :F, :])
            rights[d * LD + leaf] = block[leaf, F:, :]

    near_rest_leaves(ids, first, own, given, out, side, rights, slots, 0)


def near_rest_b_kernel(ids, first, own, side, rights, given, out, slots):
    near_rest_leaves(ids, first, own, given, out, side, rights, slots, LD // 2)


def near_rest_a(ids, first, own, before, after, given):
    return pl.pallas_call(
        near_rest_a_kernel,
        in_specs=[SM, SM, VM, VM, VM, VM],
        out_specs=[VM] * 3,
        out_shape=[
            jax.ShapeDtypeStruct((LD // 2, RHS, LP), F32),
            jax.ShapeDtypeStruct((2 * LD, LP, AUG), BF),
            jax.ShapeDtypeStruct((2 * LD, RHS, LP), BF),
        ],
        scratch_shapes=[pltpu.SMEM((16,), jnp.int32)],
        compiler_params=params(16),
        cost_estimate=cost(0.01),
        name="near_rest_a",
    )(ids, first, own, before, after, given)


def near_rest_b(ids, first, own, side, rights, given):
    return pl.pallas_call(
        near_rest_b_kernel,
        in_specs=[SM, SM, VM, VM, VM, VM],
        out_specs=VM,
        out_shape=jax.ShapeDtypeStruct((LD // 2, RHS, LP), F32),
        scratch_shapes=[pltpu.SMEM((16,), jnp.int32)],
        compiler_params=params(16),
        cost_estimate=cost(0.01),
        name="near_rest_b",
    )(ids, first, own, side, rights, given)


def final_kernel(near_a, near_b, basis, transfer, own, r1, r2, r3, top, q1, q2, q3, out):
    nt = (((1,), (1,)), ((), ()))
    total = top[...]
    for q in (q1, q2, q3):
        total += q[...].astype(F32)
    total = total.astype(BF)
    half = LD // 2
    for h, near_sum in enumerate((near_a, near_b)):

        @pl.loop(0, half, unroll=half)
        def _(k, h=h, near_sum=near_sum):
            leaf = h * half + k
            rows = rows_of(leaf)
            potential = own[rows, :]
            for r in (r1, r2, r3):
                potential += r[rows, :].astype(F32)
            potential += lax.dot_general(total, transfer[leaf], nt, preferred_element_type=F32)
            far_out = lax.dot_general(
                potential.astype(BF), basis[leaf], nt, preferred_element_type=F32
            )
            out[leaf] = (near_sum[k] + far_out).astype(BF)


def final(near_sums, basis, transfer, own, returned, top, others):
    return pl.pallas_call(
        final_kernel,
        in_specs=[VM] * 12,
        out_specs=VM,
        out_shape=jax.ShapeDtypeStruct((LD, RHS, LP), BF),
        compiler_params=params(16),
        cost_estimate=cost(3),
        name="final",
    )(*near_sums, basis, transfer, own, *returned, top, *others)


def shifted(value, dx, dz):
    pairs = []
    for x in range(SIDE):
        for z in range(SIDE):
            to = (x + dx) % SIDE * SIDE + (z + dz) % SIDE
            pairs.append((x * SIDE + z, to))
    return lax.ppermute(value, "top", pairs)


def leaf_shifted(value, dy):
    count = lax.axis_size("leaf")
    if dy == 0:
        return lax.ppermute(value, "leaf", [(i, i ^ 1) for i in range(count)])
    return lax.ppermute(value, "leaf", [(i, (i + 2 * dy) % count) for i in range(count)])


def on_device(
    points, right_sides, leaf_basis, transfer, node_points, neighbours, far_sources, skeleton
):
    node, at = lax.axis_index("leaf"), lax.axis_index("top")
    position = node * SIDE * SIDE + at
    near_msg, source_msg, target_msg = prep(
        points, right_sides, leaf_basis, transfer, skeleton, far_sources
    )
    sources = [source_msg] + [shifted(source_msg, dx, 0) for dx in (1, -1)]
    targets = [target_msg] + [shifted(target_msg, 0, dz) for dz in (1, -1, 2)]
    first = (position * LD).astype(jnp.int32).reshape(1)
    near_sum = near_own(neighbours, first, near_msg)

    targets[:3], sources, near_msg, near_sum = lax.optimization_barrier(
        (targets[:3], sources, near_msg, near_sum)
    )
    opposite = shifted(sources[1], 1, 0)
    side = sides_of(sources)
    near_msg, side = lax.optimization_barrier((near_msg, side))
    count = lax.axis_size("leaf") * lax.axis_size("top")
    up = [(i, i + 1) for i in range(count - 1)]
    before = lax.ppermute(near_msg, ("leaf", "top"), up)
    after = lax.ppermute(near_msg, ("leaf", "top"), [(j, i) for i, j in up])

    def ids_of(which):
        ids = jnp.concatenate([t[LD * F : LD * F + LD, : SIDE * SIDE] for t in which])
        return ids.astype(jnp.int32)

    place = jnp.stack([at // SIDE, at % SIDE]).astype(jnp.int32)
    given = far_a(ids_of(targets[:3]), place, side, sources, targets[:3])
    opposite, given, targets[3] = lax.optimization_barrier((opposite, given, targets[3]))
    sources.append(opposite)
    line_charge = sum(s[2 * LD * F :].astype(F32) for s in sources)
    mine = jnp.concatenate([line_charge.astype(BF), node_points[0]], axis=0)
    pair = leaf_shifted(mine, 0)
    ids = ids_of(targets)
    r3, last = far_b(ids, place, side, sources, targets[3])
    pair, r3, last = lax.optimization_barrier((pair, r3, last))
    both = jnp.concatenate([mine, pair], axis=0)
    others = [leaf_shifted(both, dy) for dy in (1, -1, 2)]
    own, r1, r2 = far_c(ids, place, last, opposite, targets[:3], given)
    before, after, r1, r2, r3 = lax.optimization_barrier((before, after, r1, r2, r3))
    returned = [shifted(r, 0, dz) for r, dz in zip((r1, r2, r3), (-1, 1, 2))]
    near_a, near_side, near_rights = near_rest_a(
        neighbours, first, near_msg, before, after, near_sum
    )
    others, near_side = lax.optimization_barrier((others, near_side))
    top, sent = top_sum(mine, pair, others)
    tops = [shifted(sent, 0, dz) for dz in (1, -1, 2)]
    top, near_side, returned[2] = lax.optimization_barrier((top, near_side, returned[2]))
    near_b = near_rest_b(neighbours, first, near_msg, near_side, near_rights, near_sum)
    return final((near_a, near_b), leaf_basis, transfer, own, returned, top, tops)


def solution(mesh):
    leaves = P(("leaf", "top"), None, None)
    lists = P(("leaf", "top"), None)
    in_specs = (leaves, leaves, leaves, leaves, P("leaf", None, None), lists, lists, lists)
    return jax.shard_map(
        on_device, mesh=mesh, in_specs=in_specs, out_specs=leaves, check_vma=False
    )
```

```python
import functools

import jax
import jax.numpy as jnp
from jax import lax
from jax.experimental import pallas as pl
from jax.experimental.pallas import tpu as pltpu
from jax.sharding import PartitionSpec as P

BF = jnp.bfloat16
F32 = jnp.float32
F = 64
RHS = 64
LP = 512
SK = 256
LD = 8
HALF = 4
ABSENT = -32
SIDE = 4
AUG = 128
UNROLL = 8
BATCH = 2
VM = pl.BlockSpec(memory_space=pltpu.VMEM)
SM = pl.BlockSpec(memory_space=pltpu.SMEM)


def params(mib=40):
    return pltpu.CompilerParams(vmem_limit_bytes=mib * 2**20)


def cost(us):
    return pl.CostEstimate(flops=int(us * 10**9), bytes_accessed=10**6, transcendentals=0)


def norm_rows(points, first):
    norm = jnp.sum(points * points, axis=0, keepdims=True) * (-2.0 / F)
    high = norm.astype(BF).astype(F32)
    mid = (norm - high).astype(BF).astype(F32)
    low = norm - high - mid
    row = lax.broadcasted_iota(jnp.int32, (16, points.shape[1]), 0)
    at = 0 if first else 3
    ones = jnp.where(row < 6, 1.0, 0.0).astype(F32)
    rows = jnp.where(row == at + 1, mid, jnp.where(row == at + 2, low, ones))
    return jnp.where(row == at, high, rows)


def source_side(points):
    points = points.astype(F32)
    zeros = jnp.zeros((AUG - F - 16, points.shape[1]), F32)
    full = jnp.concatenate([points, norm_rows(points, True), zeros], axis=0)
    return full.astype(BF).T


def target_side(points):
    points = points.astype(F32)
    zeros = jnp.zeros((AUG - F - 16, points.shape[1]), F32)
    full = jnp.concatenate([points * (4.0 / F), norm_rows(points, False), zeros], axis=0)
    return full.astype(BF)


def half_of(low, high, leaf):
    return (low, leaf) if leaf < HALF else (high, leaf - HALF)


def points_at(pair):
    block, leaf = pair
    return block.at[leaf * 2 * F : leaf * 2 * F + F, :]


def sides_at(pair):
    block, leaf = pair
    return block.at[leaf * 2 * F + F : (leaf + 1) * 2 * F, :]


def prep_kernel(
    first, points, sides, basis, transfer, skeleton, far, near, low, high, source_msg,
    target_msg, own_basis, own_transfer, node, ids, near_ids, sems,
):
    def fetch(leaf):
        place = half_of(low, high, leaf)
        pairs = (
            (points, points_at(place)),
            (sides, sides_at(place)),
            (basis, own_basis.at[leaf]),
            (transfer, own_transfer.at[leaf]),
        )
        return [
            pltpu.make_async_copy(src.at[leaf], dst, sems.at[k, leaf])
            for k, (src, dst) in enumerate(pairs)
        ]

    for leaf in range(LD):
        for copy in fetch(leaf):
            copy.start()
    ids[...] = jnp.zeros_like(ids)
    named = far[...]
    ids[:LD, : SIDE * SIDE] = jnp.where(named >= 0, named & (LD - 1), -1).astype(F32)
    target_msg[LD * F :, :] = ids[...].astype(BF)
    near_ids[...] = jnp.zeros_like(near_ids)
    named = near[...]
    own_leaf = first[0] + lax.broadcasted_iota(jnp.int32, named.shape, 0)
    near_ids[:LD, : named.shape[1]] = jnp.where(named >= 0, named - own_leaf, ABSENT).astype(F32)
    for block in (low, high):
        block[HALF * 2 * F :, :] = near_ids[...].astype(BF)
    position = lax.broadcasted_iota(jnp.int32, (LP, SK), 0)
    node[...] = jnp.zeros_like(node)
    for leaf in range(LD):
        place = half_of(low, high, leaf)
        for copy in fetch(leaf):
            copy.wait()
        charge = jnp.dot(
            sides_at(place)[...], own_basis[leaf], preferred_element_type=F32
        ).astype(BF)
        chosen = jnp.where(position == skeleton[leaf : leaf + 1, :], 1.0, 0.0).astype(BF)
        skel = jnp.dot(points_at(place)[...], chosen, preferred_element_type=F32).astype(BF)
        source_msg[leaf * 2 * F : leaf * 2 * F + F, :] = charge
        source_msg[leaf * 2 * F + F : (leaf + 1) * 2 * F, :] = skel
        target_msg[leaf * F : (leaf + 1) * F, :] = skel
        node[...] += jnp.dot(charge, own_transfer[leaf], preferred_element_type=F32)
    source_msg[LD * 2 * F :, :] = node[...].astype(BF)


def prep(first, points, sides, basis, transfer, skeleton, far, near):
    anywhere = pl.BlockSpec(memory_space=pl.ANY)
    return pl.pallas_call(
        prep_kernel,
        in_specs=[SM] + [anywhere] * 4 + [VM] * 3,
        out_specs=[VM] * 4,
        out_shape=[jax.ShapeDtypeStruct((HALF * 2 * F + 16, LP), BF)] * 2
        + [
            jax.ShapeDtypeStruct((LD * 2 * F + RHS, SK), BF),
            jax.ShapeDtypeStruct((LD * F + 16, SK), BF),
        ],
        scratch_shapes=[
            pltpu.VMEM((LD, LP, SK), BF),
            pltpu.VMEM((LD, SK, SK), BF),
            pltpu.VMEM((RHS, SK), F32),
            pltpu.VMEM((16, SK), F32),
            pltpu.VMEM((16, LP), F32),
            pltpu.SemaphoreType.DMA((4, LD)),
        ],
        compiler_params=params(56),
        cost_estimate=cost(4),
        name="prep",
    )(first, points, sides, basis, transfer, skeleton, far, near)


def far_run(ids, columns, jobs, side_of, weight_of, tile):
    depth = len(columns)

    def first(slot, job):
        row, target, _ = job
        points = target_side(target())
        for d, column in enumerate(columns):
            at = jnp.maximum(ids[row, column], 0)
            tile[slot, d * SK : (d + 1) * SK, :] = jnp.exp(
                jnp.dot(side_of(d, at), points, preferred_element_type=F32)
            ).astype(BF)

    def second(slot, job):
        row, _, store = job
        weights = []
        for d, column in enumerate(columns):
            named = ids[row, column]
            weight = weight_of(d, jnp.maximum(named, 0))
            weights.append(jnp.where(named >= 0, weight, jnp.zeros_like(weight)))
        weight = weights[0] if depth == 1 else jnp.concatenate(weights, axis=1)
        store(jnp.dot(weight, tile[slot, : depth * SK, :], preferred_element_type=F32))

    slots = 2 * BATCH
    groups = [jobs[i : i + BATCH] for i in range(0, len(jobs), BATCH)]
    for g in range(len(groups) + 1):
        if g < len(groups):
            for k, job in enumerate(groups[g]):
                first((g * BATCH + k) % slots, job)
        if g > 0:
            for k, job in enumerate(groups[g - 1]):
                second(((g - 1) * BATCH + k) % slots, job)


def target_jobs(base, target, out, given=None):
    def job(leaf):
        rows = slice(leaf * F, leaf * F + F)

        def store(total):
            if given is not None:
                total = total + given[rows, :]
            out[rows, :] = total.astype(out.dtype)

        return base * LD + leaf, lambda: target[rows, :], store

    return [job(leaf) for leaf in range(LD)]


def rows_of(leaf):
    return pl.ds(pl.multiple_of(leaf * F, F), F)


def charges_at(source, leaf):
    return source[pl.ds(pl.multiple_of(leaf * 2 * F, 2 * F), RHS), :]


def skeleton_at(source, leaf):
    return source[pl.ds(pl.multiple_of(leaf * 2 * F + F, F), F), :]


def columns_of(place):
    x, z = place[0], place[1]
    return [lax.rem(x + shift, SIDE) * SIDE + z for shift in (0, SIDE - 1, 1, 2)]


def sides_kernel(s0, s1, s2, side):
    for d, source in enumerate((s0, s1, s2)):

        @pl.loop(0, LD, unroll=UNROLL)
        def _(leaf, d=d, source=source):
            side[d * LD + leaf] = source_side(skeleton_at(source, leaf))


def sides_of(sources):
    return pl.pallas_call(
        sides_kernel,
        in_specs=[VM] * 3,
        out_specs=VM,
        out_shape=jax.ShapeDtypeStruct((3 * LD, SK, AUG), BF),
        compiler_params=params(16),
        cost_estimate=cost(0.01),
        name="sides",
    )(*sources)


def far_a_kernel(ids, place, side, s0, s1, s2, t0, t1, t2, o0, o1, o2, tile):
    jobs = []
    for b, (target, out) in enumerate(((t0, o0), (t1, o1), (t2, o2))):
        jobs += target_jobs(b, target, out)
    far_run(
        ids, columns_of(place)[:3], jobs, lambda d, at: side[d * LD + at],
        lambda d, at: charges_at((s0, s1, s2)[d], at), tile,
    )


def far_a(ids, place, side, sources, targets):
    return pl.pallas_call(
        far_a_kernel,
        in_specs=[SM, SM] + [VM] * 7,
        out_specs=[VM] * 3,
        out_shape=[jax.ShapeDtypeStruct((LD * F, SK), F32)] * 3,
        scratch_shapes=[pltpu.VMEM((2 * BATCH, 3 * SK, SK), BF)],
        compiler_params=params(16),
        cost_estimate=cost(0.01),
        name="far_a",
    )(ids, place, side, *sources, *targets)


def far_b_kernel(ids, place, side, s0, s1, s2, s3, t3, o3, last, tile):
    @pl.loop(0, LD, unroll=UNROLL)
    def _(leaf):
        last[leaf] = source_side(skeleton_at(s3, leaf))

    far_run(
        ids, columns_of(place), target_jobs(3, t3, o3),
        lambda d, at: last[at] if d == 3 else side[d * LD + at],
        lambda d, at: charges_at((s0, s1, s2, s3)[d], at), tile,
    )


def far_b(ids, place, side, sources, target):
    return pl.pallas_call(
        far_b_kernel,
        in_specs=[SM, SM] + [VM] * 6,
        out_specs=[VM] * 2,
        out_shape=[
            jax.ShapeDtypeStruct((LD * F, SK), BF),
            jax.ShapeDtypeStruct((LD, SK, AUG), BF),
        ],
        scratch_shapes=[pltpu.VMEM((2 * BATCH, SIDE * SK, SK), BF)],
        compiler_params=params(16),
        cost_estimate=cost(3),
        name="far_b",
    )(ids, place, side, *sources, target)


def far_c_kernel(ids, place, side, s3, t0, t1, t2, a0, a1, a2, own, r1, r2, tile):
    jobs = []
    for b, (target, given, out) in enumerate(((t0, a0, own), (t1, a1, r1), (t2, a2, r2))):
        jobs += target_jobs(b, target, out, given)
    far_run(
        ids, columns_of(place)[3:], jobs, lambda d, at: side[at],
        lambda d, at: charges_at(s3, at), tile,
    )


def far_c(ids, place, side, source, targets, given):
    return pl.pallas_call(
        far_c_kernel,
        in_specs=[SM, SM] + [VM] * 8,
        out_specs=[VM] * 3,
        out_shape=[jax.ShapeDtypeStruct((LD * F, SK), F32)]
        + [jax.ShapeDtypeStruct((LD * F, SK), BF)] * 2,
        scratch_shapes=[pltpu.VMEM((2 * BATCH, SK, SK), BF)],
        compiler_params=params(16),
        cost_estimate=cost(4),
        name="far_c",
    )(ids, place, side, source, *targets, *given)


def top_kernel(mine, pair, n1, n2, n3, a1, a2, a3, top, r1, r2, r3):
    points = target_side(mine[RHS:, :])
    total = jnp.zeros((RHS, SK), F32)
    rows = 2 * RHS
    others = [pair] + [n.at[i * rows : (i + 1) * rows] for n in (n1, n2, n3) for i in range(2)]
    for other in others:
        kernel = jnp.exp(
            jnp.dot(source_side(other[RHS:, :]), points, preferred_element_type=F32)
        ).astype(BF)
        total += jnp.dot(other[:RHS, :], kernel, preferred_element_type=F32)
    top[...] = total
    for given, out in ((a1, r1), (a2, r2), (a3, r3)):
        out[: LD * F, :] = given[...]
        out[LD * F :, :] = total.astype(BF)


def top_sum(mine, pair, others, parts):
    return pl.pallas_call(
        top_kernel,
        in_specs=[VM] * 8,
        out_specs=[VM] * 4,
        out_shape=[jax.ShapeDtypeStruct((RHS, SK), F32)]
        + [jax.ShapeDtypeStruct((LD * F + RHS, SK), BF)] * 3,
        compiler_params=params(16),
        cost_estimate=cost(2),
        name="top_sum",
    )(mine, pair, *others, *parts)


def near_groups(ids, leaf, place_of, points, side, rights, slots, out, given=None):
    count = jnp.int32(0)
    for d in range(ids.shape[1]):
        slots[d] = 0
    for d in range(ids.shape[1]):
        here, at = place_of(ids[leaf, d])
        slots[count] = jnp.where(here, at, 0)
        count += here.astype(jnp.int32)
    size = 4

    def group(start, used, total):
        tiles, weights = [], []
        for d in range(used):
            at = slots[start + d]
            tiles.append(
                jnp.exp(jnp.dot(side[at], points, preferred_element_type=F32)).astype(BF)
            )
            weights.append(rights(at))
        return total + jnp.dot(
            jnp.concatenate(weights, axis=1),
            jnp.concatenate(tiles, axis=0),
            preferred_element_type=F32,
        )

    full = lax.div(count, size)
    total = lax.fori_loop(
        0, full, lambda g, t: group(g * size, size, t), jnp.zeros((RHS, LP), F32)
    )
    out[...] = total if given is None else total + given[...]
    for used in range(1, size):

        @pl.when(count - full * size == used)
        def _(used=used):
            out[...] = group(full * size, used, out[...])


def near_own_kernel(ids, first, low, high, out, side, rights, slots):
    for leaf in range(LD):
        place = half_of(low, high, leaf)
        side[leaf] = source_side(points_at(place)[...])
        rights[leaf] = sides_at(place)[...]

    def place_of(named):
        at = named - first[0]
        return (named >= 0) & (at >= 0) & (at < LD), at

    for h, block in enumerate((low, high)):

        @pl.loop(0, HALF)
        def _(k, h=h, block=block):
            leaf = h * HALF + k
            near_groups(
                ids, leaf, place_of, target_side(block_points(block, k)), side,
                lambda at: rights[at], slots, out.at[leaf],
            )


def block_points(block, k):
    return block[pl.ds(pl.multiple_of(k * 2 * F, 2 * F), F), :]


def near_own(ids, first, low, high):
    return pl.pallas_call(
        near_own_kernel,
        in_specs=[SM, SM, VM, VM],
        out_specs=[VM] * 3,
        out_shape=[
            jax.ShapeDtypeStruct((LD, RHS, LP), F32),
            jax.ShapeDtypeStruct((LD, LP, AUG), BF),
            jax.ShapeDtypeStruct((LD, RHS, LP), BF),
        ],
        scratch_shapes=[pltpu.SMEM((16,), jnp.int32)],
        compiler_params=params(16),
        cost_estimate=cost(9),
        name="near_own",
    )(ids, first, low, high)


def near_lent_kernel(offsets, side, rights, before, after, to_prev, to_next, sums, slots):
    for block, out, row, shift, least in (
        (before, to_prev, HALF, HALF - LD, HALF),
        (after, to_next, LD, LD, 0),
    ):

        @pl.loop(0, HALF)
        def _(k, block=block, row=row, shift=shift, least=least):
            def place_of(offset):
                at = k + shift + offset
                return (offset > ABSENT) & (at >= least) & (at < least + HALF), at

            near_groups(
                offsets, row + k, place_of, target_side(block_points(block, k)), side,
                lambda at: rights[at], slots, sums.at[k],
            )

        out[...] = sums[...].astype(BF)


def near_lent(offsets, side, rights, before, after):
    return pl.pallas_call(
        near_lent_kernel,
        in_specs=[SM] + [VM] * 4,
        out_specs=[VM] * 2,
        out_shape=[jax.ShapeDtypeStruct((HALF, RHS, LP), BF)] * 2,
        scratch_shapes=[
            pltpu.VMEM((HALF, RHS, LP), F32),
            pltpu.SMEM((16,), jnp.int32),
        ],
        compiler_params=params(16),
        cost_estimate=cost(4),
        name="near_lent",
    )(offsets, side, rights, before, after)


def near_rest_kernel(ids, first, low, high, before, after, given, out, side, rights, slots):
    for d, block in enumerate((before, after)):
        for leaf in range(HALF):
            side[d * HALF + leaf] = source_side(points_at((block, leaf))[...])
            rights[d * HALF + leaf] = sides_at((block, leaf))[...]

    def place_of(named):
        at = named - first[0]
        below = (at >= -HALF) & (at < 0)
        above = (at >= LD) & (at < LD + HALF)
        return (named >= 0) & (below | above), jnp.where(below, at + HALF, at - HALF)

    for h, block in enumerate((low, high)):

        @pl.loop(0, HALF)
        def _(k, h=h, block=block):
            leaf = h * HALF + k
            near_groups(
                ids, leaf, place_of, target_side(block_points(block, k)), side,
                lambda at: rights[at], slots, out.at[leaf], given.at[leaf],
            )


def near_rest(ids, first, low, high, before, after, given):
    return pl.pallas_call(
        near_rest_kernel,
        in_specs=[SM, SM] + [VM] * 5,
        out_specs=VM,
        out_shape=jax.ShapeDtypeStruct((LD, RHS, LP), F32),
        scratch_shapes=[
            pltpu.VMEM((LD, LP, AUG), BF),
            pltpu.VMEM((LD, RHS, LP), BF),
            pltpu.SMEM((16,), jnp.int32),
        ],
        compiler_params=params(16),
        cost_estimate=cost(7),
        name="near_rest",
    )(ids, first, low, high, before, after, given)


def final_kernel(near_sum, lent_low, lent_high, basis, transfer, own, r1, r2, r3, top, out):
    nt = (((1,), (1,)), ((), ()))
    last = LD * F
    total = top[...]
    for r in (r1, r2, r3):
        total += r[last:, :].astype(F32)
    total = total.astype(BF)

    for leaf in range(LD):
        rows = slice(leaf * F, leaf * F + F)
        potential = own[rows, :]
        for r in (r1, r2, r3):
            potential += r[rows, :].astype(F32)
        potential += lax.dot_general(total, transfer[leaf], nt, preferred_element_type=F32)
        far_out = lax.dot_general(
            potential.astype(BF), basis[leaf], nt, preferred_element_type=F32
        )
        lent, k = half_of(lent_low, lent_high, leaf)
        out[leaf] = (near_sum[leaf] + lent[k].astype(F32) + far_out).astype(BF)


def final(near_sum, lent, basis, transfer, own, returned, top):
    return pl.pallas_call(
        final_kernel,
        in_specs=[VM] * 10,
        out_specs=VM,
        out_shape=jax.ShapeDtypeStruct((LD, RHS, LP), BF),
        compiler_params=params(16),
        cost_estimate=cost(3),
        name="final",
    )(near_sum, *lent, basis, transfer, own, *returned, top)


def shifted(value, dx, dz):
    pairs = []
    for x in range(SIDE):
        for z in range(SIDE):
            to = (x + dx) % SIDE * SIDE + (z + dz) % SIDE
            pairs.append((x * SIDE + z, to))
    return lax.ppermute(value, "top", pairs)


def leaf_shifted(value, dy):
    count = lax.axis_size("leaf")
    if dy == 0:
        return lax.ppermute(value, "leaf", [(i, i ^ 1) for i in range(count)])
    return lax.ppermute(value, "leaf", [(i, (i + 2 * dy) % count) for i in range(count)])


def on_device(
    points, right_sides, leaf_basis, transfer, node_points, neighbours, far_sources, skeleton
):
    node, at = lax.axis_index("leaf"), lax.axis_index("top")
    position = node * SIDE * SIDE + at
    first = (position * LD).astype(jnp.int32).reshape(1)
    near_low, near_high, source_msg, target_msg = prep(
        first, points, right_sides, leaf_basis, transfer, skeleton, far_sources, neighbours
    )
    sources = [source_msg] + [shifted(source_msg, dx, 0) for dx in (1, -1)]
    targets = [target_msg] + [shifted(target_msg, 0, dz) for dz in (1, -1, 2)]
    near_sum, near_side, near_rights = near_own(neighbours, first, near_low, near_high)

    targets[:3], sources, near_low, near_high, near_sum = lax.optimization_barrier(
        (targets[:3], sources, near_low, near_high, near_sum)
    )
    opposite = shifted(sources[1], 1, 0)
    side = sides_of(sources)
    near_low, near_high, side = lax.optimization_barrier((near_low, near_high, side))
    count = lax.axis_size("leaf") * lax.axis_size("top")
    up = [(i, i + 1) for i in range(count - 1)]
    down = [(j, i) for i, j in up]
    before = lax.ppermute(near_high, ("leaf", "top"), up)
    after = lax.ppermute(near_low, ("leaf", "top"), down)

    def ids_of(which):
        ids = jnp.concatenate([t[LD * F : LD * F + LD, : SIDE * SIDE] for t in which])
        return ids.astype(jnp.int32)

    place = jnp.stack([at // SIDE, at % SIDE]).astype(jnp.int32)
    given = far_a(ids_of(targets[:3]), place, side, sources, targets[:3])
    opposite, given, targets[3] = lax.optimization_barrier((opposite, given, targets[3]))
    sources.append(opposite)
    line_charge = sum(s[2 * LD * F :].astype(F32) for s in sources)
    mine = jnp.concatenate([line_charge.astype(BF), node_points[0]], axis=0)
    pair = leaf_shifted(mine, 0)
    ids = ids_of(targets)
    r3, last = far_b(ids, place, side, sources, targets[3])
    pair, r3, last = lax.optimization_barrier((pair, r3, last))
    both = jnp.concatenate([mine, pair], axis=0)
    others = [leaf_shifted(both, dy) for dy in (1, -1, 2)]
    own, r1, r2 = far_c(ids, place, last, opposite, targets[:3], given)
    width = neighbours.shape[1]
    before, after, own = lax.optimization_barrier((before, after, own))
    offsets = jnp.concatenate(
        [block[HALF * 2 * F : HALF * 2 * F + LD, :width] for block in (before, after)]
    ).astype(jnp.int32)
    to_prev, to_next = near_lent(offsets, near_side, near_rights, before, after)
    others, to_prev, to_next = lax.optimization_barrier((others, to_prev, to_next))
    lent = (
        lax.ppermute(to_next, ("leaf", "top"), up),
        lax.ppermute(to_prev, ("leaf", "top"), down),
    )
    top, *parts = top_sum(mine, pair, others, (r1, r2, r3))
    returned = [shifted(r, 0, dz) for r, dz in zip(parts, (-1, 1, 2))]
    near_sum = near_rest(neighbours, first, near_low, near_high, before, after, near_sum)
    return final(near_sum, lent, leaf_basis, transfer, own, returned, top)


def solution(mesh):
    leaves = P(("leaf", "top"), None, None)
    lists = P(("leaf", "top"), None)
    in_specs = (leaves, leaves, leaves, leaves, P("leaf", None, None), lists, lists, lists)
    return jax.shard_map(
        on_device, mesh=mesh, in_specs=in_specs, out_specs=leaves, check_vma=False
    )
```

```python
import functools

import jax
import jax.numpy as jnp
from jax import lax
from jax.experimental import pallas as pl
from jax.experimental.pallas import tpu as pltpu
from jax.sharding import PartitionSpec as P

BF = jnp.bfloat16
F32 = jnp.float32
F = 64
RHS = 64
LP = 512
SK = 256
LD = 8
SIDE = 4
AUG = 128
UNROLL = 8
BATCH = 2
VM = pl.BlockSpec(memory_space=pltpu.VMEM)
SM = pl.BlockSpec(memory_space=pltpu.SMEM)


def params(mib=40):
    return pltpu.CompilerParams(vmem_limit_bytes=mib * 2**20)


def cost(us):
    return pl.CostEstimate(flops=int(us * 10**9), bytes_accessed=10**6, transcendentals=0)


def norm_rows(points, first):
    norm = jnp.sum(points * points, axis=0, keepdims=True) * (-2.0 / F)
    high = norm.astype(BF).astype(F32)
    mid = (norm - high).astype(BF).astype(F32)
    low = norm - high - mid
    row = lax.broadcasted_iota(jnp.int32, (16, points.shape[1]), 0)
    at = 0 if first else 3
    ones = jnp.where(row < 6, 1.0, 0.0).astype(F32)
    rows = jnp.where(row == at + 1, mid, jnp.where(row == at + 2, low, ones))
    return jnp.where(row == at, high, rows)


def source_side(points):
    points = points.astype(F32)
    zeros = jnp.zeros((AUG - F - 16, points.shape[1]), F32)
    full = jnp.concatenate([points, norm_rows(points, True), zeros], axis=0)
    return full.astype(BF).T


def target_side(points):
    points = points.astype(F32)
    zeros = jnp.zeros((AUG - F - 16, points.shape[1]), F32)
    full = jnp.concatenate([points * (4.0 / F), norm_rows(points, False), zeros], axis=0)
    return full.astype(BF)


def prep_kernel(
    points, sides, basis, transfer, skeleton, far, near_msg, source_msg, target_msg,
    own_basis, own_transfer, node, ids, sems,
):
    def fetch(leaf):
        pairs = (
            (points, near_msg.at[leaf, :F, :]),
            (sides, near_msg.at[leaf, F:, :]),
            (basis, own_basis.at[leaf]),
            (transfer, own_transfer.at[leaf]),
        )
        return [
            pltpu.make_async_copy(src.at[leaf], dst, sems.at[k, leaf])
            for k, (src, dst) in enumerate(pairs)
        ]

    for leaf in range(LD):
        for copy in fetch(leaf):
            copy.start()
    ids[...] = jnp.zeros_like(ids)
    named = far[...]
    ids[:LD, : SIDE * SIDE] = jnp.where(named >= 0, named & (LD - 1), -1).astype(F32)
    target_msg[LD * F :, :] = ids[...].astype(BF)
    position = lax.broadcasted_iota(jnp.int32, (LP, SK), 0)
    node[...] = jnp.zeros_like(node)
    for leaf in range(LD):
        for copy in fetch(leaf):
            copy.wait()
        charge = jnp.dot(
            near_msg[leaf, F:, :], own_basis[leaf], preferred_element_type=F32
        ).astype(BF)
        chosen = jnp.where(position == skeleton[leaf : leaf + 1, :], 1.0, 0.0).astype(BF)
        skel = jnp.dot(near_msg[leaf, :F, :], chosen, preferred_element_type=F32).astype(BF)
        source_msg[leaf * 2 * F : leaf * 2 * F + F, :] = charge
        source_msg[leaf * 2 * F + F : (leaf + 1) * 2 * F, :] = skel
        target_msg[leaf * F : (leaf + 1) * F, :] = skel
        node[...] += jnp.dot(charge, own_transfer[leaf], preferred_element_type=F32)
    source_msg[LD * 2 * F :, :] = node[...].astype(BF)


def prep(points, sides, basis, transfer, skeleton, far):
    anywhere = pl.BlockSpec(memory_space=pl.ANY)
    return pl.pallas_call(
        prep_kernel,
        in_specs=[anywhere] * 4 + [VM] * 2,
        out_specs=[VM] * 3,
        out_shape=[
            jax.ShapeDtypeStruct((LD, 2 * F, LP), BF),
            jax.ShapeDtypeStruct((LD * 2 * F + RHS, SK), BF),
            jax.ShapeDtypeStruct((LD * F + 16, SK), BF),
        ],
        scratch_shapes=[
            pltpu.VMEM((LD, LP, SK), BF),
            pltpu.VMEM((LD, SK, SK), BF),
            pltpu.VMEM((RHS, SK), F32),
            pltpu.VMEM((16, SK), F32),
            pltpu.SemaphoreType.DMA((4, LD)),
        ],
        compiler_params=params(56),
        cost_estimate=cost(4),
        name="prep",
    )(points, sides, basis, transfer, skeleton, far)


def far_run(ids, columns, jobs, side_of, weight_of, tile):
    depth = len(columns)

    def first(slot, job):
        row, target, _ = job
        points = target_side(target())
        for d, column in enumerate(columns):
            at = jnp.maximum(ids[row, column], 0)
            tile[slot, d * SK : (d + 1) * SK, :] = jnp.exp(
                jnp.dot(side_of(d, at), points, preferred_element_type=F32)
            ).astype(BF)

    def second(slot, job):
        row, _, store = job
        weights = []
        for d, column in enumerate(columns):
            named = ids[row, column]
            weight = weight_of(d, jnp.maximum(named, 0))
            weights.append(jnp.where(named >= 0, weight, jnp.zeros_like(weight)))
        weight = weights[0] if depth == 1 else jnp.concatenate(weights, axis=1)
        store(jnp.dot(weight, tile[slot, : depth * SK, :], preferred_element_type=F32))

    slots = 2 * BATCH
    groups = [jobs[i : i + BATCH] for i in range(0, len(jobs), BATCH)]
    for g in range(len(groups) + 1):
        if g < len(groups):
            for k, job in enumerate(groups[g]):
                first((g * BATCH + k) % slots, job)
        if g > 0:
            for k, job in enumerate(groups[g - 1]):
                second(((g - 1) * BATCH + k) % slots, job)


def target_jobs(base, target, out, given=None):
    def job(leaf):
        rows = slice(leaf * F, leaf * F + F)

        def store(total):
            if given is not None:
                total = total + given[rows, :]
            out[rows, :] = total.astype(out.dtype)

        return base * LD + leaf, lambda: target[rows, :], store

    return [job(leaf) for leaf in range(LD)]


def rows_of(leaf):
    return pl.ds(pl.multiple_of(leaf * F, F), F)


def charges_at(source, leaf):
    return source[pl.ds(pl.multiple_of(leaf * 2 * F, 2 * F), RHS), :]


def skeleton_at(source, leaf):
    return source[pl.ds(pl.multiple_of(leaf * 2 * F + F, F), F), :]


def columns_of(place):
    x, z = place[0], place[1]
    return [lax.rem(x + shift, SIDE) * SIDE + z for shift in (0, SIDE - 1, 1, 2)]


def sides_kernel(s0, s1, s2, side):
    for d, source in enumerate((s0, s1, s2)):

        @pl.loop(0, LD, unroll=UNROLL)
        def _(leaf, d=d, source=source):
            side[d * LD + leaf] = source_side(skeleton_at(source, leaf))


def sides_of(sources):
    return pl.pallas_call(
        sides_kernel,
        in_specs=[VM] * 3,
        out_specs=VM,
        out_shape=jax.ShapeDtypeStruct((3 * LD, SK, AUG), BF),
        compiler_params=params(16),
        cost_estimate=cost(0.01),
        name="sides",
    )(*sources)


def far_a_kernel(ids, place, side, s0, s1, s2, t0, t1, o0, o1, tile):
    far_run(
        ids, columns_of(place)[:3], target_jobs(0, t0, o0) + target_jobs(1, t1, o1),
        lambda d, at: side[d * LD + at], lambda d, at: charges_at((s0, s1, s2)[d], at), tile,
    )


def far_a(ids, place, side, sources, targets):
    return pl.pallas_call(
        far_a_kernel,
        in_specs=[SM, SM] + [VM] * 6,
        out_specs=[VM] * 2,
        out_shape=[jax.ShapeDtypeStruct((LD * F, SK), F32)] * 2,
        scratch_shapes=[pltpu.VMEM((2 * BATCH, 3 * SK, SK), BF)],
        compiler_params=params(16),
        cost_estimate=cost(0.01),
        name="far_a",
    )(ids, place, side, *sources, *targets)


def far_b_kernel(ids, place, side, s0, s1, s2, s3, t3, o3, last, tile):
    @pl.loop(0, LD, unroll=UNROLL)
    def _(leaf):
        last[leaf] = source_side(skeleton_at(s3, leaf))

    far_run(
        ids, columns_of(place), target_jobs(3, t3, o3),
        lambda d, at: last[at] if d == 3 else side[d * LD + at],
        lambda d, at: charges_at((s0, s1, s2, s3)[d], at), tile,
    )


def far_b(ids, place, side, sources, target):
    return pl.pallas_call(
        far_b_kernel,
        in_specs=[SM, SM] + [VM] * 6,
        out_specs=[VM] * 2,
        out_shape=[
            jax.ShapeDtypeStruct((LD * F, SK), BF),
            jax.ShapeDtypeStruct((LD, SK, AUG), BF),
        ],
        scratch_shapes=[pltpu.VMEM((2 * BATCH, SIDE * SK, SK), BF)],
        compiler_params=params(16),
        cost_estimate=cost(3),
        name="far_b",
    )(ids, place, side, *sources, target)


def far_c_kernel(
    ids, place, side, last, s0, s1, s2, s3, t0, t1, t2, a0, a1, own, r1, r2, tile
):
    columns = columns_of(place)
    far_run(
        ids, columns, target_jobs(2, t2, r2),
        lambda d, at: last[at] if d == 3 else side[d * LD + at],
        lambda d, at: charges_at((s0, s1, s2, s3)[d], at), tile,
    )
    far_run(
        ids, columns[3:], target_jobs(0, t0, own, a0) + target_jobs(1, t1, r1, a1),
        lambda d, at: last[at], lambda d, at: charges_at(s3, at), tile,
    )


def far_c(ids, place, side, last, sources, targets, given):
    return pl.pallas_call(
        far_c_kernel,
        in_specs=[SM, SM] + [VM] * 11,
        out_specs=[VM] * 3,
        out_shape=[jax.ShapeDtypeStruct((LD * F, SK), F32)]
        + [jax.ShapeDtypeStruct((LD * F, SK), BF)] * 2,
        scratch_shapes=[pltpu.VMEM((2 * BATCH, SIDE * SK, SK), BF)],
        compiler_params=params(16),
        cost_estimate=cost(4),
        name="far_c",
    )(ids, place, side, last, *sources, *targets, *given)


def top_kernel(mine, pair, n1, n2, n3, a1, a2, a3, top, r1, r2, r3):
    points = target_side(mine[RHS:, :])
    total = jnp.zeros((RHS, SK), F32)
    rows = 2 * RHS
    others = [pair] + [n.at[i * rows : (i + 1) * rows] for n in (n1, n2, n3) for i in range(2)]
    for other in others:
        kernel = jnp.exp(
            jnp.dot(source_side(other[RHS:, :]), points, preferred_element_type=F32)
        ).astype(BF)
        total += jnp.dot(other[:RHS, :], kernel, preferred_element_type=F32)
    top[...] = total
    for given, out in ((a1, r1), (a2, r2), (a3, r3)):
        out[: LD * F, :] = given[...]
        out[LD * F :, :] = total.astype(BF)


def top_sum(mine, pair, others, parts):
    return pl.pallas_call(
        top_kernel,
        in_specs=[VM] * 8,
        out_specs=[VM] * 4,
        out_shape=[jax.ShapeDtypeStruct((RHS, SK), F32)]
        + [jax.ShapeDtypeStruct((LD * F + RHS, SK), BF)] * 3,
        compiler_params=params(16),
        cost_estimate=cost(2),
        name="top_sum",
    )(mine, pair, *others, *parts)


def near_groups(ids, leaf, place_of, points, side, rights, slots, out, given=None):
    count = jnp.int32(0)
    for d in range(ids.shape[1]):
        slots[d] = 0
    for d in range(ids.shape[1]):
        here, at = place_of(ids[leaf, d])
        slots[count] = jnp.where(here, at, 0)
        count += here.astype(jnp.int32)
    size = 4

    def group(start, used, total):
        tiles, weights = [], []
        for d in range(used):
            at = slots[start + d]
            tiles.append(
                jnp.exp(jnp.dot(side[at], points, preferred_element_type=F32)).astype(BF)
            )
            weights.append(rights(at))
        return total + jnp.dot(
            jnp.concatenate(weights, axis=1),
            jnp.concatenate(tiles, axis=0),
            preferred_element_type=F32,
        )

    full = lax.div(count, size)
    total = lax.fori_loop(
        0, full, lambda g, t: group(g * size, size, t), jnp.zeros((RHS, LP), F32)
    )
    out[...] = total if given is None else total + given[...]
    for used in range(1, size):

        @pl.when(count - full * size == used)
        def _(used=used):
            out[...] = group(full * size, used, out[...])


def near_own_kernel(ids, first, own, out, side, slots):
    @pl.loop(0, LD, unroll=4)
    def _(leaf):
        side[leaf] = source_side(own[leaf, :F, :])

    def place_of(named):
        at = named - first[0]
        return (named >= 0) & (at >= 0) & (at < LD), at

    @pl.loop(0, LD)
    def _(leaf):
        points = target_side(own[leaf, :F, :])
        near_groups(
            ids, leaf, place_of, points, side, lambda at: own[at, F:, :], slots, out.at[leaf]
        )


def near_own(ids, first, own):
    return pl.pallas_call(
        near_own_kernel,
        in_specs=[SM, SM, VM],
        out_specs=VM,
        out_shape=jax.ShapeDtypeStruct((LD, RHS, LP), F32),
        scratch_shapes=[pltpu.VMEM((LD, LP, AUG), BF), pltpu.SMEM((16,), jnp.int32)],
        compiler_params=params(16),
        cost_estimate=cost(9),
        name="near_own",
    )(ids, first, own)


def near_rest_kernel(ids, first, own, before, after, given, out, side, rights, slots):
    for d, block in enumerate((before, after)):

        @pl.loop(0, LD, unroll=4)
        def _(leaf, d=d, block=block):
            side[d * LD + leaf] = source_side(block[leaf, :F, :])
            rights[d * LD + leaf] = block[leaf, F:, :]

    def place_of(named):
        at = named - first[0]
        below = (at >= -LD) & (at < 0)
        above = (at >= LD) & (at < 2 * LD)
        return (named >= 0) & (below | above), jnp.where(below, at + LD, at)

    @pl.loop(0, LD)
    def _(leaf):
        points = target_side(own[leaf, :F, :])
        near_groups(
            ids, leaf, place_of, points, side, lambda at: rights[at], slots, out.at[leaf],
            given.at[leaf],
        )


def near_rest(ids, first, own, before, after, given):
    return pl.pallas_call(
        near_rest_kernel,
        in_specs=[SM, SM, VM, VM, VM, VM],
        out_specs=VM,
        out_shape=jax.ShapeDtypeStruct((LD, RHS, LP), F32),
        scratch_shapes=[
            pltpu.VMEM((2 * LD, LP, AUG), BF),
            pltpu.VMEM((2 * LD, RHS, LP), BF),
            pltpu.SMEM((16,), jnp.int32),
        ],
        compiler_params=params(24),
        cost_estimate=cost(11),
        name="near_rest",
    )(ids, first, own, before, after, given)


def final_kernel(near_sum, basis, transfer, own, r1, r2, r3, top, out):
    nt = (((1,), (1,)), ((), ()))
    last = LD * F
    total = top[...]
    for r in (r1, r2, r3):
        total += r[last:, :].astype(F32)
    total = total.astype(BF)

    @pl.loop(0, LD, unroll=UNROLL)
    def _(leaf):
        rows = pl.ds(pl.multiple_of(leaf * F, F), F)
        potential = own[rows, :]
        for r in (r1, r2, r3):
            potential += r[rows, :].astype(F32)
        potential += lax.dot_general(total, transfer[leaf], nt, preferred_element_type=F32)
        far_out = lax.dot_general(
            potential.astype(BF), basis[leaf], nt, preferred_element_type=F32
        )
        out[leaf] = (near_sum[leaf] + far_out).astype(BF)


def final(near_sum, basis, transfer, own, returned, top):
    return pl.pallas_call(
        final_kernel,
        in_specs=[VM] * 8,
        out_specs=VM,
        out_shape=jax.ShapeDtypeStruct((LD, RHS, LP), BF),
        compiler_params=params(16),
        cost_estimate=cost(3),
        name="final",
    )(near_sum, basis, transfer, own, *returned, top)


def shifted(value, dx, dz):
    pairs = []
    for x in range(SIDE):
        for z in range(SIDE):
            to = (x + dx) % SIDE * SIDE + (z + dz) % SIDE
            pairs.append((x * SIDE + z, to))
    return lax.ppermute(value, "top", pairs)


def leaf_shifted(value, dy):
    count = lax.axis_size("leaf")
    if dy == 0:
        return lax.ppermute(value, "leaf", [(i, i ^ 1) for i in range(count)])
    return lax.ppermute(value, "leaf", [(i, (i + 2 * dy) % count) for i in range(count)])


def on_device(
    points, right_sides, leaf_basis, transfer, node_points, neighbours, far_sources, skeleton
):
    node, at = lax.axis_index("leaf"), lax.axis_index("top")
    position = node * SIDE * SIDE + at
    near_msg, source_msg, target_msg = prep(
        points, right_sides, leaf_basis, transfer, skeleton, far_sources
    )
    sources = [source_msg] + [shifted(source_msg, dx, 0) for dx in (1, -1)]
    targets = [target_msg] + [shifted(target_msg, 0, dz) for dz in (1, -1, 2)]
    first = (position * LD).astype(jnp.int32).reshape(1)
    near_sum = near_own(neighbours, first, near_msg)

    targets, sources, near_msg, near_sum = lax.optimization_barrier(
        (targets, sources, near_msg, near_sum)
    )
    opposite = shifted(sources[1], 1, 0)
    side = sides_of(sources)
    near_msg, side = lax.optimization_barrier((near_msg, side))
    count = lax.axis_size("leaf") * lax.axis_size("top")
    up = [(i, i + 1) for i in range(count - 1)]
    before = lax.ppermute(near_msg, ("leaf", "top"), up)
    after = lax.ppermute(near_msg, ("leaf", "top"), [(j, i) for i, j in up])

    def ids_of(which):
        ids = jnp.concatenate([t[LD * F : LD * F + LD, : SIDE * SIDE] for t in which])
        return ids.astype(jnp.int32)

    place = jnp.stack([at // SIDE, at % SIDE]).astype(jnp.int32)
    given = far_a(ids_of(targets[:2]), place, side, sources, targets[:2])
    opposite, given, targets[2:] = lax.optimization_barrier((opposite, given, targets[2:]))
    sources.append(opposite)
    line_charge = sum(s[2 * LD * F :].astype(F32) for s in sources)
    mine = jnp.concatenate([line_charge.astype(BF), node_points[0]], axis=0)
    pair = leaf_shifted(mine, 0)
    ids = ids_of(targets)
    r3, last = far_b(ids, place, side, sources, targets[3])
    pair, r3, last = lax.optimization_barrier((pair, r3, last))
    both = jnp.concatenate([mine, pair], axis=0)
    others = [leaf_shifted(both, dy) for dy in (1, -1, 2)]
    own, r1, r2 = far_c(ids, place, side, last, sources, targets[:3], given)
    top, *parts = top_sum(mine, pair, others, (r1, r2, r3))
    returned = [shifted(r, 0, dz) for r, dz in zip(parts, (-1, 1, 2))]
    near_sum = near_rest(neighbours, first, near_msg, before, after, near_sum)
    return final(near_sum, leaf_basis, transfer, own, returned, top)


def solution(mesh):
    leaves = P(("leaf", "top"), None, None)
    lists = P(("leaf", "top"), None)
    in_specs = (leaves, leaves, leaves, leaves, P("leaf", None, None), lists, lists, lists)
    return jax.shard_map(
        on_device, mesh=mesh, in_specs=in_specs, out_specs=leaves, check_vma=False
    )
```

```python
import functools

import jax
import jax.numpy as jnp
from jax import lax
from jax.experimental import pallas as pl
from jax.experimental.pallas import tpu as pltpu
from jax.sharding import PartitionSpec as P

BF = jnp.bfloat16
F32 = jnp.float32
F = 64
RHS = 64
LP = 512
SK = 256
LD = 8
SIDE = 4
AUG = 128
UNROLL = 8
BATCH = 2
VM = pl.BlockSpec(memory_space=pltpu.VMEM)
SM = pl.BlockSpec(memory_space=pltpu.SMEM)


def params(mib=40):
    return pltpu.CompilerParams(vmem_limit_bytes=mib * 2**20)


def cost(us):
    return pl.CostEstimate(flops=int(us * 10**9), bytes_accessed=10**6, transcendentals=0)


def norm_rows(points, first):
    norm = jnp.sum(points * points, axis=0, keepdims=True) * (-2.0 / F)
    high = norm.astype(BF).astype(F32)
    mid = (norm - high).astype(BF).astype(F32)
    low = norm - high - mid
    row = lax.broadcasted_iota(jnp.int32, (16, points.shape[1]), 0)
    at = 0 if first else 3
    ones = jnp.where(row < 6, 1.0, 0.0).astype(F32)
    rows = jnp.where(row == at + 1, mid, jnp.where(row == at + 2, low, ones))
    return jnp.where(row == at, high, rows)


def source_side(points):
    points = points.astype(F32)
    zeros = jnp.zeros((AUG - F - 16, points.shape[1]), F32)
    full = jnp.concatenate([points, norm_rows(points, True), zeros], axis=0)
    return full.astype(BF).T


def target_side(points):
    points = points.astype(F32)
    zeros = jnp.zeros((AUG - F - 16, points.shape[1]), F32)
    full = jnp.concatenate([points * (4.0 / F), norm_rows(points, False), zeros], axis=0)
    return full.astype(BF)


def prep_kernel(
    points, sides, basis, transfer, skeleton, far, near_msg, source_msg, target_msg,
    own_basis, own_transfer, node, ids, sems,
):
    def fetch(leaf):
        pairs = (
            (points, near_msg.at[leaf, :F, :]),
            (sides, near_msg.at[leaf, F:, :]),
            (basis, own_basis.at[leaf]),
            (transfer, own_transfer.at[leaf]),
        )
        return [
            pltpu.make_async_copy(src.at[leaf], dst, sems.at[k, leaf])
            for k, (src, dst) in enumerate(pairs)
        ]

    for leaf in range(LD):
        for copy in fetch(leaf):
            copy.start()
    ids[...] = jnp.zeros_like(ids)
    named = far[...]
    ids[:LD, : SIDE * SIDE] = jnp.where(named >= 0, named & (LD - 1), -1).astype(F32)
    target_msg[LD * F :, :] = ids[...].astype(BF)
    position = lax.broadcasted_iota(jnp.int32, (LP, SK), 0)
    node[...] = jnp.zeros_like(node)
    for leaf in range(LD):
        for copy in fetch(leaf):
            copy.wait()
        charge = jnp.dot(
            near_msg[leaf, F:, :], own_basis[leaf], preferred_element_type=F32
        ).astype(BF)
        chosen = jnp.where(position == skeleton[leaf : leaf + 1, :], 1.0, 0.0).astype(BF)
        skel = jnp.dot(near_msg[leaf, :F, :], chosen, preferred_element_type=F32).astype(BF)
        source_msg[leaf * 2 * F : leaf * 2 * F + F, :] = charge
        source_msg[leaf * 2 * F + F : (leaf + 1) * 2 * F, :] = skel
        target_msg[leaf * F : (leaf + 1) * F, :] = skel
        node[...] += jnp.dot(charge, own_transfer[leaf], preferred_element_type=F32)
    source_msg[LD * 2 * F :, :] = node[...].astype(BF)


def prep(points, sides, basis, transfer, skeleton, far):
    anywhere = pl.BlockSpec(memory_space=pl.ANY)
    return pl.pallas_call(
        prep_kernel,
        in_specs=[anywhere] * 4 + [VM] * 2,
        out_specs=[VM] * 3,
        out_shape=[
            jax.ShapeDtypeStruct((LD, 2 * F, LP), BF),
            jax.ShapeDtypeStruct((LD * 2 * F + RHS, SK), BF),
            jax.ShapeDtypeStruct((LD * F + 16, SK), BF),
        ],
        scratch_shapes=[
            pltpu.VMEM((LD, LP, SK), BF),
            pltpu.VMEM((LD, SK, SK), BF),
            pltpu.VMEM((RHS, SK), F32),
            pltpu.VMEM((16, SK), F32),
            pltpu.SemaphoreType.DMA((4, LD)),
        ],
        compiler_params=params(56),
        cost_estimate=cost(4),
        name="prep",
    )(points, sides, basis, transfer, skeleton, far)


def far_run(ids, columns, jobs, side_of, weight_of, tile):
    depth = len(columns)

    def first(slot, job):
        row, target, _ = job
        points = target_side(target())
        for d, column in enumerate(columns):
            at = jnp.maximum(ids[row, column], 0)
            tile[slot, d * SK : (d + 1) * SK, :] = jnp.exp(
                jnp.dot(side_of(d, at), points, preferred_element_type=F32)
            ).astype(BF)

    def second(slot, job):
        row, _, store = job
        weights = []
        for d, column in enumerate(columns):
            named = ids[row, column]
            weight = weight_of(d, jnp.maximum(named, 0))
            weights.append(jnp.where(named >= 0, weight, jnp.zeros_like(weight)))
        weight = weights[0] if depth == 1 else jnp.concatenate(weights, axis=1)
        store(jnp.dot(weight, tile[slot, : depth * SK, :], preferred_element_type=F32))

    slots = 2 * BATCH
    groups = [jobs[i : i + BATCH] for i in range(0, len(jobs), BATCH)]
    for g in range(len(groups) + 1):
        if g < len(groups):
            for k, job in enumerate(groups[g]):
                first((g * BATCH + k) % slots, job)
        if g > 0:
            for k, job in enumerate(groups[g - 1]):
                second(((g - 1) * BATCH + k) % slots, job)


def target_jobs(base, target, out, given=None):
    def job(leaf):
        rows = slice(leaf * F, leaf * F + F)

        def store(total):
            if given is not None:
                total = total + given[rows, :]
            out[rows, :] = total.astype(out.dtype)

        return base * LD + leaf, lambda: target[rows, :], store

    return [job(leaf) for leaf in range(LD)]


def rows_of(leaf):
    return pl.ds(pl.multiple_of(leaf * F, F), F)


def charges_at(source, leaf):
    return source[pl.ds(pl.multiple_of(leaf * 2 * F, 2 * F), RHS), :]


def skeleton_at(source, leaf):
    return source[pl.ds(pl.multiple_of(leaf * 2 * F + F, F), F), :]


def columns_of(place):
    x, z = place[0], place[1]
    return [lax.rem(x + shift, SIDE) * SIDE + z for shift in (0, SIDE - 1, 1, 2)]


def sides_kernel(s0, s1, s2, side):
    for d, source in enumerate((s0, s1, s2)):

        @pl.loop(0, LD, unroll=UNROLL)
        def _(leaf, d=d, source=source):
            side[d * LD + leaf] = source_side(skeleton_at(source, leaf))


def sides_of(sources):
    return pl.pallas_call(
        sides_kernel,
        in_specs=[VM] * 3,
        out_specs=VM,
        out_shape=jax.ShapeDtypeStruct((3 * LD, SK, AUG), BF),
        compiler_params=params(16),
        cost_estimate=cost(0.01),
        name="sides",
    )(*sources)


def far_a_kernel(ids, place, side, s0, s1, s2, t0, t1, o0, o1, tile):
    far_run(
        ids, columns_of(place)[:3], target_jobs(0, t0, o0) + target_jobs(1, t1, o1),
        lambda d, at: side[d * LD + at], lambda d, at: charges_at((s0, s1, s2)[d], at), tile,
    )


def far_a(ids, place, side, sources, targets):
    return pl.pallas_call(
        far_a_kernel,
        in_specs=[SM, SM] + [VM] * 6,
        out_specs=[VM] * 2,
        out_shape=[jax.ShapeDtypeStruct((LD * F, SK), F32)] * 2,
        scratch_shapes=[pltpu.VMEM((2 * BATCH, 3 * SK, SK), BF)],
        compiler_params=params(16),
        cost_estimate=cost(0.01),
        name="far_a",
    )(ids, place, side, *sources, *targets)


def far_b_kernel(ids, place, side, s0, s1, s2, s3, t3, o3, last, tile):
    @pl.loop(0, LD, unroll=UNROLL)
    def _(leaf):
        last[leaf] = source_side(skeleton_at(s3, leaf))

    far_run(
        ids, columns_of(place), target_jobs(3, t3, o3),
        lambda d, at: last[at] if d == 3 else side[d * LD + at],
        lambda d, at: charges_at((s0, s1, s2, s3)[d], at), tile,
    )


def far_b(ids, place, side, sources, target):
    return pl.pallas_call(
        far_b_kernel,
        in_specs=[SM, SM] + [VM] * 6,
        out_specs=[VM] * 2,
        out_shape=[
            jax.ShapeDtypeStruct((LD * F, SK), BF),
            jax.ShapeDtypeStruct((LD, SK, AUG), BF),
        ],
        scratch_shapes=[pltpu.VMEM((2 * BATCH, SIDE * SK, SK), BF)],
        compiler_params=params(16),
        cost_estimate=cost(3),
        name="far_b",
    )(ids, place, side, *sources, target)


def far_c_kernel(
    ids, place, side, last, s0, s1, s2, s3, t0, t1, t2, a0, a1, own, r1, r2, tile
):
    columns = columns_of(place)
    far_run(
        ids, columns, target_jobs(2, t2, r2),
        lambda d, at: last[at] if d == 3 else side[d * LD + at],
        lambda d, at: charges_at((s0, s1, s2, s3)[d], at), tile,
    )
    far_run(
        ids, columns[3:], target_jobs(0, t0, own, a0) + target_jobs(1, t1, r1, a1),
        lambda d, at: last[at], lambda d, at: charges_at(s3, at), tile,
    )


def far_c(ids, place, side, last, sources, targets, given):
    return pl.pallas_call(
        far_c_kernel,
        in_specs=[SM, SM] + [VM] * 11,
        out_specs=[VM] * 3,
        out_shape=[jax.ShapeDtypeStruct((LD * F, SK), F32)]
        + [jax.ShapeDtypeStruct((LD * F, SK), BF)] * 2,
        scratch_shapes=[pltpu.VMEM((2 * BATCH, SIDE * SK, SK), BF)],
        compiler_params=params(16),
        cost_estimate=cost(4),
        name="far_c",
    )(ids, place, side, last, *sources, *targets, *given)


def top_kernel(mine, pair, n1, n2, n3, a1, a2, a3, top, r1, r2, r3):
    points = target_side(mine[RHS:, :])
    total = jnp.zeros((RHS, SK), F32)
    rows = 2 * RHS
    others = [pair] + [n.at[i * rows : (i + 1) * rows] for n in (n1, n2, n3) for i in range(2)]
    for other in others:
        kernel = jnp.exp(
            jnp.dot(source_side(other[RHS:, :]), points, preferred_element_type=F32)
        ).astype(BF)
        total += jnp.dot(other[:RHS, :], kernel, preferred_element_type=F32)
    top[...] = total
    for given, out in ((a1, r1), (a2, r2), (a3, r3)):
        out[: LD * F, :] = given[...]
        out[LD * F :, :] = total.astype(BF)


def top_sum(mine, pair, others, parts):
    return pl.pallas_call(
        top_kernel,
        in_specs=[VM] * 8,
        out_specs=[VM] * 4,
        out_shape=[jax.ShapeDtypeStruct((RHS, SK), F32)]
        + [jax.ShapeDtypeStruct((LD * F + RHS, SK), BF)] * 3,
        compiler_params=params(16),
        cost_estimate=cost(2),
        name="top_sum",
    )(mine, pair, *others, *parts)


def near_groups(ids, leaf, place_of, points, side, rights, slots, out, given=None):
    count = jnp.int32(0)
    for d in range(ids.shape[1]):
        slots[d] = 0
    for d in range(ids.shape[1]):
        here, at = place_of(ids[leaf, d])
        slots[count] = jnp.where(here, at, 0)
        count += here.astype(jnp.int32)
    size = 4

    def group(start, used, total):
        tiles, weights = [], []
        for d in range(used):
            at = slots[start + d]
            tiles.append(
                jnp.exp(jnp.dot(side[at], points, preferred_element_type=F32)).astype(BF)
            )
            weights.append(rights(at))
        return total + jnp.dot(
            jnp.concatenate(weights, axis=1),
            jnp.concatenate(tiles, axis=0),
            preferred_element_type=F32,
        )

    full = lax.div(count, size)
    total = lax.fori_loop(
        0, full, lambda g, t: group(g * size, size, t), jnp.zeros((RHS, LP), F32)
    )
    out[...] = total if given is None else total + given[...]
    for used in range(1, size):

        @pl.when(count - full * size == used)
        def _(used=used):
            out[...] = group(full * size, used, out[...])


def near_own_kernel(ids, first, own, out, side, slots):
    @pl.loop(0, LD, unroll=4)
    def _(leaf):
        side[leaf] = source_side(own[leaf, :F, :])

    def place_of(named):
        at = named - first[0]
        return (named >= 0) & (at >= 0) & (at < LD), at

    @pl.loop(0, LD)
    def _(leaf):
        points = target_side(own[leaf, :F, :])
        near_groups(
            ids, leaf, place_of, points, side, lambda at: own[at, F:, :], slots, out.at[leaf]
        )


def near_own(ids, first, own):
    return pl.pallas_call(
        near_own_kernel,
        in_specs=[SM, SM, VM],
        out_specs=VM,
        out_shape=jax.ShapeDtypeStruct((LD, RHS, LP), F32),
        scratch_shapes=[pltpu.VMEM((LD, LP, AUG), BF), pltpu.SMEM((16,), jnp.int32)],
        compiler_params=params(16),
        cost_estimate=cost(9),
        name="near_own",
    )(ids, first, own)


def near_rest_kernel(ids, first, own, before, after, given, out, side, rights, slots):
    for d, block in enumerate((before, after)):

        @pl.loop(0, LD, unroll=4)
        def _(leaf, d=d, block=block):
            side[d * LD + leaf] = source_side(block[leaf, :F, :])
            rights[d * LD + leaf] = block[leaf, F:, :]

    def place_of(named):
        at = named - first[0]
        below = (at >= -LD) & (at < 0)
        above = (at >= LD) & (at < 2 * LD)
        return (named >= 0) & (below | above), jnp.where(below, at + LD, at)

    @pl.loop(0, LD)
    def _(leaf):
        points = target_side(own[leaf, :F, :])
        near_groups(
            ids, leaf, place_of, points, side, lambda at: rights[at], slots, out.at[leaf],
            given.at[leaf],
        )


def near_rest(ids, first, own, before, after, given):
    return pl.pallas_call(
        near_rest_kernel,
        in_specs=[SM, SM, VM, VM, VM, VM],
        out_specs=VM,
        out_shape=jax.ShapeDtypeStruct((LD, RHS, LP), F32),
        scratch_shapes=[
            pltpu.VMEM((2 * LD, LP, AUG), BF),
            pltpu.VMEM((2 * LD, RHS, LP), BF),
            pltpu.SMEM((16,), jnp.int32),
        ],
        compiler_params=params(24),
        cost_estimate=cost(11),
        name="near_rest",
    )(ids, first, own, before, after, given)


def final_kernel(near_sum, basis, transfer, own, r1, r2, r3, top, out):
    nt = (((1,), (1,)), ((), ()))
    last = LD * F
    total = top[...]
    for r in (r1, r2, r3):
        total += r[last:, :].astype(F32)
    total = total.astype(BF)

    @pl.loop(0, LD, unroll=UNROLL)
    def _(leaf):
        rows = pl.ds(pl.multiple_of(leaf * F, F), F)
        potential = own[rows, :]
        for r in (r1, r2, r3):
            potential += r[rows, :].astype(F32)
        potential += lax.dot_general(total, transfer[leaf], nt, preferred_element_type=F32)
        far_out = lax.dot_general(
            potential.astype(BF), basis[leaf], nt, preferred_element_type=F32
        )
        out[leaf] = (near_sum[leaf] + far_out).astype(BF)


def final(near_sum, basis, transfer, own, returned, top):
    return pl.pallas_call(
        final_kernel,
        in_specs=[VM] * 8,
        out_specs=VM,
        out_shape=jax.ShapeDtypeStruct((LD, RHS, LP), BF),
        compiler_params=params(16),
        cost_estimate=cost(3),
        name="final",
    )(near_sum, basis, transfer, own, *returned, top)


def shifted(value, dx, dz):
    pairs = []
    for x in range(SIDE):
        for z in range(SIDE):
            to = (x + dx) % SIDE * SIDE + (z + dz) % SIDE
            pairs.append((x * SIDE + z, to))
    return lax.ppermute(value, "top", pairs)


def leaf_shifted(value, dy):
    count = lax.axis_size("leaf")
    if dy == 0:
        return lax.ppermute(value, "leaf", [(i, i ^ 1) for i in range(count)])
    return lax.ppermute(value, "leaf", [(i, (i + 2 * dy) % count) for i in range(count)])


def on_device(
    points, right_sides, leaf_basis, transfer, node_points, neighbours, far_sources, skeleton
):
    node, at = lax.axis_index("leaf"), lax.axis_index("top")
    position = node * SIDE * SIDE + at
    near_msg, source_msg, target_msg = prep(
        points, right_sides, leaf_basis, transfer, skeleton, far_sources
    )
    sources = [source_msg] + [shifted(source_msg, dx, 0) for dx in (1, -1)]
    targets = [target_msg] + [shifted(target_msg, 0, dz) for dz in (1, -1, 2)]
    first = (position * LD).astype(jnp.int32).reshape(1)
    near_sum = near_own(neighbours, first, near_msg)

    targets, sources, near_msg, near_sum = lax.optimization_barrier(
        (targets, sources, near_msg, near_sum)
    )
    opposite = shifted(sources[1], 1, 0)
    count = lax.axis_size("leaf") * lax.axis_size("top")
    up = [(i, i + 1) for i in range(count - 1)]
    after = lax.ppermute(near_msg, ("leaf", "top"), [(j, i) for i, j in up])
    side = sides_of(sources)
    near_msg, side = lax.optimization_barrier((near_msg, side))
    before = lax.ppermute(near_msg, ("leaf", "top"), up)

    def ids_of(which):
        ids = jnp.concatenate([t[LD * F : LD * F + LD, : SIDE * SIDE] for t in which])
        return ids.astype(jnp.int32)

    place = jnp.stack([at // SIDE, at % SIDE]).astype(jnp.int32)
    given = far_a(ids_of(targets[:2]), place, side, sources, targets[:2])
    opposite, given, targets[2:] = lax.optimization_barrier((opposite, given, targets[2:]))
    sources.append(opposite)
    line_charge = sum(s[2 * LD * F :].astype(F32) for s in sources)
    mine = jnp.concatenate([line_charge.astype(BF), node_points[0]], axis=0)
    pair = leaf_shifted(mine, 0)
    ids = ids_of(targets)
    r3, last = far_b(ids, place, side, sources, targets[3])
    pair, r3, last = lax.optimization_barrier((pair, r3, last))
    both = jnp.concatenate([mine, pair], axis=0)
    others = [leaf_shifted(both, dy) for dy in (1, -1, 2)]
    own, r1, r2 = far_c(ids, place, side, last, sources, targets[:3], given)
    top, *parts = top_sum(mine, pair, others, (r1, r2, r3))
    returned = [shifted(r, 0, dz) for r, dz in zip(parts, (-1, 1, 2))]
    near_sum = near_rest(neighbours, first, near_msg, before, after, near_sum)
    return final(near_sum, leaf_basis, transfer, own, returned, top)


def solution(mesh):
    leaves = P(("leaf", "top"), None, None)
    lists = P(("leaf", "top"), None)
    in_specs = (leaves, leaves, leaves, leaves, P("leaf", None, None), lists, lists, lists)
    return jax.shard_map(
        on_device, mesh=mesh, in_specs=in_specs, out_specs=leaves, check_vma=False
    )
```
